32 devices in a mesh: dp: 8 (over y, x, core), tensor: 4 (over z).
Axes of the slice: x: 2, y: 2, z: 4, core: 2. Of those that a mesh axis runs over, the one named last changes fastest.
Arguments:
- images: bfloat16 [8, 576, 768], P('dp'), may hold values from -6 to 6
- cotangent: bfloat16 [8, 576, 768], P('dp'), may hold values from -6 to 6
- image_mask: int32 [8], P('dp'), may hold values 0 or 1
- in_weight: float32 [3, 768, 768], P(None, 'dp', 'tensor'), may hold values from -0.21875 to 0.21875
- in_first: float32 [3, 768, 768], P(None, 'dp', 'tensor'), may hold values from -256 to 256
- in_second: float32 [3, 768, 768], P(None, 'dp', 'tensor'), may hold values from 1658.88 to 6635.52
- out_weight: float32 [768, 768], P('tensor', 'dp'), may hold values from -0.625 to 0.625
- out_first: float32 [768, 768], P('tensor', 'dp'), may hold values from -160 to 160
- out_second: float32 [768, 768], P('tensor', 'dp'), may hold values from 737.28 to 2949.12
- up_weight: float32 [768, 3072], P('dp', 'tensor'), may hold values from -0.21875 to 0.21875
- up_first: float32 [768, 3072], P('dp', 'tensor'), may hold values from -128 to 128
- up_second: float32 [768, 3072], P('dp', 'tensor'), may hold values from 564.48 to 2257.92
- down_weight: float32 [3072, 768], P('tensor', 'dp'), may hold values from -0.15625 to 0.15625
- down_first: float32 [3072, 768], P('tensor', 'dp'), may hold values from -192 to 192
- down_second: float32 [3072, 768], P('tensor', 'dp'), may hold values from 1152 to 4608
- norm_vector: float32 [6, 768], replicated, may hold values from -1.2 to 1.6, as said below
- norm_first: float32 [6, 768], replicated, may hold values from -384 to 384
- norm_second: float32 [6, 768], replicated, may hold values from 4608 to 18432
- head_bias: float32 [2, 768], P(None, 'tensor'), may hold values from -3 to 3
- head_first: float32 [2, 768], P(None, 'tensor'), may hold values from -256 to 256
- head_second: float32 [2, 768], P(None, 'tensor'), may hold values from 1658.88 to 6635.52
- up_bias: float32 [3072], P('tensor'), may hold values from -3 to 3
- bias_first: float32 [3072], P('tensor'), may hold values from -128 to 128
- bias_second: float32 [3072], P('tensor'), may hold values from 564.48 to 2257.92
- position_table: float32 [529, 24], P(None, 'tensor'), may hold values from -4 to 4
- table_first: float32 [529, 24], P(None, 'tensor'), may hold values from -64 to 64
- table_second: float32 [529, 24], P(None, 'tensor'), may hold values from 103.68 to 414.72
Outputs:
- block_out: bfloat16 [8, 576, 768], P('dp')
- image_grad: float32 [8, 576, 768], P('dp')
- in_moment: float32 [3, 768, 768], P(None, 'dp', 'tensor')
- in_square: float32 [3, 768, 768], P(None, 'dp', 'tensor')
- in_updated: float32 [3, 768, 768], P(None, 'dp', 'tensor')
- in_copy: bfloat16 [3, 768, 768], P(None, 'dp', 'tensor')
- out_moment: float32 [768, 768], P('tensor', 'dp')
- out_square: float32 [768, 768], P('tensor', 'dp')
- out_updated: float32 [768, 768], P('tensor', 'dp')
- out_copy: bfloat16 [768, 768], P('tensor', 'dp')
- up_moment: float32 [768, 3072], P('dp', 'tensor')
- up_square: float32 [768, 3072], P('dp', 'tensor')
- up_updated: float32 [768, 3072], P('dp', 'tensor')
- up_copy: bfloat16 [768, 3072], P('dp', 'tensor')
- down_moment: float32 [3072, 768], P('tensor', 'dp')
- down_square: float32 [3072, 768], P('tensor', 'dp')
- down_updated: float32 [3072, 768], P('tensor', 'dp')
- down_copy: bfloat16 [3072, 768], P('tensor', 'dp')
- norm_moment: float32 [6, 768], replicated
- norm_square: float32 [6, 768], replicated
- norm_updated: float32 [6, 768], replicated
- head_moment: float32 [2, 768], P(None, 'tensor')
- head_square: float32 [2, 768], P(None, 'tensor')
- head_updated: float32 [2, 768], P(None, 'tensor')
- bias_moment: float32 [3072], P('tensor')
- bias_square: float32 [3072], P('tensor')
- bias_updated: float32 [3072], P('tensor')
- table_moment: float32 [529, 24], P(None, 'tensor')
- table_square: float32 [529, 24], P(None, 'tensor')
- table_updated: float32 [529, 24], P(None, 'tensor')
The draws below stay inside these ranges and needn't reach their ends.
Inputs may be any that keep to these rules, and one draw needn't show every extreme that they name: `norm_vector`: rows 0 and 2 lie within 0.4 to 1.6, the others within -1.2 to 1.2.
All inputs are finite; a program needn't handle non-finite values. No bound on the sum of `image_mask` on one device may be relied on, other than what follows from the above.
Results may differ from the reference program's by a relative error of at most 0.014.
Values may be sent and summed in bfloat16 or wider, within the bound.
A program may use at most 128 MiB of HBM per device.

```python
import math
import jax
import jax.numpy as jnp
from jax import lax

D = 768
HEADS = 24
HEAD_DIM = 32
FF = 3072
WIN = 12
SIDE = 24
STEP = 7
SHIFT = 6
REL = 529
IMAGES = 8
TOKENS = 4608


def draw_norm_vector(key, part):
    key = jax.random.fold_in(key, 11)
    base = jnp.clip(jax.random.normal(key, (6, D), jnp.float32), -4.0, 4.0)
    row_ids = jnp.arange(6)
    is_gain = (row_ids == 0) | (row_ids == 2)
    return jnp.where(is_gain[:, None], 1.0 + 0.15 * base, 0.3 * base).astype(jnp.float32)


def set_ends(entries, own_key, least, largest):
    spot = [jax.random.randint(jax.random.fold_in(own_key, axis), (), 0, length) for axis, length in enumerate(entries.shape)]
    widest = entries.shape.index(max(entries.shape))
    beside = spot[:widest] + [(spot[widest] + 1) % entries.shape[widest]] + spot[widest + 1:]
    return entries.at[tuple(spot)].set(least).at[tuple(beside)].set(largest)


def shard_levels(key, extent, pieces, smallest, high):
    def one(position, parts):
        steps = jax.random.uniform(jax.random.fold_in(jax.random.fold_in(key, 6), position), (parts,), jnp.float32, smallest / len(pieces), high / len(pieces))
        return jnp.repeat(jnp.exp(steps), extent[position] // parts).reshape((-1,) + (1,) * (len(extent) - position - 1))

    factor_of = one(*pieces[0])
    for cut in pieces[1:]:
        factor_of = factor_of * one(*cut)
    return factor_of


def bell_draw(rng, shape, scale, most, shards=(), kind=jnp.bfloat16):
    loudness = shard_levels(rng, shape, shards, -0.22, 0.18) if shards else 1.0
    drawn = jax.random.normal(rng, shape, jnp.float32) * scale * loudness
    return jnp.minimum(jnp.maximum(drawn, -most), most).astype(kind)


def setup_inputs(seed: int = 0) -> dict:
    key_list = jax.random.split(jax.random.key(seed), 28)
    images = bell_draw(key_list[0], (IMAGES, SIDE * SIDE, D), 1.0, 6.0, ((0, 8),))
    cotangent = bell_draw(key_list[1], (IMAGES, SIDE * SIDE, D), 1.0, 6.0, ((0, 8),))
    image_mask = set_ends((jax.random.randint(key_list[2], (IMAGES,), 0, 128) < 113).astype(jnp.int32), jax.random.fold_in(key_list[2], 1), 0, 1)
    in_weight = bell_draw(key_list[3], (3, D, D), D ** -0.5, 0.21875, ((1, 8), (2, 4)), jnp.float32)
    in_first = bell_draw(key_list[4], (3, D, D), (0.6 * TOKENS ** 0.5), 256.0, ((1, 8), (2, 4)), jnp.float32)
    in_second = jnp.clip(jnp.exp(math.log(6635.52) - 1.3862944 * jax.random.uniform(key_list[5], (3, D, D), jnp.float32) ** shard_levels(key_list[5], (3, D, D), ((1, 8), (2, 4)), -0.2, 0.2)), 1658.88, 6635.52)
    out_weight = bell_draw(key_list[6], (D, D), (D // 8) ** -0.5, 0.625, ((0, 4), (1, 8)), jnp.float32)
    out_first = bell_draw(key_list[7], (D, D), (0.4 * TOKENS ** 0.5), 160.0, ((0, 4), (1, 8)), jnp.float32)
    out_second = jnp.clip(jnp.exp(math.log(2949.12) - 1.3862944 * jax.random.uniform(key_list[8], (D, D), jnp.float32) ** shard_levels(key_list[8], (D, D), ((0, 4), (1, 8)), -0.2, 0.2)), 737.28, 2949.12)
    up_weight = bell_draw(key_list[9], (D, FF), D ** -0.5, 0.21875, ((0, 8), (1, 4)), jnp.float32)
    up_first = bell_draw(key_list[10], (D, FF), (0.35 * TOKENS ** 0.5), 128.0, ((0, 8), (1, 4)), jnp.float32)
    up_second = jnp.clip(jnp.exp(math.log(2257.92) - 1.3862944 * jax.random.uniform(key_list[11], (D, FF), jnp.float32) ** shard_levels(key_list[11], (D, FF), ((0, 8), (1, 4)), -0.2, 0.2)), 564.48, 2257.92)
    down_weight = bell_draw(key_list[12], (FF, D), (FF // 2) ** -0.5, 0.15625, ((0, 4), (1, 8)), jnp.float32)
    down_first = bell_draw(key_list[13], (FF, D), (0.5 * TOKENS ** 0.5), 192.0, ((0, 4), (1, 8)), jnp.float32)
    down_second = jnp.clip(jnp.exp(math.log(4608.0) - 1.3862944 * jax.random.uniform(key_list[14], (FF, D), jnp.float32) ** shard_levels(key_list[14], (FF, D), ((0, 4), (1, 8)), -0.2, 0.2)), 1152.0, 4608.0)
    norm_vector = draw_norm_vector(jax.random.fold_in(key_list[27], 71), 0)
    norm_first = bell_draw(key_list[16], (6, D), (TOKENS ** 0.5), 384.0, (), jnp.float32)
    norm_second = jnp.clip(jnp.exp(jax.random.uniform(key_list[17], (6, D), jnp.float32, math.log(4608.0), math.log(18432.0))), 4608.0, 18432.0)
    head_bias = bell_draw(key_list[18], (2, D), 0.5, 3.0, ((1, 4),), jnp.float32)
    head_first = bell_draw(key_list[19], (2, D), (0.6 * TOKENS ** 0.5), 256.0, ((1, 4),), jnp.float32)
    head_second = jnp.clip(jnp.exp(math.log(6635.52) - 1.3862944 * jax.random.uniform(key_list[20], (2, D), jnp.float32) ** shard_levels(key_list[20], (2, D), ((1, 4),), -0.2, 0.2)), 1658.88, 6635.52)
    up_bias = bell_draw(key_list[21], (FF,), 0.5, 3.0, ((0, 4),), jnp.float32)
    bias_first = bell_draw(key_list[22], (FF,), (0.35 * TOKENS ** 0.5), 128.0, ((0, 4),), jnp.float32)
    bias_second = jnp.clip(jnp.exp(math.log(2257.92) - 1.3862944 * jax.random.uniform(key_list[23], (FF,), jnp.float32) ** shard_levels(key_list[23], (FF,), ((0, 4),), -0.2, 0.2)), 564.48, 2257.92)
    position_table = bell_draw(key_list[24], (REL, HEADS), 1.0, 4.0, ((1, 4),), jnp.float32)
    table_first = bell_draw(key_list[25], (REL, HEADS), (0.15 * TOKENS ** 0.5), 64.0, ((1, 4),), jnp.float32)
    table_second = jnp.clip(jnp.exp(math.log(414.72) - 1.3862944 * jax.random.uniform(key_list[26], (REL, HEADS), jnp.float32) ** shard_levels(key_list[26], (REL, HEADS), ((1, 4),), -0.2, 0.2)), 103.68, 414.72)
    return {"images": images, "cotangent": cotangent, "image_mask": image_mask, "in_weight": in_weight, "in_first": in_first, "in_second": in_second, "out_weight": out_weight, "out_first": out_first, "out_second": out_second, "up_weight": up_weight, "up_first": up_first, "up_second": up_second, "down_weight": down_weight, "down_first": down_first, "down_second": down_second, "norm_vector": norm_vector, "norm_first": norm_first, "norm_second": norm_second, "head_bias": head_bias, "head_first": head_first, "head_second": head_second, "up_bias": up_bias, "bias_first": bias_first, "bias_second": bias_second, "position_table": position_table, "table_first": table_first, "table_second": table_second}


@jax.custom_vjp
def low(v):
    return lax.optimization_barrier(v.astype(jnp.bfloat16)).astype(jnp.float32)

@jax.custom_vjp
def low_back(v):
    return v

def low_keep(v):
    return (low(v), None)

def low_pass(kept, grad):
    return (grad,)

def back_keep(v):
    return (v, None)

def back_low(kept, grad):
    return (low(grad),)
low.defvjp(low_keep, low_pass)
low_back.defvjp(back_keep, back_low)
NORM_EPS = 1e-05
FILL_VALUE = -100.0
BETA_ONE = 0.5
BETA_TWO = 0.5
ADAM_EPS = 1e-08
RATE_MATRIX = 0.05
RATE_VECTOR = 0.3
DECAY_MATRIX = 0.05

def matmul(left_side, right_side):
    return jnp.dot(left_side, right_side, precision=lax.Precision.HIGHEST)

def layer_norm(values, gain_in, offset_in):
    center = values - lax.optimization_barrier(jnp.mean(values, axis=-1, keepdims=True))
    spread = lax.optimization_barrier(jnp.mean(center * center, axis=-1, keepdims=True))
    return center * lax.rsqrt(spread + NORM_EPS) * gain_in + offset_in

def to_windows(grid_view):
    blocks = SIDE // WIN
    channels = grid_view.shape[-1]
    grid_view = grid_view.reshape(blocks, WIN, blocks, WIN, channels).transpose(0, 2, 1, 3, 4)
    return grid_view.reshape(blocks * blocks, WIN * WIN, channels)

def from_windows(windows):
    blocks = SIDE // WIN
    channels = windows.shape[-1]
    windows = windows.reshape(blocks, blocks, WIN, WIN, channels).transpose(0, 2, 1, 3, 4)
    return windows.reshape(SIDE, SIDE, channels)

def window_tables():
    places = jnp.arange(WIN * WIN, dtype=jnp.int32)
    row_of = places // WIN
    col_of = places % WIN
    offsets = (row_of[:, None] - row_of[None, :] + WIN - 1) * (2 * WIN - 1) + (col_of[:, None] - col_of[None, :] + WIN - 1)
    cell_ids = jnp.arange(SIDE, dtype=jnp.int32)
    band_of = (cell_ids >= SIDE - WIN).astype(jnp.int32) + (cell_ids >= SIDE - SHIFT).astype(jnp.int32)
    region = band_of[:, None] * 3 + band_of[None, :]
    labels = to_windows(region[:, :, None])[:, :, 0]
    fill_add = jnp.where(labels[:, :, None] != labels[:, None, :], FILL_VALUE, 0.0).astype(jnp.float32)
    return (offsets, fill_add)

def attend_image(normed, in_weight, head_bias, position_table, offsets, fill_add):
    grid_view = jnp.roll(normed.reshape(SIDE, SIDE, D), (-SHIFT, -SHIFT), (0, 1))
    windows = to_windows(grid_view)
    win_count = windows.shape[0]
    shape_heads = (win_count, WIN * WIN, HEADS, HEAD_DIM)
    highest = lax.Precision.HIGHEST
    queries = jnp.einsum('nsc,ce->nse', windows, in_weight[0], precision=highest) + head_bias[0]
    queries = low(low_back(queries)).reshape(shape_heads)
    keys_all = jnp.einsum('nsc,ce->nse', windows, in_weight[1], precision=highest)
    keys_all = low(low_back(keys_all)).reshape(shape_heads)
    values_all = jnp.einsum('nsc,ce->nse', windows, in_weight[2], precision=highest) + head_bias[1]
    values_all = low(low_back(values_all)).reshape(shape_heads)
    bias_add = jnp.transpose(position_table[offsets], (2, 0, 1))
    scores = jnp.einsum('nqhd,nkhd->nhqk', queries, keys_all, precision=highest) * HEAD_DIM ** (-0.5)
    scores = low_back(scores + bias_add[None] + fill_add[:, None])
    row_top = lax.optimization_barrier(jnp.max(scores, axis=-1, keepdims=True))
    weights = jnp.exp(scores - row_top)
    prob_low = low(weights / lax.optimization_barrier(jnp.sum(weights, axis=-1, keepdims=True)))
    mixed = jnp.einsum('nhqk,nkhd->nqhd', prob_low, values_all, precision=highest)
    mixed = low(low_back(mixed)).reshape(win_count, WIN * WIN, D)
    grid_view = jnp.roll(from_windows(mixed), (SHIFT, SHIFT), (0, 1))
    return grid_view.reshape(SIDE * SIDE, D)

def block_forward(token_rows, norm_vector, in_weight, head_bias, position_table, out_weight, up_weight, up_bias, down_weight):
    offsets, fill_add = window_tables()
    normed_one = low(layer_norm(token_rows, norm_vector[0], norm_vector[1]))

    def attend(normed):
        return attend_image(normed, in_weight, head_bias, position_table, offsets, fill_add)
    mixed_rows = lax.map(jax.checkpoint(attend), normed_one.reshape(-1, SIDE * SIDE, D)).reshape(-1, D)
    branch = low_back(matmul(mixed_rows, out_weight) + norm_vector[4])
    middle = token_rows + branch
    normed_two = low(layer_norm(middle, norm_vector[2], norm_vector[3]))
    hidden = low_back(matmul(normed_two, up_weight) + up_bias)
    active = low(jax.nn.gelu(hidden, approximate=True))
    return middle + low_back(matmul(active, down_weight) + norm_vector[5])

def adam_update(weight, first_old, second_old, gradient, rate_of, decay_of):
    moment = BETA_ONE * first_old + (1.0 - BETA_ONE) * gradient
    square = BETA_TWO * second_old + (1.0 - BETA_TWO) * gradient * gradient
    moment_fix = moment / (1.0 - BETA_ONE ** STEP)
    square_fix = square / (1.0 - BETA_TWO ** STEP)
    updated = weight * (1.0 - rate_of * decay_of) - rate_of * moment_fix / (jnp.sqrt(square_fix) + ADAM_EPS)
    return (moment, square, updated)

def reference(images, cotangent, image_mask, in_weight, in_first, in_second, out_weight, out_first, out_second, up_weight, up_first, up_second, down_weight, down_first, down_second, norm_vector, norm_first, norm_second, head_bias, head_first, head_second, up_bias, bias_first, bias_second, position_table, table_first, table_second):
    token_rows = images.astype(jnp.float32).reshape(-1, D)
    block_rows, pullback = jax.vjp(block_forward, token_rows, norm_vector, low(in_weight), head_bias, position_table, low(out_weight), low(up_weight), up_bias, low(down_weight))
    keep_rows = jnp.repeat(image_mask.astype(jnp.float32), SIDE * SIDE)[:, None]
    gradients = pullback(cotangent.astype(jnp.float32).reshape(-1, D) * keep_rows)
    grad_rows, norm_grad, in_grad, head_grad, table_grad, out_grad, up_grad, bias_grad, down_grad = gradients
    block_out = block_rows.astype(jnp.bfloat16).reshape(images.shape)
    image_grad = grad_rows.reshape(images.shape)
    in_moment, in_square, in_updated = adam_update(in_weight, in_first, in_second, in_grad, RATE_MATRIX, DECAY_MATRIX)
    out_moment, out_square, out_updated = adam_update(out_weight, out_first, out_second, out_grad, RATE_MATRIX, DECAY_MATRIX)
    up_moment, up_square, up_updated = adam_update(up_weight, up_first, up_second, up_grad, RATE_MATRIX, DECAY_MATRIX)
    down_moment, down_square, down_updated = adam_update(down_weight, down_first, down_second, down_grad, RATE_MATRIX, DECAY_MATRIX)
    norm_moment, norm_square, norm_updated = adam_update(norm_vector, norm_first, norm_second, norm_grad, RATE_VECTOR, 0.0)
    head_moment, head_square, head_updated = adam_update(head_bias, head_first, head_second, head_grad, RATE_VECTOR, 0.0)
    bias_moment, bias_square, bias_updated = adam_update(up_bias, bias_first, bias_second, bias_grad, RATE_VECTOR, 0.0)
    table_moment, table_square, table_updated = adam_update(position_table, table_first, table_second, table_grad, RATE_VECTOR, 0.0)
    return (block_out, image_grad, in_moment, in_square, in_updated, in_updated.astype(jnp.bfloat16), out_moment, out_square, out_updated, out_updated.astype(jnp.bfloat16), up_moment, up_square, up_updated, up_updated.astype(jnp.bfloat16), down_moment, down_square, down_updated, down_updated.astype(jnp.bfloat16), norm_moment, norm_square, norm_updated, head_moment, head_square, head_updated, bias_moment, bias_square, bias_updated, table_moment, table_square, table_updated)
```

```python
import functools
from functools import partial

import jax
import jax.numpy as jnp
from jax import lax
from jax.experimental import pallas as pl
from jax.experimental.pallas import tpu as pltpu
from jax.sharding import PartitionSpec as P

D = 768
HEAD_DIM = 32
WIN = 12
SIDE = 24
STEP = 7
SHIFT = 6


NORM_EPS = 1e-05
FILL_VALUE = -100.0
BETA_ONE = 0.5
BETA_TWO = 0.5
ADAM_EPS = 1e-08
RATE_MATRIX = 0.05
RATE_VECTOR = 0.3
DECAY_MATRIX = 0.05


def layer_norm(values, gain_in, offset_in):
    center = values - jnp.mean(values, axis=-1, keepdims=True)
    spread = jnp.mean(center * center, axis=-1, keepdims=True)
    return center * lax.rsqrt(spread + NORM_EPS) * gain_in + offset_in


def adam_update(weight, first_old, second_old, gradient, rate_of, decay_of):
    moment = BETA_ONE * first_old + (1.0 - BETA_ONE) * gradient
    square = BETA_TWO * second_old + (1.0 - BETA_TWO) * gradient * gradient
    moment_fix = moment / (1.0 - BETA_ONE**STEP)
    square_fix = square / (1.0 - BETA_TWO**STEP)
    updated = weight * (1.0 - rate_of * decay_of) - rate_of * moment_fix / (
        jnp.sqrt(square_fix) + ADAM_EPS
    )
    return (moment, square, updated)


def dot_plain(left_side, right_side):
    return jnp.dot(left_side, right_side, preferred_element_type=jnp.float32)


def dot_back(left_side, right_side):
    return lax.dot_general(
        left_side, right_side, (((1,), (1,)), ((), ())), preferred_element_type=jnp.float32
    )


def dot_rows(left_side, right_side):
    return lax.dot_general(
        left_side, right_side, (((0,), (0,)), ((), ())), preferred_element_type=jnp.float32
    )


def to_heads(token_rows, images_here, heads_here):
    blocks = SIDE // WIN
    grid_view = token_rows.reshape(images_here, SIDE, SIDE, heads_here * HEAD_DIM)
    grid_view = jnp.roll(grid_view, (-SHIFT, -SHIFT), (1, 2))
    grid_view = grid_view.reshape(
        images_here, blocks, WIN, blocks, WIN, heads_here, HEAD_DIM
    ).transpose(0, 1, 3, 2, 4, 5, 6)
    return grid_view.reshape(images_here, blocks * blocks, WIN * WIN, heads_here, HEAD_DIM)


def from_heads(windows, images_here):
    blocks = SIDE // WIN
    channels = windows.shape[3] * windows.shape[4]
    grid_view = windows.reshape(images_here, blocks, blocks, WIN, WIN, channels).transpose(
        0, 1, 3, 2, 4, 5
    )
    grid_view = jnp.roll(
        grid_view.reshape(images_here, SIDE, SIDE, channels), (SHIFT, SHIFT), (1, 2)
    )
    return grid_view.reshape(images_here * SIDE * SIDE, channels)


def window_fill():
    blocks = SIDE // WIN
    cell_ids = jnp.arange(SIDE, dtype=jnp.int32)
    band_of = (cell_ids >= SIDE - WIN).astype(jnp.int32) + (cell_ids >= SIDE - SHIFT).astype(
        jnp.int32
    )
    region = band_of[:, None] * 3 + band_of[None, :]
    labels = (
        region.reshape(blocks, WIN, blocks, WIN)
        .transpose(0, 2, 1, 3)
        .reshape(blocks * blocks, WIN * WIN)
    )
    return jnp.where(labels[:, :, None] != labels[:, None, :], FILL_VALUE, 0.0).astype(jnp.float32)


def offset_onehot():
    places = jnp.arange(WIN, dtype=jnp.int32)
    spans = jnp.arange(2 * WIN - 1, dtype=jnp.int32)
    return (places[:, None, None] - places[None, :, None] + WIN - 1 == spans[None, None, :]).astype(
        jnp.float32
    )


def window_scores(query_win, key_win, bias_add, fill_add):
    scores = jnp.einsum(
        "inqhd,inkhd->inhqk", query_win, key_win, preferred_element_type=jnp.float32
    ) * HEAD_DIM ** (-0.5)
    return scores + bias_add[None, None] + fill_add[None, :, None]


def on_device(
    images,
    cotangent,
    image_mask,
    in_weight,
    in_first,
    in_second,
    out_weight,
    out_first,
    out_second,
    up_weight,
    up_first,
    up_second,
    down_weight,
    down_first,
    down_second,
    norm_vector,
    norm_first,
    norm_second,
    head_bias,
    head_first,
    head_second,
    up_bias,
    bias_first,
    bias_second,
    position_table,
    table_first,
    table_second,
):
    lowtype = jnp.bfloat16
    highest = lax.Precision.HIGHEST
    whole_in, whole_out, whole_up, whole_down = (
        lax.all_gather(in_weight.astype(lowtype), "dp", axis=1, tiled=True),
        lax.all_gather(out_weight.astype(lowtype), "dp", axis=1, tiled=True),
        lax.all_gather(up_weight.astype(lowtype), "dp", axis=0, tiled=True),
        lax.all_gather(down_weight.astype(lowtype), "dp", axis=1, tiled=True),
    )
    images_here = images.shape[0]
    heads_here = whole_in.shape[2] // HEAD_DIM
    span_count = 2 * WIN - 1
    token_rows = images.reshape(-1, D).astype(jnp.float32)
    normed_one, norm_one_back = jax.vjp(layer_norm, token_rows, norm_vector[0], norm_vector[1])
    low_one = normed_one.astype(lowtype)
    query_rows = (dot_plain(low_one, whole_in[0]) + head_bias[0]).astype(lowtype)
    key_rows = dot_plain(low_one, whole_in[1]).astype(lowtype)
    value_rows = (dot_plain(low_one, whole_in[2]) + head_bias[1]).astype(lowtype)
    query_win = to_heads(query_rows, images_here, heads_here)
    key_win = to_heads(key_rows, images_here, heads_here)
    value_win = to_heads(value_rows, images_here, heads_here)
    onehot = offset_onehot()
    table_view = position_table.reshape(span_count, span_count, heads_here)
    bias_add = jnp.einsum(
        "xya,zwb,abh->hxzyw", onehot, onehot, table_view, precision=highest
    ).reshape(heads_here, WIN * WIN, WIN * WIN)
    fill_add = window_fill()
    scores = window_scores(query_win, key_win, bias_add, fill_add)
    row_top = jnp.max(scores, axis=-1, keepdims=True)
    weights_raw = jnp.exp(scores - row_top)
    row_total = jnp.sum(weights_raw, axis=-1, keepdims=True)
    log_total = row_top + jnp.log(row_total)
    prob_low = (weights_raw / row_total).astype(lowtype)
    mixed_win = jnp.einsum(
        "inhqk,inkhd->inqhd", prob_low, value_win, preferred_element_type=jnp.float32
    ).astype(lowtype)
    mixed_rows = from_heads(mixed_win, images_here)
    branch_share = lax.psum_scatter(
        dot_plain(mixed_rows, whole_out), "tensor", scatter_dimension=0, tiled=True
    )
    branch = lax.all_gather(branch_share, "tensor", axis=0, tiled=True) + norm_vector[4]
    middle = token_rows + branch
    normed_two, norm_two_back = jax.vjp(layer_norm, middle, norm_vector[2], norm_vector[3])
    low_two = normed_two.astype(lowtype)
    hidden = dot_plain(low_two, whole_up) + up_bias
    active, gelu_back = jax.vjp(partial(jax.nn.gelu, approximate=True), hidden)
    active_low = active.astype(lowtype)
    output_share = lax.psum_scatter(
        dot_plain(active_low, whole_down).astype(jnp.bfloat16),
        "tensor",
        scatter_dimension=0,
        tiled=True,
    ).astype(jnp.float32)
    output = (
        lax.all_gather(output_share.astype(jnp.bfloat16), "tensor", axis=0, tiled=True).astype(
            output_share.dtype
        )
        + norm_vector[5]
    )
    block_out = (middle + output).astype(lowtype).reshape(images.shape)
    keep_rows = jnp.repeat(image_mask.astype(jnp.float32), SIDE * SIDE)[:, None]
    grad_out = cotangent.reshape(-1, D).astype(jnp.float32) * keep_rows
    grad_low = grad_out.astype(lowtype)
    down_grad = dot_rows(active_low, grad_low)
    grad_hidden = gelu_back(dot_back(grad_low, whole_down))[0].astype(lowtype)
    up_grad = dot_rows(low_two, grad_hidden)
    bias_grad = jnp.sum(grad_hidden.astype(jnp.float32), axis=0)
    two_share = lax.psum_scatter(
        dot_back(grad_hidden, whole_up), "tensor", scatter_dimension=0, tiled=True
    )
    grad_two = lax.all_gather(two_share, "tensor", axis=0, tiled=True)
    grad_norm_two, gain_two, offset_two = norm_two_back(grad_two)
    grad_middle = grad_out + grad_norm_two
    grad_branch = grad_middle.astype(lowtype)
    out_grad = dot_rows(mixed_rows, grad_branch)
    grad_mixed = dot_back(grad_branch, whole_out).astype(lowtype)
    grad_win = to_heads(grad_mixed, images_here, heads_here)
    scores_again = window_scores(query_win, key_win, bias_add, fill_add)
    probs = jnp.exp(scores_again - log_total)
    grad_probs = jnp.einsum(
        "inqhd,inkhd->inhqk", grad_win, value_win, preferred_element_type=jnp.float32
    )
    grad_value = jnp.einsum(
        "inhqk,inqhd->inkhd", probs.astype(lowtype), grad_win, preferred_element_type=jnp.float32
    ).astype(lowtype)
    grad_scores = (
        probs * (grad_probs - jnp.sum(grad_probs * probs, axis=-1, keepdims=True))
    ).astype(lowtype)
    grad_query = (
        jnp.einsum("inhqk,inkhd->inqhd", grad_scores, key_win, preferred_element_type=jnp.float32)
        * HEAD_DIM ** (-0.5)
    ).astype(lowtype)
    grad_key = (
        jnp.einsum("inhqk,inqhd->inkhd", grad_scores, query_win, preferred_element_type=jnp.float32)
        * HEAD_DIM ** (-0.5)
    ).astype(lowtype)
    score_sums = jnp.sum(grad_scores.astype(jnp.float32), axis=(0, 1)).reshape(
        heads_here, WIN, WIN, WIN, WIN
    )
    table_grad = jnp.einsum(
        "xya,zwb,hxzyw->abh", onehot, onehot, score_sums, precision=highest
    ).reshape(span_count * span_count, heads_here)
    query_back = from_heads(grad_query, images_here)
    key_back = from_heads(grad_key, images_here)
    value_back = from_heads(grad_value, images_here)
    in_grad = jnp.stack(
        [dot_rows(low_one, query_back), dot_rows(low_one, key_back), dot_rows(low_one, value_back)]
    )
    head_grad = jnp.stack(
        [
            jnp.sum(query_back.astype(jnp.float32), axis=0),
            jnp.sum(value_back.astype(jnp.float32), axis=0),
        ]
    )
    grad_one_terms = (
        dot_back(query_back, whole_in[0])
        + dot_back(key_back, whole_in[1])
        + dot_back(value_back, whole_in[2])
    )
    one_share = lax.psum_scatter(
        grad_one_terms.astype(jnp.bfloat16), "tensor", scatter_dimension=0, tiled=True
    ).astype(jnp.float32)
    grad_one = lax.all_gather(one_share.astype(jnp.bfloat16), "tensor", axis=0, tiled=True).astype(
        one_share.dtype
    )
    grad_norm_one, gain_one, offset_one = norm_one_back(grad_one)
    image_grad = (grad_middle + grad_norm_one).reshape(images.shape)
    norm_grad = jnp.stack(
        [
            gain_one,
            offset_one,
            gain_two,
            offset_two,
            jnp.sum(grad_branch.astype(jnp.float32), axis=0),
            jnp.sum(grad_low.astype(jnp.float32), axis=0),
        ]
    )
    summed = lax.psum(
        (in_grad, out_grad, up_grad, down_grad, norm_grad, head_grad, bias_grad, table_grad), "dp"
    )
    position = lax.axis_index("dp")
    in_total = lax.dynamic_slice_in_dim(
        summed[0], position * in_weight.shape[1], in_weight.shape[1], 1
    )
    out_total = lax.dynamic_slice_in_dim(
        summed[1], position * out_weight.shape[1], out_weight.shape[1], 1
    )
    up_total = lax.dynamic_slice_in_dim(
        summed[2], position * up_weight.shape[0], up_weight.shape[0], 0
    )
    down_total = lax.dynamic_slice_in_dim(
        summed[3], position * down_weight.shape[1], down_weight.shape[1], 1
    )
    norm_total, head_total, bias_total, table_total = (summed[4], summed[5], summed[6], summed[7])
    in_moment, in_square, in_updated = adam_update(
        in_weight, in_first, in_second, in_total, RATE_MATRIX, DECAY_MATRIX
    )
    out_moment, out_square, out_updated = adam_update(
        out_weight, out_first, out_second, out_total, RATE_MATRIX, DECAY_MATRIX
    )
    up_moment, up_square, up_updated = adam_update(
        up_weight, up_first, up_second, up_total, RATE_MATRIX, DECAY_MATRIX
    )
    down_moment, down_square, down_updated = adam_update(
        down_weight, down_first, down_second, down_total, RATE_MATRIX, DECAY_MATRIX
    )
    norm_moment, norm_square, norm_updated = adam_update(
        norm_vector, norm_first, norm_second, norm_total, RATE_VECTOR, 0.0
    )
    head_moment, head_square, head_updated = adam_update(
        head_bias, head_first, head_second, head_total, RATE_VECTOR, 0.0
    )
    bias_moment, bias_square, bias_updated = adam_update(
        up_bias, bias_first, bias_second, bias_total, RATE_VECTOR, 0.0
    )
    table_moment, table_square, table_updated = adam_update(
        position_table, table_first, table_second, table_total, RATE_VECTOR, 0.0
    )
    return (
        block_out,
        image_grad,
        in_moment,
        in_square,
        in_updated,
        in_updated.astype(lowtype),
        out_moment,
        out_square,
        out_updated,
        out_updated.astype(lowtype),
        up_moment,
        up_square,
        up_updated,
        up_updated.astype(lowtype),
        down_moment,
        down_square,
        down_updated,
        down_updated.astype(lowtype),
        norm_moment,
        norm_square,
        norm_updated,
        head_moment,
        head_square,
        head_updated,
        bias_moment,
        bias_square,
        bias_updated,
        table_moment,
        table_square,
        table_updated,
    )


MESH = pl.DeviceIdType.MESH
TOK = SIDE * SIDE
WTOK = WIN * WIN
ROWP = 16
WPAD = WIN * ROWP
FQ = 768
SHARD = 96
HG = 6
TABL = 640
ZL = 384
SCALE = HEAD_DIM ** (-0.5)
F32 = jnp.float32
BF = jnp.bfloat16


def dot(a, b):
    return lax.dot_general(a, b, (((1,), (0,)), ((), ())), preferred_element_type=F32)


def dot_nt(a, b):
    return lax.dot_general(a, b, (((1,), (1,)), ((), ())), preferred_element_type=F32)


def dot_tn(a, b):
    return lax.dot_general(a, b, (((0,), (0,)), ((), ())), preferred_element_type=F32)


def iota(shape, axis):
    return lax.broadcasted_iota(jnp.int32, shape, axis)


def div12(i):
    return lax.shift_right_logical(i * 171, 11)


def hot(condition):
    return jnp.where(condition, 1.0, 0.0).astype(BF)


def split_two(v):
    high = v.astype(BF)
    return high, (v - high.astype(F32)).astype(BF)


def split_three(v):
    high, _ = split_two(v)
    rest = v - high.astype(F32)
    mid, low = split_two(rest)
    return high, mid, low


def token_of(row, col, win):
    r = row + WIN * (win // 2) + SHIFT
    c = col + WIN * (win % 2) + SHIFT
    r = jnp.where(r >= SIDE, r - SIDE, r)
    c = jnp.where(c >= SIDE, c - SIDE, c)
    return r * SIDE + c


def padded_rows(win):
    i = iota((WPAD, 1), 0)
    col = jnp.bitwise_and(i, ROWP - 1)
    token = token_of(lax.shift_right_logical(i, 4), col, win)
    token = jnp.where(col < WIN, token, -1)
    return hot(token == iota((WPAD, TOK), 1))


def compact_rows(win):
    i = iota((WTOK, 1), 0)
    row = div12(i)
    return hot(token_of(row, i - WIN * row, win) == iota((WTOK, TOK), 1))


def pad_hot():
    j = iota((WPAD, WTOK), 1)
    return hot(iota((WPAD, WTOK), 0) == j + 4 * div12(j))


def pad_hot_t():
    j = iota((WTOK, WPAD), 0)
    return hot(iota((WTOK, WPAD), 1) == j + 4 * div12(j))


def offset_hot(ci):
    lane = iota((1, ZL), 1)
    cj = jnp.bitwise_and(lane, ROWP - 1)
    u = lax.shift_right_logical(lane, 4)
    entry = (22 - u) * 23 + 11 + ci - cj
    entry = jnp.where((cj < WIN) & (u < 23), entry, -1)
    return hot(iota((TABL, ZL), 0) == entry)


def mask_head(tile, lane0):
    lane = iota((1, 128), 1)
    return jnp.where((lane >= lane0) & (lane < lane0 + HEAD_DIM), tile, jnp.zeros_like(tile))


def norm_stats(values):
    center = values - jnp.mean(values, axis=-1, keepdims=True)
    spread = jnp.mean(center * center, axis=-1, keepdims=True)
    rs = lax.rsqrt(spread + NORM_EPS)
    return center * rs, rs


def norm_back(grad, gain, normal, rs):
    e = grad * gain
    return rs * (
        e
        - jnp.mean(e, axis=-1, keepdims=True)
        - normal * jnp.mean(e * normal, axis=-1, keepdims=True)
    )


def col_sum(v):
    return jnp.sum(v, axis=0, keepdims=True)


def main_kernel(
    img, cot, msk, w_in, w_out, w_up, w_dn, nv, hb, ub, tab,
    g_a, g_u, g_d, sm_out, bo_out, ig_out,
    G, GB, RBS, T1, R1, T2, R2, ZB, RZ,
    PB, ZT, QVK, MX, DS, DZ, LOW1, N1, RS1, XC, BR, N2H, RS2, N2, GL, ACT, GH,
    G2P, G2S, G2R, OUTP, OS, OR, GMID, GBP, ET, GONE, BO, IG,
    SMI, SMG, SMO, SMR, SMT, SMS, FULL,
    gs, gr, zs, zr, ms, mr, es, er, rs_s, rs_r, os_s, os_r, qs, qr,
):
    d = lax.axis_index("dp")
    z = lax.axis_index("tensor")
    chip = d // 2
    c = d % 2
    chip_x = chip + 1 - 2 * (chip % 2)
    chip_y = (chip + 2) % 4
    chip_d = 3 - chip
    first = (1 - c) * chip_y + c * chip_x
    second = (1 - c) * chip_x + c * chip_y
    zx = [z, z + 1 - 2 * (z % 2), (z + 2) % 4, 3 - z]
    dev_s = (chip * 2 + 1 - c, z)
    dev_x = (chip_x * 2 + c, z)
    dev_y = (chip_y * 2 + c, z)
    dev_1 = (first * 2 + c, z)
    dev_2 = (second * 2 + c, z)
    dev_z = [None] + [(d, zx[k]) for k in (1, 2, 3)]

    def copy(src, dst, ssem, rsem, dev):
        return pltpu.make_async_remote_copy(
            src_ref=src, dst_ref=dst, send_sem=ssem, recv_sem=rsem, device_id=dev, device_id_type=MESH
        )

    def send(src, dst, ssem, rsem, dev):
        copy(src, dst, ssem, rsem, dev).start()

    def got(dst, rsem):
        copy(dst, dst, rsem, rsem, dev_s).wait_recv()

    def sent(src, ssem):
        copy(src, src, ssem, ssem, dev_s).wait_send()

    def slot(k):
        return zx[k] if k < 4 else k

    def s0(k):
        s = slot(k)
        if k in (1, 2, 3):
            got(G.at[s, chip, c], zr.at[k])
        if k in (5, 7):
            got(G.at[s, chip, c], zr.at[k])
        item = G.at[s, chip, c]
        send(item, item, gs.at[k, 0], gr.at[k, 0], dev_x)
        send(item, item, gs.at[k, 1], gr.at[k, 1], dev_y)
        send(item, item, gs.at[k, 3], gr.at[k, 3], dev_s)

    def s1(k):
        s = slot(k)
        got(G.at[s, chip_x, c], gr.at[k, 0])
        got(G.at[s, chip_y, c], gr.at[k, 1])
        item = G.at[s, second, c]
        send(item, item, gs.at[k, 2], gr.at[k, 2], dev_1)
        item = G.at[s, chip_x, c]
        send(item, item, gs.at[k, 4], gr.at[k, 4], dev_s)
        item = G.at[s, chip_y, c]
        send(item, item, gs.at[k, 5], gr.at[k, 5], dev_s)

    def s2(k):
        s = slot(k)
        got(G.at[s, chip_d, c], gr.at[k, 2])
        item = G.at[s, chip_d, c]
        send(item, item, gs.at[k, 6], gr.at[k, 6], dev_s)

    def s3(k):
        s = slot(k)
        for j, from_chip in ((3, chip), (4, chip_x), (5, chip_y), (6, chip_d)):
            got(G.at[s, from_chip, 1 - c], gr.at[k, j])

    def gather_step(t):
        if t <= 7:
            s0(t)
        if 1 <= t <= 8:
            s1(t - 1)
        if 2 <= t <= 9:
            s2(t - 2)

    far = {0: 2, 1: 2, 4: 3, 5: 2, 6: 1}

    def r0(p):
        send(GB.at[p, :, 1 - c], RBS.at[p], rs_s.at[p, 0], rs_r.at[p, 0], dev_s)

    def r1(p):
        got(RBS.at[p], rs_r.at[p, 0])
        T1[p, 0] = (GB[p, chip_d, c].astype(F32) + RBS[p, chip_d].astype(F32)).astype(BF)
        T1[p, 1] = (GB[p, first, c].astype(F32) + RBS[p, first].astype(F32)).astype(BF)
        send(T1.at[p], R1.at[p], rs_s.at[p, 1], rs_r.at[p, 1], dev_1)

    def r2(p):
        got(R1.at[p], rs_r.at[p, 1])
        T2[p] = (
            GB[p, second, c].astype(F32) + RBS[p, second].astype(F32) + R1[p, 0].astype(F32)
        ).astype(BF)
        send(T2.at[p], R2.at[p], rs_s.at[p, 2], rs_r.at[p, 2], dev_2)

    def r3(p):
        got(R2.at[p], rs_r.at[p, 2])
        own = (
            GB[p, chip, c].astype(F32)
            + RBS[p, chip].astype(F32)
            + R1[p, 1].astype(F32)
            + R2[p].astype(F32)
        )
        if p in far:
            ZB[p] = own.astype(BF)
            send(ZB.at[p], RZ.at[p], rs_s.at[p, 3], rs_r.at[p, 3], dev_z[far[p]])
        elif p == 2:
            g_u[...] = own
        elif p == 3:
            g_d[...] = own
        else:
            g_a[...] = own

    def reduce_step(t):
        if 0 <= t <= 7:
            r0(t)
        if 1 <= t <= 8:
            r1(t - 1)
        if 2 <= t <= 9:
            r2(t - 2)
        if 3 <= t <= 10:
            r3(t - 3)

    barrier = pltpu.get_barrier_semaphore()
    for dev in (dev_s, dev_x, dev_y, dev_z[1], dev_z[2], dev_z[3]):
        pl.semaphore_signal(barrier, inc=1, device_id=dev, device_id_type=MESH)

    src_row = iota((192, 768), 0)
    src_lane = iota((192, 768), 1)

    def place(at):
        return hot(src_lane == src_row + at)

    shard = dot(w_in[0].astype(BF), place(0)) + dot(w_in[2].astype(BF), place(192))
    shard = shard + dot(w_in[1].astype(BF), place(384)) + dot_tn(w_out[...].astype(BF), place(576))
    G[z, chip, c] = shard.astype(BF)
    G[4, chip, c] = w_up[...].astype(BF)
    eye = hot(iota((SHARD, SHARD), 0) == iota((SHARD, SHARD), 1))
    G[6, chip, c] = dot_nt(eye, w_dn[...].astype(BF)).astype(BF)
    SMI[...] = jnp.zeros_like(SMI)
    eye8 = hot(iota((8, HG), 0) == iota((8, HG), 1))
    tab_rows = sum(dot_nt(eye8, part) for part in split_three(tab[...]))
    SMI[0:8, 0:529] = tab_rows
    bias_row = sum(dot(part, place(0)) for part in split_three(hb[0:1, :]))
    bias_row = bias_row + sum(dot(part, place(192)) for part in split_three(hb[1:2, :]))
    SMI[6:7, :] = bias_row
    SMI[8:9, :] = ub[...].reshape(1, FQ)
    pl.semaphore_wait(barrier, 6)

    for k in (1, 2, 3):
        send(SMI, SMG.at[z], ms.at[k], mr.at[k], dev_z[k])
    for k in (1, 2, 3):
        item = G.at[z, chip, c]
        send(item, item, zs.at[k], zr.at[k], dev_z[k])
    send(G.at[4, chip, c], G.at[5, chip, c], zs.at[5], zr.at[5], dev_z[2])
    send(G.at[6, chip, c], G.at[7, chip, c], zs.at[7], zr.at[7], dev_z[2])
    gather_step(0)
    SMG[z] = SMI[...]

    ET[...] = pad_hot_t()
    xp = dot(padded_rows(z), img[...])
    XC[...] = dot(ET[...], xp.astype(BF))
    normal, rs = norm_stats(xp)
    N1[...] = normal
    RS1[...] = rs
    LOW1[...] = (normal * nv[0:1, :] + nv[1:2, :]).astype(BF)
    keep = msk[0].astype(F32)
    GL[0] = (dot(compact_rows(z), cot[...]) * keep).astype(BF)
    GL[1] = (dot(compact_rows(zx[1]), cot[...]) * keep).astype(BF)
    BR[...] = jnp.zeros_like(BR)
    GONE[...] = jnp.zeros_like(GONE)
    DZ[...] = jnp.zeros_like(DZ)
    SMO[...] = jnp.zeros_like(SMO)
    gather_step(1)

    for k in (1, 2, 3):
        got(SMG.at[zx[k]], mr.at[k])
    table = SMG[:, 0:8, 0:TABL].reshape(32, TABL)
    table_parts = jnp.concatenate(split_three(table), axis=0)

    def spread_step(ci, carry):
        parts = dot(table_parts, offset_hot(ci))
        parts = parts[0:32] + parts[32:64] + parts[64:96]
        for t in range(3):
            ZT[t, pl.ds(ci, 32, stride=ROWP), :] = parts[:, t * 128 : t * 128 + 128]
        return carry

    ZT[...] = jnp.zeros_like(ZT)
    lax.fori_loop(0, WIN, spread_step, 0)

    qi = iota((WPAD, 1), 0)
    kj = iota((1, WPAD), 1)
    q_r, q_c = lax.shift_right_logical(qi, 4), jnp.bitwise_and(qi, ROWP - 1)
    k_r, k_c = lax.shift_right_logical(kj, 4), jnp.bitwise_and(kj, ROWP - 1)
    cut_r = ((q_r >= SHIFT) != (k_r >= SHIFT)) & (z // 2 == 1)
    cut_c = ((q_c >= SHIFT) != (k_c >= SHIFT)) & (z % 2 == 1)
    fill = jnp.where(cut_r | cut_c, FILL_VALUE, 0.0)
    fill = jnp.where(k_c < WIN, fill, -1e30)
    DS[0] = fill.astype(BF)
    z_high, z_low = split_two(jnp.concatenate([ZT[0], ZT[1], ZT[2]], axis=1))

    def bias_step(ri, carry):
        pick = hot(iota((ZL, WPAD), 0) == iota((ZL, WPAD), 1) + (WIN - 1 - ri) * ROWP)
        at = pl.ds(pl.multiple_of(ri * ROWP, ROWP), ROWP)
        block = (dot(z_high, pick) + dot(z_low, pick)).reshape(32, ROWP, WPAD)
        block = block + DS[0, at, :].astype(F32)[None]
        for zz in range(4):
            PB[zz * HG : zz * HG + HG, at, :] = block[zz * 8 : zz * 8 + HG]
        return carry

    lax.fori_loop(0, WIN, bias_step, 0)

    def zk(k):
        return (z // 2 + k // 2) % 2 * 2 + (z % 2 + k % 2) % 2

    def group_forward(zz):
        whole = G[zz].reshape(768, 768)
        qvk = (dot(LOW1[...], whole) + SMG[zz, 6:7, :]).astype(BF)
        QVK[zz] = qvk
        mixed = [None, None]
        for e in range(HG):
            ta, la, tb, lb = e // 4, 32 * (e % 4), (e + 2) // 4, 32 * ((e + 2) % 4)
            q_t = qvk[:, ta * 128 : ta * 128 + 128]
            k_t = qvk[:, 384 + ta * 128 : 512 + ta * 128]
            v_t = qvk[:, 128 + tb * 128 : 256 + tb * 128]
            s = dot_nt(mask_head(q_t, la), k_t) * SCALE + PB[zz * HG + e]
            p = jnp.exp(s - jnp.max(s, axis=-1, keepdims=True))
            p = p * (1.0 / jnp.sum(p, axis=-1, keepdims=True))
            PB[zz * HG + e] = p
            add = dot(p.astype(BF), mask_head(v_t, lb))
            mixed[tb] = add if mixed[tb] is None else mixed[tb] + add
        mixed = jnp.concatenate(mixed, axis=1).astype(BF)
        MX[zz] = mixed
        BR[...] += dot_nt(dot(ET[...], mixed).astype(BF), whole[:, 512:768])

    def forward_step(k, carry):
        for j in range(4):
            @pl.when(k == j)
            def _():
                gather_step(j + 2)
                s3(j)

        group_forward(zk(k))
        return carry

    lax.fori_loop(0, 4, forward_step, 0)

    gather_step(6)
    normal, rs = norm_stats(XC[...] + BR[...] + nv[4:5, :])
    N2H[...] = normal
    RS2[...] = rs
    N2[0] = (normal * nv[2:3, :] + nv[3:4, :]).astype(BF)
    send(N2.at[0], N2.at[1], es.at[0], er.at[0], dev_z[1])

    def ff_block(b):
        rows = N2[b]
        grads = GL[b]

        def ff_step(i, carry):
            q, n = i // 3, i % 3
            at = pl.ds(pl.multiple_of(n * 256, 256), 256)
            up = G[4 + q, :, :, :, at].reshape(768, 256)
            down = G[6 + q, :, :, :, at].reshape(768, 256)
            zq = (z // 2 + q) % 2 * 2 + z % 2
            u = dot(rows, up) + SMG[zq, 8:9, at]
            u2 = u * u
            th = jnp.tanh(0.7978845608028654 * (u + 0.044715 * (u2 * u)))
            half = 0.5 * (1.0 + th)
            ACT[q, b, :, at] = (u * half).astype(BF)
            slope = half + 0.5 * u * (1.0 - th * th) * (
                0.7978845608028654 * (1.0 + 3 * 0.044715 * u2)
            )
            GH[q, b, :, at] = (dot(grads, down) * slope).astype(BF)
            return carry

        lax.fori_loop(0, 6, ff_step, 0)

    def ff_two(b):
        return dot_nt(GH[0, b], G[4].reshape(768, 768)) + dot_nt(GH[1, b], G[5].reshape(768, 768))

    def ff_out(b):
        return dot_nt(ACT[0, b], G[6].reshape(768, 768)) + dot_nt(ACT[1, b], G[7].reshape(768, 768))

    gather_step(7)
    gather_step(8)
    gather_step(9)
    for k in (4, 5, 6, 7):
        s3(k)
    ff_block(0)
    got(N2.at[1], er.at[0])
    ff_block(1)
    G2S[...] = ff_two(1).astype(BF)
    send(G2S, G2R, es.at[1], er.at[1], dev_z[1])
    OS[...] = ff_out(1).astype(BF)
    send(OS, OR, es.at[2], er.at[2], dev_z[1])

    def ff_grad(p):
        q = 1 if p < 2 else 0
        left, right = (N2, GH) if p % 2 == 0 else (GL, ACT)

        def grad_step(j, carry):
            at = pl.ds(pl.multiple_of(j * 384, 384), 384)
            rows = left[:, :, at].reshape(2 * WTOK, 384)
            grad = dot_tn(rows, right[q].reshape(2 * WTOK, 768))
            GB[p, pl.ds(2 * j, 2)] = grad.astype(BF).reshape(2, 2, SHARD, 768)
            return carry

        lax.fori_loop(0, 2, grad_step, 0)

    ff_grad(0)
    reduce_step(0)
    ff_grad(1)
    reduce_step(1)
    G2P[...] = ff_two(0)
    ff_grad(2)
    reduce_step(2)
    ff_grad(3)
    reduce_step(3)
    OUTP[...] = ff_out(0)

    for q in range(2):
        zq = (z // 2 + q) % 2 * 2 + z % 2
        SMO[zq, 8:9, :] = col_sum(GH[q].reshape(2 * WTOK, 768).astype(F32))

    got(G2R, er.at[1])
    g2 = G2P[...] + G2R[...].astype(F32)
    g_out = GL[0].astype(F32)
    gain2 = col_sum(g2 * N2H[...])
    shift2 = col_sum(g2)
    g_mid = g_out + norm_back(g2, nv[2:3, :], N2H[...], RS2[...])
    GMID[...] = g_mid
    g_branch = g_mid.astype(BF)
    GBP[...] = dot(pad_hot(), g_branch).astype(BF)
    bias_b = col_sum(g_branch.astype(F32))
    bias_o = col_sum(g_out)

    def group_backward(zz, p_at):
        whole = G[zz].reshape(768, 768)
        d_out = dot(GBP[...], whole[:, 512:768]).astype(BF)
        qvk = QVK[zz]
        dq, dk, dv = [None, None], [None, None], [None, None]

        def add(parts, t, v):
            parts[t] = v if parts[t] is None else parts[t] + v

        for e in range(HG):
            ta, la, tb, lb = e // 4, 32 * (e % 4), (e + 2) // 4, 32 * ((e + 2) % 4)
            q_t = qvk[:, ta * 128 : ta * 128 + 128]
            k_t = qvk[:, 384 + ta * 128 : 512 + ta * 128]
            v_t = qvk[:, 128 + tb * 128 : 256 + tb * 128]
            p = PB[zz * HG + e]
            d_o = mask_head(d_out[:, tb * 128 : tb * 128 + 128], lb)
            dp = dot_nt(d_o, v_t)
            add(dv, tb, dot_tn(p.astype(BF), d_o))
            ds = (p * (dp - jnp.sum(dp * p, axis=-1, keepdims=True))).astype(BF)
            DS[e] = ds
            add(dq, ta, dot(ds, mask_head(k_t, la)))
            add(dk, ta, dot_tn(ds, mask_head(q_t, la)))
        dq = [v * SCALE for v in dq]
        dk = [v * SCALE for v in dk]
        full = jnp.concatenate(
            [dq[0], dq[1] + dv[0], dv[1], dk[0], dk[1], jnp.zeros_like(dk[1])], axis=1
        ).astype(BF)
        GONE[...] += dot_nt(full[:, 0:640], whole[:, 0:640])
        SMO[zz, 6:7, :] = col_sum(full.astype(F32))
        FULL[...] = full

        def grad_step(j, carry):
            at = pl.ds(pl.multiple_of(j * 384, 384), 384)
            rows = LOW1[:, at]
            main = dot_tn(rows, FULL[:, 0:512])
            tail = dot_tn(rows, FULL[:, 512:768]) + dot_tn(GBP[:, at], MX[zz])
            grad = jnp.concatenate([main, tail], axis=1).astype(BF)
            GB[p_at, pl.ds(2 * j, 2)] = grad.reshape(2, 2, SHARD, 768)
            return carry

        lax.fori_loop(0, 2, grad_step, 0)

        def table_step(ri, carry):
            at = pl.ds(pl.multiple_of(ri * ROWP, ROWP), ROWP)
            pick = hot(iota((WPAD, ZL), 1) == iota((WPAD, ZL), 0) + (WIN - 1 - ri) * ROWP)
            rows = DS[:, at, :].reshape(HG * ROWP, WPAD)
            sums = dot(rows, pick)
            own = pl.ds(pl.multiple_of(zz * 8 * ROWP, 8 * ROWP), HG * ROWP)
            for t in range(3):
                DZ[t, own, :] += sums[:, t * 128 : t * 128 + 128]
            return carry

        lax.fori_loop(0, WIN, table_step, 0)

    def backward_step(i, carry):
        group_backward(zk(3 - i), 4 + i)
        for j in range(4):
            @pl.when(i == j)
            def _():
                reduce_step(4 + j)
                if j == 0:
                    got(OR, er.at[2])
                    out = OUTP[...] + OR[...].astype(F32) + nv[5:6, :]
                    BO[z] = (XC[...] + BR[...] + nv[4:5, :] + out).astype(BF)
                    for k in (1, 2, 3):
                        send(BO.at[z], BO.at[z], os_s.at[0, k], os_r.at[0, k], dev_z[k])
        return carry

    lax.fori_loop(0, 4, backward_step, 0)

    g_one = GONE[...]
    gain1 = col_sum(g_one * N1[...])
    shift1 = col_sum(g_one)
    back = norm_back(g_one, nv[0:1, :], N1[...], RS1[...])
    b_high, b_low = split_two(back)
    back = dot(ET[...], b_high) + dot(ET[...], b_low)
    IG[z] = (GMID[...] + back).astype(BF)
    for k in (1, 2, 3):
        send(IG.at[z], IG.at[z], os_s.at[1, k], os_r.at[1, k], dev_z[k])
    reduce_step(8)

    def table_sum(ci, total):
        rows = jnp.concatenate([DZ[t, pl.ds(ci, 32, stride=ROWP), :] for t in range(3)], axis=1)
        high, low = split_two(rows)
        parts = dot_nt(jnp.concatenate([high, low], axis=0), offset_hot(ci))
        return total + parts[0:32] + parts[32:64]

    total = lax.fori_loop(0, WIN, table_sum, jnp.zeros((32, TABL), F32))
    for zz in range(4):
        SMO[zz, 0:HG, 0:TABL] = total[zz * 8 : zz * 8 + HG]
        for j, row in enumerate((gain1, shift1, gain2, shift2, bias_b, bias_o)):
            SMO[zz, 9 + j : 10 + j, :] = row
    for k in (1, 2, 3):
        send(SMO.at[zx[k]], SMR.at[k], qs.at[k], qr.at[k], dev_z[k])
    reduce_step(9)
    small = SMO[z]
    for k in (1, 2, 3):
        got(SMR.at[k], qr.at[k])
        small = small + SMR[k]
    reduce_step(10)
    for j, dev in enumerate((dev_s, dev_x, dev_y)):
        SMT[j] = small
        send(SMT.at[j], SMS.at[j], qs.at[4 + j], qr.at[4 + j], dev)
        got(SMS.at[j], qr.at[4 + j])
        small = small + SMS[j]
    sm_out[...] = small

    for p in far:
        got(RZ.at[p], rs_r.at[p, 3])
    g_u[...] += RZ[0].astype(F32)
    g_d[...] += RZ[1].astype(F32)
    g_a[...] += RZ[4].astype(F32) + RZ[5].astype(F32) + RZ[6].astype(F32)
    for k in (1, 2, 3):
        got(BO.at[zx[k]], os_r.at[0, k])
        got(IG.at[zx[k]], os_r.at[1, k])
    bo_out[...] = BO[...]
    ig_out[...] = IG[...]

    item = G.at[0, 0, 0]
    for k in (1, 2, 3):
        sent(SMI, ms.at[k])
        sent(item, zs.at[k])
        sent(BO.at[0], os_s.at[0, k])
        sent(IG.at[0], os_s.at[1, k])
        sent(SMI, qs.at[k])
        sent(SMI, qs.at[3 + k])
    sent(item, zs.at[5])
    sent(item, zs.at[7])
    sent(G2S, es.at[0])
    sent(G2S, es.at[1])
    sent(OS, es.at[2])
    for k in range(8):
        for j in range(7):
            sent(item, gs.at[k, j])
    for p in range(8):
        sent(RBS.at[p], rs_s.at[p, 0])
        sent(T1.at[p], rs_s.at[p, 1])
        sent(T2.at[p], rs_s.at[p, 2])
    for p in far:
        sent(ZB.at[p], rs_s.at[p, 3])


def vm(shape, dtype=F32):
    return pltpu.VMEM(shape, dtype)


def main_call(args):
    f32 = lambda *s: jax.ShapeDtypeStruct(s, F32)
    bf = lambda *s: jax.ShapeDtypeStruct(s, BF)
    dma = lambda *s: pltpu.SemaphoreType.DMA(s)
    vspec = pl.BlockSpec(memory_space=pltpu.VMEM)
    specs = [vspec] * len(args)
    specs[2] = pl.BlockSpec(memory_space=pltpu.SMEM)
    scratch = [
        vm((8, 4, 2, SHARD, 768), BF),
        vm((8, 4, 2, SHARD, 768), BF),
        vm((8, 4, SHARD, 768), BF),
        vm((8, 2, SHARD, 768), BF),
        vm((8, 2, SHARD, 768), BF),
        vm((8, SHARD, 768), BF),
        vm((8, SHARD, 768), BF),
        vm((8, SHARD, 768), BF),
        vm((8, SHARD, 768), BF),
        vm((4 * HG, WPAD, WPAD)),
        vm((3, 32 * ROWP, 128)),
        vm((4, WPAD, 768), BF),
        vm((4, WPAD, 256), BF),
        vm((HG, WPAD, WPAD), BF),
        vm((3, 32 * ROWP, 128)),
        vm((WPAD, 768), BF),
        vm((WPAD, 768)),
        vm((WPAD, 1)),
        vm((WTOK, 768)),
        vm((WTOK, 768)),
        vm((WTOK, 768)),
        vm((WTOK, 1)),
        vm((2, WTOK, 768), BF),
        vm((2, WTOK, 768), BF),
        vm((2, 2, WTOK, FQ), BF),
        vm((2, 2, WTOK, FQ), BF),
        vm((WTOK, 768)),
        vm((WTOK, 768), BF),
        vm((WTOK, 768), BF),
        vm((WTOK, 768)),
        vm((WTOK, 768), BF),
        vm((WTOK, 768), BF),
        vm((WTOK, 768)),
        vm((WPAD, 768), BF),
        vm((WTOK, WPAD), BF),
        vm((WPAD, 768)),
        vm((4, WTOK, 768), BF),
        vm((4, WTOK, 768), BF),
        vm((16, 768)),
        vm((4, 16, 768)),
        vm((4, 16, 768)),
        vm((4, 16, 768)),
        vm((3, 16, 768)),
        vm((3, 16, 768)),
        vm((WPAD, 768), BF),
        dma(8, 7), dma(8, 7),
        dma(8), dma(8),
        dma(4), dma(4),
        dma(3), dma(3),
        dma(8, 4), dma(8, 4),
        dma(2, 4), dma(2, 4),
        dma(8), dma(8),
    ]
    return pl.pallas_call(
        main_kernel,
        out_shape=(
            f32(SHARD, 768), f32(SHARD, 768), f32(SHARD, 768), f32(16, 768),
            bf(4, WTOK, 768), bf(4, WTOK, 768),
        ),
        in_specs=specs,
        out_specs=tuple([vspec] * 6),
        scratch_shapes=scratch,
        compiler_params=pltpu.CompilerParams(
            collective_id=0, has_side_effects=True, vmem_limit_bytes=62 * 2**20
        ),
        cost_estimate=pl.CostEstimate(flops=7 * 10**9, bytes_accessed=10**7, transcendentals=10**6),
    )(*args)


def last_kernel(
    g_a, g_u, g_d, sm, bo, ig,
    in_w, in_f, in_s, out_w, out_f, out_s, up_w, up_f, up_s, dn_w, dn_f, dn_s,
    nv_w, nv_f, nv_s, hb_w, hb_f, hb_s, ub_w, ub_f, ub_s, tb_w, tb_f, tb_s,
    block_out, image_grad,
    in_m, in_q, in_u, in_c, out_m, out_q, out_u, out_c, up_m, up_q, up_u, up_c, dn_m, dn_q, dn_u, dn_c,
    nv_m, nv_q, nv_u, hb_m, hb_q, hb_u, ub_m, ub_q, ub_u, tb_m, tb_q, tb_u,
):
    highest = lax.Precision.HIGHEST

    def exact(a, b, dims):
        return lax.dot_general(a, b, (dims, ((), ())), precision=highest, preferred_element_type=F32)

    token = iota((TOK, 1), 0)
    row = lax.shift_right_logical(token * 2731, 16)
    col = token - row * SIDE
    row = jnp.where(row >= SHIFT, row - SHIFT, row + SIDE - SHIFT)
    col = jnp.where(col >= SHIFT, col - SHIFT, col + SIDE - SHIFT)
    wr, wc = (row >= WIN).astype(jnp.int32), (col >= WIN).astype(jnp.int32)
    at = (wr * 2 + wc) * WTOK + (row - WIN * wr) * WIN + col - WIN * wc
    back = hot(at == iota((TOK, TOK), 1))
    block_out[0] = dot(back, bo[...].reshape(TOK, 768)).astype(BF)
    image_grad[0] = dot(back, ig[...].reshape(TOK, 768))

    def adam(w, f, s, g, rate, decay):
        return adam_update(w, f, s, g, rate, decay)

    for j, lane in ((0, 0), (1, 384), (2, 192)):
        m, q, u = adam(in_w[j], in_f[j], in_s[j], g_a[:, lane : lane + 192], RATE_MATRIX, DECAY_MATRIX)
        in_m[j], in_q[j], in_u[j], in_c[j] = m, q, u, u.astype(BF)
    eye = jnp.where(iota((SHARD, SHARD), 0) == iota((SHARD, SHARD), 1), 1.0, 0.0)
    g_out = exact(g_a[:, 576:768], eye, ((0,), (0,)))
    m, q, u = adam(out_w[...], out_f[...], out_s[...], g_out, RATE_MATRIX, DECAY_MATRIX)
    out_m[...], out_q[...], out_u[...], out_c[...] = m, q, u, u.astype(BF)
    m, q, u = adam(up_w[...], up_f[...], up_s[...], g_u[...], RATE_MATRIX, DECAY_MATRIX)
    up_m[...], up_q[...], up_u[...], up_c[...] = m, q, u, u.astype(BF)
    g_dn = exact(g_d[...], eye, ((0,), (0,)))
    m, q, u = adam(dn_w[...], dn_f[...], dn_s[...], g_dn, RATE_MATRIX, DECAY_MATRIX)
    dn_m[...], dn_q[...], dn_u[...], dn_c[...] = m, q, u, u.astype(BF)

    m, q, u = adam(nv_w[...], nv_f[...], nv_s[...], sm[9:15, :], RATE_VECTOR, 0.0)
    nv_m[...], nv_q[...], nv_u[...] = m, q, u
    for j in (0, 1):
        g = sm[6:7, 192 * j : 192 * j + 192]
        m, q, u = adam(hb_w[j : j + 1, :], hb_f[j : j + 1, :], hb_s[j : j + 1, :], g, RATE_VECTOR, 0.0)
        hb_m[j : j + 1, :], hb_q[j : j + 1, :], hb_u[j : j + 1, :] = m, q, u
    g = sm[8:9, :].reshape(FQ)
    m, q, u = adam(ub_w[...], ub_f[...], ub_s[...], g, RATE_VECTOR, 0.0)
    ub_m[...], ub_q[...], ub_u[...] = m, q, u
    eye6 = jnp.where(iota((8, HG), 0) == iota((8, HG), 1), 1.0, 0.0)
    g_tab = exact(sm[0:8, 0:529], eye6, ((0,), (0,)))
    m, q, u = adam(tb_w[...], tb_f[...], tb_s[...], g_tab, RATE_VECTOR, 0.0)
    tb_m[...], tb_q[...], tb_u[...] = m, q, u


def last_call(sums, params):
    vspec = pl.BlockSpec(memory_space=pltpu.VMEM)
    like = lambda a, t=F32: jax.ShapeDtypeStruct(a.shape, t)
    outs = [jax.ShapeDtypeStruct((1, TOK, 768), BF), jax.ShapeDtypeStruct((1, TOK, 768), F32)]
    for j in range(0, 12, 3):
        outs += [like(params[j])] * 3 + [like(params[j], BF)]
    for j in range(12, 24, 3):
        outs += [like(params[j])] * 3
    return pl.pallas_call(
        last_kernel,
        out_shape=tuple(outs),
        in_specs=[vspec] * (len(sums) + len(params)),
        out_specs=tuple([vspec] * len(outs)),
        compiler_params=pltpu.CompilerParams(vmem_limit_bytes=48 * 2**20),
        cost_estimate=pl.CostEstimate(flops=10**9, bytes_accessed=15 * 10**6, transcendentals=10**6),
    )(*sums, *params)


def on_device_windows(images, cotangent, image_mask, *params):
    (in_w, _, _, out_w, _, _, up_w, _, _, dn_w, _, _, nv, _, _, hb, _, _, ub, _, _, tab, _, _) = params
    sums = main_call(
        (
            images.reshape(TOK, D), cotangent.reshape(TOK, D), image_mask,
            in_w, out_w, up_w, dn_w, nv, hb, ub, tab,
        )
    )
    return last_call(sums, params)


def solution(mesh):
    shape = mesh.shape
    windows = shape["dp"] == 8 and shape["tensor"] == 4
    return jax.shard_map(
        on_device_windows if windows else on_device,
        mesh=mesh,
        in_specs=(
            P("dp", None, None),
            P("dp", None, None),
            P("dp"),
            P(None, "dp", "tensor"),
            P(None, "dp", "tensor"),
            P(None, "dp", "tensor"),
            P("tensor", "dp"),
            P("tensor", "dp"),
            P("tensor", "dp"),
            P("dp", "tensor"),
            P("dp", "tensor"),
            P("dp", "tensor"),
            P("tensor", "dp"),
            P("tensor", "dp"),
            P("tensor", "dp"),
            P(),
            P(),
            P(),
            P(None, "tensor"),
            P(None, "tensor"),
            P(None, "tensor"),
            P("tensor"),
            P("tensor"),
            P("tensor"),
            P(None, "tensor"),
            P(None, "tensor"),
            P(None, "tensor"),
        ),
        out_specs=(
            P("dp", None, None),
            P("dp", None, None),
            P(None, "dp", "tensor"),
            P(None, "dp", "tensor"),
            P(None, "dp", "tensor"),
            P(None, "dp", "tensor"),
            P("tensor", "dp"),
            P("tensor", "dp"),
            P("tensor", "dp"),
            P("tensor", "dp"),
            P("dp", "tensor"),
            P("dp", "tensor"),
            P("dp", "tensor"),
            P("dp", "tensor"),
            P("tensor", "dp"),
            P("tensor", "dp"),
            P("tensor", "dp"),
            P("tensor", "dp"),
            P(),
            P(),
            P(),
            P(None, "tensor"),
            P(None, "tensor"),
            P(None, "tensor"),
            P("tensor"),
            P("tensor"),
            P("tensor"),
            P(None, "tensor"),
            P(None, "tensor"),
            P(None, "tensor"),
        ),
        check_vma=False,
    )
```

```python
import functools
from functools import partial

import jax
import jax.numpy as jnp
from jax import lax
from jax.experimental import pallas as pl
from jax.experimental.pallas import tpu as pltpu
from jax.sharding import PartitionSpec as P

D = 768
HEAD_DIM = 32
WIN = 12
SIDE = 24
STEP = 7
SHIFT = 6


NORM_EPS = 1e-05
FILL_VALUE = -100.0
BETA_ONE = 0.5
BETA_TWO = 0.5
ADAM_EPS = 1e-08
RATE_MATRIX = 0.05
RATE_VECTOR = 0.3
DECAY_MATRIX = 0.05


def layer_norm(values, gain_in, offset_in):
    center = values - jnp.mean(values, axis=-1, keepdims=True)
    spread = jnp.mean(center * center, axis=-1, keepdims=True)
    return center * lax.rsqrt(spread + NORM_EPS) * gain_in + offset_in


def adam_update(weight, first_old, second_old, gradient, rate_of, decay_of):
    moment = BETA_ONE * first_old + (1.0 - BETA_ONE) * gradient
    square = BETA_TWO * second_old + (1.0 - BETA_TWO) * gradient * gradient
    moment_fix = moment / (1.0 - BETA_ONE**STEP)
    square_fix = square / (1.0 - BETA_TWO**STEP)
    updated = weight * (1.0 - rate_of * decay_of) - rate_of * moment_fix / (
        jnp.sqrt(square_fix) + ADAM_EPS
    )
    return (moment, square, updated)


def dot_plain(left_side, right_side):
    return jnp.dot(left_side, right_side, preferred_element_type=jnp.float32)


def dot_back(left_side, right_side):
    return lax.dot_general(
        left_side, right_side, (((1,), (1,)), ((), ())), preferred_element_type=jnp.float32
    )


def dot_rows(left_side, right_side):
    return lax.dot_general(
        left_side, right_side, (((0,), (0,)), ((), ())), preferred_element_type=jnp.float32
    )


def to_heads(token_rows, images_here, heads_here):
    blocks = SIDE // WIN
    grid_view = token_rows.reshape(images_here, SIDE, SIDE, heads_here * HEAD_DIM)
    grid_view = jnp.roll(grid_view, (-SHIFT, -SHIFT), (1, 2))
    grid_view = grid_view.reshape(
        images_here, blocks, WIN, blocks, WIN, heads_here, HEAD_DIM
    ).transpose(0, 1, 3, 2, 4, 5, 6)
    return grid_view.reshape(images_here, blocks * blocks, WIN * WIN, heads_here, HEAD_DIM)


def from_heads(windows, images_here):
    blocks = SIDE // WIN
    channels = windows.shape[3] * windows.shape[4]
    grid_view = windows.reshape(images_here, blocks, blocks, WIN, WIN, channels).transpose(
        0, 1, 3, 2, 4, 5
    )
    grid_view = jnp.roll(
        grid_view.reshape(images_here, SIDE, SIDE, channels), (SHIFT, SHIFT), (1, 2)
    )
    return grid_view.reshape(images_here * SIDE * SIDE, channels)


def window_fill():
    blocks = SIDE // WIN
    cell_ids = jnp.arange(SIDE, dtype=jnp.int32)
    band_of = (cell_ids >= SIDE - WIN).astype(jnp.int32) + (cell_ids >= SIDE - SHIFT).astype(
        jnp.int32
    )
    region = band_of[:, None] * 3 + band_of[None, :]
    labels = (
        region.reshape(blocks, WIN, blocks, WIN)
        .transpose(0, 2, 1, 3)
        .reshape(blocks * blocks, WIN * WIN)
    )
    return jnp.where(labels[:, :, None] != labels[:, None, :], FILL_VALUE, 0.0).astype(jnp.float32)


def offset_onehot():
    places = jnp.arange(WIN, dtype=jnp.int32)
    spans = jnp.arange(2 * WIN - 1, dtype=jnp.int32)
    return (places[:, None, None] - places[None, :, None] + WIN - 1 == spans[None, None, :]).astype(
        jnp.float32
    )


def window_scores(query_win, key_win, bias_add, fill_add):
    scores = jnp.einsum(
        "inqhd,inkhd->inhqk", query_win, key_win, preferred_element_type=jnp.float32
    ) * HEAD_DIM ** (-0.5)
    return scores + bias_add[None, None] + fill_add[None, :, None]


def on_device(
    images,
    cotangent,
    image_mask,
    in_weight,
    in_first,
    in_second,
    out_weight,
    out_first,
    out_second,
    up_weight,
    up_first,
    up_second,
    down_weight,
    down_first,
    down_second,
    norm_vector,
    norm_first,
    norm_second,
    head_bias,
    head_first,
    head_second,
    up_bias,
    bias_first,
    bias_second,
    position_table,
    table_first,
    table_second,
):
    lowtype = jnp.bfloat16
    highest = lax.Precision.HIGHEST
    whole_in, whole_out, whole_up, whole_down = (
        lax.all_gather(in_weight.astype(lowtype), "dp", axis=1, tiled=True),
        lax.all_gather(out_weight.astype(lowtype), "dp", axis=1, tiled=True),
        lax.all_gather(up_weight.astype(lowtype), "dp", axis=0, tiled=True),
        lax.all_gather(down_weight.astype(lowtype), "dp", axis=1, tiled=True),
    )
    images_here = images.shape[0]
    heads_here = whole_in.shape[2] // HEAD_DIM
    span_count = 2 * WIN - 1
    token_rows = images.reshape(-1, D).astype(jnp.float32)
    normed_one, norm_one_back = jax.vjp(layer_norm, token_rows, norm_vector[0], norm_vector[1])
    low_one = normed_one.astype(lowtype)
    query_rows = (dot_plain(low_one, whole_in[0]) + head_bias[0]).astype(lowtype)
    key_rows = dot_plain(low_one, whole_in[1]).astype(lowtype)
    value_rows = (dot_plain(low_one, whole_in[2]) + head_bias[1]).astype(lowtype)
    query_win = to_heads(query_rows, images_here, heads_here)
    key_win = to_heads(key_rows, images_here, heads_here)
    value_win = to_heads(value_rows, images_here, heads_here)
    onehot = offset_onehot()
    table_view = position_table.reshape(span_count, span_count, heads_here)
    bias_add = jnp.einsum(
        "xya,zwb,abh->hxzyw", onehot, onehot, table_view, precision=highest
    ).reshape(heads_here, WIN * WIN, WIN * WIN)
    fill_add = window_fill()
    scores = window_scores(query_win, key_win, bias_add, fill_add)
    row_top = jnp.max(scores, axis=-1, keepdims=True)
    weights_raw = jnp.exp(scores - row_top)
    row_total = jnp.sum(weights_raw, axis=-1, keepdims=True)
    log_total = row_top + jnp.log(row_total)
    prob_low = (weights_raw / row_total).astype(lowtype)
    mixed_win = jnp.einsum(
        "inhqk,inkhd->inqhd", prob_low, value_win, preferred_element_type=jnp.float32
    ).astype(lowtype)
    mixed_rows = from_heads(mixed_win, images_here)
    branch_share = lax.psum_scatter(
        dot_plain(mixed_rows, whole_out), "tensor", scatter_dimension=0, tiled=True
    )
    branch = lax.all_gather(branch_share, "tensor", axis=0, tiled=True) + norm_vector[4]
    middle = token_rows + branch
    normed_two, norm_two_back = jax.vjp(layer_norm, middle, norm_vector[2], norm_vector[3])
    low_two = normed_two.astype(lowtype)
    hidden = dot_plain(low_two, whole_up) + up_bias
    active, gelu_back = jax.vjp(partial(jax.nn.gelu, approximate=True), hidden)
    active_low = active.astype(lowtype)
    output_share = lax.psum_scatter(
        dot_plain(active_low, whole_down).astype(jnp.bfloat16),
        "tensor",
        scatter_dimension=0,
        tiled=True,
    ).astype(jnp.float32)
    output = (
        lax.all_gather(output_share.astype(jnp.bfloat16), "tensor", axis=0, tiled=True).astype(
            output_share.dtype
        )
        + norm_vector[5]
    )
    block_out = (middle + output).astype(lowtype).reshape(images.shape)
    keep_rows = jnp.repeat(image_mask.astype(jnp.float32), SIDE * SIDE)[:, None]
    grad_out = cotangent.reshape(-1, D).astype(jnp.float32) * keep_rows
    grad_low = grad_out.astype(lowtype)
    down_grad = dot_rows(active_low, grad_low)
    grad_hidden = gelu_back(dot_back(grad_low, whole_down))[0].astype(lowtype)
    up_grad = dot_rows(low_two, grad_hidden)
    bias_grad = jnp.sum(grad_hidden.astype(jnp.float32), axis=0)
    two_share = lax.psum_scatter(
        dot_back(grad_hidden, whole_up), "tensor", scatter_dimension=0, tiled=True
    )
    grad_two = lax.all_gather(two_share, "tensor", axis=0, tiled=True)
    grad_norm_two, gain_two, offset_two = norm_two_back(grad_two)
    grad_middle = grad_out + grad_norm_two
    grad_branch = grad_middle.astype(lowtype)
    out_grad = dot_rows(mixed_rows, grad_branch)
    grad_mixed = dot_back(grad_branch, whole_out).astype(lowtype)
    grad_win = to_heads(grad_mixed, images_here, heads_here)
    scores_again = window_scores(query_win, key_win, bias_add, fill_add)
    probs = jnp.exp(scores_again - log_total)
    grad_probs = jnp.einsum(
        "inqhd,inkhd->inhqk", grad_win, value_win, preferred_element_type=jnp.float32
    )
    grad_value = jnp.einsum(
        "inhqk,inqhd->inkhd", probs.astype(lowtype), grad_win, preferred_element_type=jnp.float32
    ).astype(lowtype)
    grad_scores = (
        probs * (grad_probs - jnp.sum(grad_probs * probs, axis=-1, keepdims=True))
    ).astype(lowtype)
    grad_query = (
        jnp.einsum("inhqk,inkhd->inqhd", grad_scores, key_win, preferred_element_type=jnp.float32)
        * HEAD_DIM ** (-0.5)
    ).astype(lowtype)
    grad_key = (
        jnp.einsum("inhqk,inqhd->inkhd", grad_scores, query_win, preferred_element_type=jnp.float32)
        * HEAD_DIM ** (-0.5)
    ).astype(lowtype)
    score_sums = jnp.sum(grad_scores.astype(jnp.float32), axis=(0, 1)).reshape(
        heads_here, WIN, WIN, WIN, WIN
    )
    table_grad = jnp.einsum(
        "xya,zwb,hxzyw->abh", onehot, onehot, score_sums, precision=highest
    ).reshape(span_count * span_count, heads_here)
    query_back = from_heads(grad_query, images_here)
    key_back = from_heads(grad_key, images_here)
    value_back = from_heads(grad_value, images_here)
    in_grad = jnp.stack(
        [dot_rows(low_one, query_back), dot_rows(low_one, key_back), dot_rows(low_one, value_back)]
    )
    head_grad = jnp.stack(
        [
            jnp.sum(query_back.astype(jnp.float32), axis=0),
            jnp.sum(value_back.astype(jnp.float32), axis=0),
        ]
    )
    grad_one_terms = (
        dot_back(query_back, whole_in[0])
        + dot_back(key_back, whole_in[1])
        + dot_back(value_back, whole_in[2])
    )
    one_share = lax.psum_scatter(
        grad_one_terms.astype(jnp.bfloat16), "tensor", scatter_dimension=0, tiled=True
    ).astype(jnp.float32)
    grad_one = lax.all_gather(one_share.astype(jnp.bfloat16), "tensor", axis=0, tiled=True).astype(
        one_share.dtype
    )
    grad_norm_one, gain_one, offset_one = norm_one_back(grad_one)
    image_grad = (grad_middle + grad_norm_one).reshape(images.shape)
    norm_grad = jnp.stack(
        [
            gain_one,
            offset_one,
            gain_two,
            offset_two,
            jnp.sum(grad_branch.astype(jnp.float32), axis=0),
            jnp.sum(grad_low.astype(jnp.float32), axis=0),
        ]
    )
    summed = lax.psum(
        (in_grad, out_grad, up_grad, down_grad, norm_grad, head_grad, bias_grad, table_grad), "dp"
    )
    position = lax.axis_index("dp")
    in_total = lax.dynamic_slice_in_dim(
        summed[0], position * in_weight.shape[1], in_weight.shape[1], 1
    )
    out_total = lax.dynamic_slice_in_dim(
        summed[1], position * out_weight.shape[1], out_weight.shape[1], 1
    )
    up_total = lax.dynamic_slice_in_dim(
        summed[2], position * up_weight.shape[0], up_weight.shape[0], 0
    )
    down_total = lax.dynamic_slice_in_dim(
        summed[3], position * down_weight.shape[1], down_weight.shape[1], 1
    )
    norm_total, head_total, bias_total, table_total = (summed[4], summed[5], summed[6], summed[7])
    in_moment, in_square, in_updated = adam_update(
        in_weight, in_first, in_second, in_total, RATE_MATRIX, DECAY_MATRIX
    )
    out_moment, out_square, out_updated = adam_update(
        out_weight, out_first, out_second, out_total, RATE_MATRIX, DECAY_MATRIX
    )
    up_moment, up_square, up_updated = adam_update(
        up_weight, up_first, up_second, up_total, RATE_MATRIX, DECAY_MATRIX
    )
    down_moment, down_square, down_updated = adam_update(
        down_weight, down_first, down_second, down_total, RATE_MATRIX, DECAY_MATRIX
    )
    norm_moment, norm_square, norm_updated = adam_update(
        norm_vector, norm_first, norm_second, norm_total, RATE_VECTOR, 0.0
    )
    head_moment, head_square, head_updated = adam_update(
        head_bias, head_first, head_second, head_total, RATE_VECTOR, 0.0
    )
    bias_moment, bias_square, bias_updated = adam_update(
        up_bias, bias_first, bias_second, bias_total, RATE_VECTOR, 0.0
    )
    table_moment, table_square, table_updated = adam_update(
        position_table, table_first, table_second, table_total, RATE_VECTOR, 0.0
    )
    return (
        block_out,
        image_grad,
        in_moment,
        in_square,
        in_updated,
        in_updated.astype(lowtype),
        out_moment,
        out_square,
        out_updated,
        out_updated.astype(lowtype),
        up_moment,
        up_square,
        up_updated,
        up_updated.astype(lowtype),
        down_moment,
        down_square,
        down_updated,
        down_updated.astype(lowtype),
        norm_moment,
        norm_square,
        norm_updated,
        head_moment,
        head_square,
        head_updated,
        bias_moment,
        bias_square,
        bias_updated,
        table_moment,
        table_square,
        table_updated,
    )


MESH = pl.DeviceIdType.MESH
TOK = SIDE * SIDE
WTOK = WIN * WIN
ROWP = 16
WPAD = WIN * ROWP
FQ = 768
SHARD = 96
HG = 6
TABL = 640
ZL = 384
SCALE = HEAD_DIM ** (-0.5)
F32 = jnp.float32
BF = jnp.bfloat16


def dot(a, b):
    return lax.dot_general(a, b, (((1,), (0,)), ((), ())), preferred_element_type=F32)


def dot_nt(a, b):
    return lax.dot_general(a, b, (((1,), (1,)), ((), ())), preferred_element_type=F32)


def dot_tn(a, b):
    return lax.dot_general(a, b, (((0,), (0,)), ((), ())), preferred_element_type=F32)


def iota(shape, axis):
    return lax.broadcasted_iota(jnp.int32, shape, axis)


def div12(i):
    return lax.shift_right_logical(i * 171, 11)


def hot(condition):
    return jnp.where(condition, 1.0, 0.0).astype(BF)


def split_two(v):
    high = v.astype(BF)
    return high, (v - high.astype(F32)).astype(BF)


def split_three(v):
    high, _ = split_two(v)
    rest = v - high.astype(F32)
    mid, low = split_two(rest)
    return high, mid, low


def token_of(row, col, win):
    r = row + WIN * (win // 2) + SHIFT
    c = col + WIN * (win % 2) + SHIFT
    r = jnp.where(r >= SIDE, r - SIDE, r)
    c = jnp.where(c >= SIDE, c - SIDE, c)
    return r * SIDE + c


def padded_rows(win):
    i = iota((WPAD, 1), 0)
    col = jnp.bitwise_and(i, ROWP - 1)
    token = token_of(lax.shift_right_logical(i, 4), col, win)
    token = jnp.where(col < WIN, token, -1)
    return hot(token == iota((WPAD, TOK), 1))


def compact_rows(win):
    i = iota((WTOK, 1), 0)
    row = div12(i)
    return hot(token_of(row, i - WIN * row, win) == iota((WTOK, TOK), 1))


def pad_hot():
    j = iota((WPAD, WTOK), 1)
    return hot(iota((WPAD, WTOK), 0) == j + 4 * div12(j))


def pad_hot_t():
    j = iota((WTOK, WPAD), 0)
    return hot(iota((WTOK, WPAD), 1) == j + 4 * div12(j))


def offset_hot(ci):
    lane = iota((1, ZL), 1)
    cj = jnp.bitwise_and(lane, ROWP - 1)
    u = lax.shift_right_logical(lane, 4)
    entry = (22 - u) * 23 + 11 + ci - cj
    entry = jnp.where((cj < WIN) & (u < 23), entry, -1)
    return hot(iota((TABL, ZL), 0) == entry)


def mask_head(tile, lane0):
    lane = iota((1, 128), 1)
    return jnp.where((lane >= lane0) & (lane < lane0 + HEAD_DIM), tile, jnp.zeros_like(tile))


def norm_stats(values):
    center = values - jnp.mean(values, axis=-1, keepdims=True)
    spread = jnp.mean(center * center, axis=-1, keepdims=True)
    rs = lax.rsqrt(spread + NORM_EPS)
    return center * rs, rs


def norm_back(grad, gain, normal, rs):
    e = grad * gain
    return rs * (
        e
        - jnp.mean(e, axis=-1, keepdims=True)
        - normal * jnp.mean(e * normal, axis=-1, keepdims=True)
    )


def col_sum(v):
    return jnp.sum(v, axis=0, keepdims=True)


def main_kernel(
    img_in, cot_in, msk, w_in, w_out, w_up, w_dn, nv, hb, ub, tab,
    ga_out, gu_out, gd_out, sm_out, bo_out, ig_out,
    G, GB, RBS, T1, R1, T2, R2, ZB, RZ,
    PB, ZT, QVK, MX, DS, DZ, LOW1, N1, RS1, XC, BR, N2H, RS2, N2, GL, ACT, GH,
    G2P, G2S, G2R, OUTP, OS, OR, GMID, GBP, ET, GONE, BO, IG,
    SMI, SMG, SMO, SMR, SMT, SMS, FULL, img, cot, g_a, g_u, g_d,
    gs, gr, zs, zr, ms, mr, es, er, rs_s, rs_r, os_s, os_r, qs, qr, ls,
):
    def local(src, dst, j):
        return pltpu.make_async_copy(src, dst, ls.at[j])

    local(img_in, img, 0).start()
    local(cot_in, cot, 1).start()
    d = lax.axis_index("dp")
    z = lax.axis_index("tensor")
    chip = d // 2
    c = d % 2
    chip_x = chip + 1 - 2 * (chip % 2)
    chip_y = (chip + 2) % 4
    chip_d = 3 - chip
    first = (1 - c) * chip_y + c * chip_x
    second = (1 - c) * chip_x + c * chip_y
    zx = [z, z + 1 - 2 * (z % 2), (z + 2) % 4, 3 - z]
    half = z // 2
    near = [z, zx[1], 2 - half, 3 - 3 * half]
    dev_s = (chip * 2 + 1 - c, z)
    dev_x = (chip_x * 2 + c, z)
    dev_y = (chip_y * 2 + c, z)
    dev_1 = (first * 2 + c, z)
    dev_2 = (second * 2 + c, z)
    dev_z = [None] + [(d, zx[k]) for k in (1, 2, 3)]

    def copy(src, dst, ssem, rsem, dev):
        return pltpu.make_async_remote_copy(
            src_ref=src, dst_ref=dst, send_sem=ssem, recv_sem=rsem, device_id=dev, device_id_type=MESH
        )

    def send(src, dst, ssem, rsem, dev):
        copy(src, dst, ssem, rsem, dev).start()

    def got(dst, rsem):
        copy(dst, dst, rsem, rsem, dev_s).wait_recv()

    def sent(src, ssem):
        copy(src, src, ssem, ssem, dev_s).wait_send()

    def blocks_of(ref):
        return lambda block: ref.at[block]

    def own_items(block):
        return G.at[block, chip, c]

    dev_up = (d, (z + 1) % 4)
    dev_dn = (d, (z + 3) % 4)

    def line_send(buf, which, j, block, live_up, live_dn):
        def go(ok, side, dev):
            @pl.when(ok)
            def _():
                send(buf(block), buf(block), os_s.at[which, j, side], os_r.at[which, block], dev)

        go(live_up, 0, dev_up)
        go(live_dn, 1, dev_dn)

    def line_start(buf, which):
        line_send(buf, which, 0, z, z < 3, z > 0)

    def line_step(buf, which, j):
        below, above = (z + 4 - j) % 4, (z + j) % 4

        @pl.when(z >= j)
        def _():
            got(buf(below), os_r.at[which, below])

            @pl.when(z < 3)
            def _():
                send(buf(below), buf(below), os_s.at[which, j, 0], os_r.at[which, below], dev_up)

        @pl.when(z + j <= 3)
        def _():
            got(buf(above), os_r.at[which, above])

            @pl.when(z > 0)
            def _():
                send(buf(above), buf(above), os_s.at[which, j, 1], os_r.at[which, above], dev_dn)

    def line_drain(buf, which):
        for j in range(4):
            @pl.when((z >= j) & (z < 3))
            def _():
                sent(buf(0), os_s.at[which, j, 0])

            @pl.when((z + j <= 3) & (z > 0))
            def _():
                sent(buf(0), os_s.at[which, j, 1])

    def slot(k):
        return near[k] if k < 4 else k

    def s0(k):
        s = slot(k)
        if k in (6, 7):
            got(G.at[s, chip, c], zr.at[k])
        item = G.at[s, chip, c]
        send(item, item, gs.at[k, 0], gr.at[k, 0], dev_x)
        send(item, item, gs.at[k, 1], gr.at[k, 1], dev_y)
        send(item, item, gs.at[k, 3], gr.at[k, 3], dev_s)

    def s1(k):
        s = slot(k)
        got(G.at[s, chip_x, c], gr.at[k, 0])
        got(G.at[s, chip_y, c], gr.at[k, 1])
        item = G.at[s, second, c]
        send(item, item, gs.at[k, 2], gr.at[k, 2], dev_1)
        item = G.at[s, chip_x, c]
        send(item, item, gs.at[k, 4], gr.at[k, 4], dev_s)
        item = G.at[s, chip_y, c]
        send(item, item, gs.at[k, 5], gr.at[k, 5], dev_s)

    def s2(k):
        s = slot(k)
        got(G.at[s, chip_d, c], gr.at[k, 2])
        item = G.at[s, chip_d, c]
        send(item, item, gs.at[k, 6], gr.at[k, 6], dev_s)

    def s3(k):
        s = slot(k)
        for j, from_chip in ((3, chip), (4, chip_x), (5, chip_y), (6, chip_d)):
            got(G.at[s, from_chip, 1 - c], gr.at[k, j])

    def gather_step(t):
        if t == 0:
            line_start(own_items, 2)
        if 1 <= t <= 3:
            line_step(own_items, 2, t)
        if t == 2:
            for k in (6, 7):
                send(G.at[k - 2, chip, c], G.at[k, chip, c], zs.at[k], zr.at[k], dev_z[2])
        if t <= 7:
            s0(t)
        if 1 <= t <= 8:
            s1(t - 1)
        if 2 <= t <= 9:
            s2(t - 2)

    far = {2: 2, 3: 2, 4: 3, 5: 2, 6: 1}

    def r0(p):
        send(GB.at[p, :, 1 - c], RBS.at[p], rs_s.at[p, 0], rs_r.at[p, 0], dev_s)

    def r1(p):
        got(RBS.at[p], rs_r.at[p, 0])
        T1[p, 0] = (GB[p, chip_d, c].astype(F32) + RBS[p, chip_d].astype(F32)).astype(BF)
        T1[p, 1] = (GB[p, first, c].astype(F32) + RBS[p, first].astype(F32)).astype(BF)
        send(T1.at[p], R1.at[p], rs_s.at[p, 1], rs_r.at[p, 1], dev_1)

    def r2(p):
        got(R1.at[p], rs_r.at[p, 1])
        T2[p] = (
            GB[p, second, c].astype(F32) + RBS[p, second].astype(F32) + R1[p, 0].astype(F32)
        ).astype(BF)
        send(T2.at[p], R2.at[p], rs_s.at[p, 2], rs_r.at[p, 2], dev_2)

    def r3(p):
        got(R2.at[p], rs_r.at[p, 2])
        own = (
            GB[p, chip, c].astype(F32)
            + RBS[p, chip].astype(F32)
            + R1[p, 1].astype(F32)
            + R2[p].astype(F32)
        )
        if p in far:
            ZB[p] = own.astype(BF)
            send(ZB.at[p], RZ.at[p], rs_s.at[p, 3], rs_r.at[p, 3], dev_z[far[p]])
        elif p == 0:
            g_u[...] = own
        elif p == 1:
            g_d[...] = own
        else:
            g_a[...] = own

    def reduce(*steps):
        for step, p in steps:
            (r0, r1, r2, r3)[step](p)

    barrier = pltpu.get_barrier_semaphore()
    for dev in (dev_s, dev_x, dev_y, dev_z[1], dev_z[2], dev_z[3]):
        pl.semaphore_signal(barrier, inc=1, device_id=dev, device_id_type=MESH)

    src_row = iota((192, 768), 0)
    src_lane = iota((192, 768), 1)

    def place(at):
        return hot(src_lane == src_row + at)

    shard = dot(w_in[0].astype(BF), place(0)) + dot(w_in[2].astype(BF), place(192))
    shard = shard + dot(w_in[1].astype(BF), place(384)) + dot_tn(w_out[...].astype(BF), place(576))
    G[z, chip, c] = shard.astype(BF)
    G[4, chip, c] = w_up[...].astype(BF)
    G[5, chip, c] = w_dn[...].astype(BF)
    SMI[...] = jnp.zeros_like(SMI)
    SMI[0:HG, 0:529] = tab[...]
    bias_row = sum(dot(part, place(0)) for part in split_three(hb[0:1, :]))
    bias_row = bias_row + sum(dot(part, place(192)) for part in split_three(hb[1:2, :]))
    SMI[6:7, :] = bias_row
    SMI[7:8, :] = ub[...].reshape(1, FQ)
    pl.semaphore_wait(barrier, 6)

    for k in (1, 2, 3):
        send(SMI, SMG.at[z], ms.at[k], mr.at[k], dev_z[k])
    gather_step(0)
    SMG[z] = SMI[...]

    ET[...] = pad_hot_t()
    local(img_in, img, 0).wait()
    xp = dot(padded_rows(z), img[...])
    XC[...] = dot(ET[...], xp.astype(BF))
    normal, rs = norm_stats(xp)
    N1[...] = normal
    RS1[...] = rs
    LOW1[...] = (normal * nv[0:1, :] + nv[1:2, :]).astype(BF)
    keep = msk[0].astype(F32)
    local(cot_in, cot, 1).wait()
    GL[0] = (dot(compact_rows(z), cot[...]) * keep).astype(BF)
    GL[1] = (dot(compact_rows(zx[1]), cot[...]) * keep).astype(BF)
    BR[...] = jnp.zeros_like(BR)
    GONE[...] = jnp.zeros_like(GONE)
    DZ[...] = jnp.zeros_like(DZ)
    SMO[...] = jnp.zeros_like(SMO)
    gather_step(1)

    for k in (1, 2, 3):
        got(SMG.at[zx[k]], mr.at[k])
    table = SMG[:, :, 0:TABL].reshape(32, TABL)
    table_parts = jnp.concatenate(split_three(table), axis=0)

    def spread_step(ci, carry):
        parts = dot(table_parts, offset_hot(ci))
        parts = parts[0:32] + parts[32:64] + parts[64:96]
        for t in range(3):
            ZT[t, pl.ds(ci, 32, stride=ROWP), :] = parts[:, t * 128 : t * 128 + 128]
        return carry

    ZT[...] = jnp.zeros_like(ZT)
    lax.fori_loop(0, WIN, spread_step, 0)
    gather_step(2)

    qi = iota((WPAD, 1), 0)
    kj = iota((1, WPAD), 1)
    q_r, q_c = lax.shift_right_logical(qi, 4), jnp.bitwise_and(qi, ROWP - 1)
    k_r, k_c = lax.shift_right_logical(kj, 4), jnp.bitwise_and(kj, ROWP - 1)
    cut_r = ((q_r >= SHIFT) != (k_r >= SHIFT)) & (z // 2 == 1)
    cut_c = ((q_c >= SHIFT) != (k_c >= SHIFT)) & (z % 2 == 1)
    fill = jnp.where(cut_r | cut_c, FILL_VALUE, 0.0)
    fill = jnp.where(k_c < WIN, fill, -1e30)
    DS[0] = fill.astype(BF)
    z_high, z_low = split_two(jnp.concatenate([ZT[0], ZT[1], ZT[2]], axis=1))

    def bias_step(ri, carry):
        pick = hot(iota((ZL, WPAD), 0) == iota((ZL, WPAD), 1) + (WIN - 1 - ri) * ROWP)
        at = pl.ds(pl.multiple_of(ri * ROWP, ROWP), ROWP)
        block = (dot(z_high, pick) + dot(z_low, pick)).reshape(32, ROWP, WPAD)
        block = block + DS[0, at, :].astype(F32)[None]
        for zz in range(4):
            PB[zz * HG : zz * HG + HG, at, :] = block[zz * 8 : zz * 8 + HG]
        return carry

    lax.fori_loop(0, WIN, bias_step, 0)

    def zk(k):
        return (z // 2 + k // 2) % 2 * 2 + (z % 2 + k % 2) % 2

    def near_of(k):
        across = (1 - half) * k + half * (3 - k)
        beside = z + (1 - 2 * (z % 2)) * k
        far_half = k // 2
        return far_half * across + (1 - far_half) * beside

    def group_forward(zz):
        whole = G[zz].reshape(768, 768)
        qvk = (dot(LOW1[...], whole) + SMG[zz, 6:7, :]).astype(BF)
        QVK[zz] = qvk
        mixed = [None, None]
        for e in range(HG):
            ta, la, tb, lb = e // 4, 32 * (e % 4), (e + 2) // 4, 32 * ((e + 2) % 4)
            q_t = qvk[:, ta * 128 : ta * 128 + 128]
            k_t = qvk[:, 384 + ta * 128 : 512 + ta * 128]
            v_t = qvk[:, 128 + tb * 128 : 256 + tb * 128]
            s = dot_nt(mask_head(q_t, la), k_t) * SCALE + PB[zz * HG + e]
            p = jnp.exp(s - jnp.max(s, axis=-1, keepdims=True))
            p = p * (1.0 / jnp.sum(p, axis=-1, keepdims=True))
            PB[zz * HG + e] = p
            add = dot(p.astype(BF), mask_head(v_t, lb))
            mixed[tb] = add if mixed[tb] is None else mixed[tb] + add
        mixed = jnp.concatenate(mixed, axis=1).astype(BF)
        MX[zz] = mixed
        BR[...] += dot_nt(dot(ET[...], mixed).astype(BF), whole[:, 512:768])

    def forward_step(k, carry):
        for j in range(4):
            @pl.when(k == j)
            def _():
                gather_step(j + 3)
                s3(j)

        group_forward(near_of(k))
        return carry

    lax.fori_loop(0, 4, forward_step, 0)

    normal, rs = norm_stats(XC[...] + BR[...] + nv[4:5, :])
    N2H[...] = normal
    RS2[...] = rs
    N2[0] = (normal * nv[2:3, :] + nv[3:4, :]).astype(BF)
    send(N2.at[0], N2.at[1], es.at[0], er.at[0], dev_z[1])

    def ff_quarter(b, q):
        zq = (z // 2 + q) % 2 * 2 + z % 2

        def ff_step(n, carry):
            at = pl.ds(pl.multiple_of(n * 256, 256), 256)
            up = G[4 + 2 * q, :, :, :, at].reshape(768, 256)
            down = G[5 + 2 * q, :, :, :, at].reshape(768, 256)
            u = dot(N2[b], up) + SMG[zq, 7:8, at]
            u2 = u * u
            th = jnp.tanh(0.7978845608028654 * (u + 0.044715 * (u2 * u)))
            half = 0.5 * (1.0 + th)
            ACT[q, b, :, at] = (u * half).astype(BF)
            slope = half + 0.5 * u * (1.0 - th * th) * (
                0.7978845608028654 * (1.0 + 3 * 0.044715 * u2)
            )
            GH[q, b, :, at] = (dot(GL[b], down) * slope).astype(BF)
            return carry

        lax.fori_loop(0, 3, ff_step, 0)

    def ff_two(b):
        return dot_nt(GH[0, b], G[4].reshape(768, 768)) + dot_nt(GH[1, b], G[6].reshape(768, 768))

    def ff_out(b):
        return dot_nt(ACT[0, b], G[5].reshape(768, 768)) + dot_nt(ACT[1, b], G[7].reshape(768, 768))

    def ff_grad(p):
        q = p // 2
        left, right = (N2, GH) if p % 2 == 0 else (GL, ACT)

        def grad_step(j, carry):
            at = pl.ds(pl.multiple_of(j * 384, 384), 384)
            rows = left[:, :, at].reshape(2 * WTOK, 384)
            grad = dot_tn(rows, right[q].reshape(2 * WTOK, 768))
            GB[p, pl.ds(2 * j, 2)] = grad.astype(BF).reshape(2, 2, SHARD, 768)
            return carry

        lax.fori_loop(0, 2, grad_step, 0)

    gather_step(7)
    s3(4)
    s3(5)
    ff_quarter(0, 0)
    gather_step(8)
    got(N2.at[1], er.at[0])
    ff_quarter(1, 0)
    ff_grad(0)
    reduce((0, 0))
    ff_grad(1)
    gather_step(9)
    reduce((0, 1), (1, 0))
    s3(6)
    s3(7)
    ff_quarter(1, 1)
    G2S[...] = ff_two(1).astype(BF)
    send(G2S, G2R, es.at[1], er.at[1], dev_z[1])
    OS[...] = ff_out(1).astype(BF)
    send(OS, OR, es.at[2], er.at[2], dev_z[1])
    ff_quarter(0, 1)
    ff_grad(2)
    reduce((0, 2), (1, 1), (2, 0))
    ff_grad(3)
    reduce((0, 3), (1, 2))
    G2P[...] = ff_two(0)
    OUTP[...] = ff_out(0)

    for q in range(2):
        zq = (z // 2 + q) % 2 * 2 + z % 2
        SMO[zq, 8:9, :] = col_sum(GH[q].reshape(2 * WTOK, 768).astype(F32))

    got(G2R, er.at[1])
    g2 = G2P[...] + G2R[...].astype(F32)
    g_out = GL[0].astype(F32)
    gain2 = col_sum(g2 * N2H[...])
    shift2 = col_sum(g2)
    g_mid = g_out + norm_back(g2, nv[2:3, :], N2H[...], RS2[...])
    GMID[...] = g_mid
    g_branch = g_mid.astype(BF)
    GBP[...] = dot(pad_hot(), g_branch).astype(BF)
    bias_b = col_sum(g_branch.astype(F32))
    bias_o = col_sum(g_out)

    def group_backward(zz, p_at):
        whole = G[zz].reshape(768, 768)
        d_out = dot(GBP[...], whole[:, 512:768]).astype(BF)
        qvk = QVK[zz]
        dq, dk, dv = [None, None], [None, None], [None, None]

        def add(parts, t, v):
            parts[t] = v if parts[t] is None else parts[t] + v

        for e in range(HG):
            ta, la, tb, lb = e // 4, 32 * (e % 4), (e + 2) // 4, 32 * ((e + 2) % 4)
            q_t = qvk[:, ta * 128 : ta * 128 + 128]
            k_t = qvk[:, 384 + ta * 128 : 512 + ta * 128]
            v_t = qvk[:, 128 + tb * 128 : 256 + tb * 128]
            p = PB[zz * HG + e]
            d_o = mask_head(d_out[:, tb * 128 : tb * 128 + 128], lb)
            dp = dot_nt(d_o, v_t)
            add(dv, tb, dot_tn(p.astype(BF), d_o))
            ds = (p * (dp - jnp.sum(dp * p, axis=-1, keepdims=True))).astype(BF)
            DS[zz * HG + e] = ds
            add(dq, ta, dot(ds, mask_head(k_t, la)))
            add(dk, ta, dot_tn(ds, mask_head(q_t, la)))
        dq = [v * SCALE for v in dq]
        dk = [v * SCALE for v in dk]
        full = jnp.concatenate(
            [dq[0], dq[1] + dv[0], dv[1], dk[0], dk[1], jnp.zeros_like(dk[1])], axis=1
        ).astype(BF)
        GONE[...] += dot_nt(full[:, 0:640], whole[:, 0:640])
        SMO[zz, 6:7, :] = col_sum(full.astype(F32))
        FULL[...] = full

        def grad_step(j, carry):
            at = pl.ds(pl.multiple_of(j * 384, 384), 384)
            rows = LOW1[:, at]
            main = dot_tn(rows, FULL[:, 0:512])
            tail = dot_tn(rows, FULL[:, 512:768]) + dot_tn(GBP[:, at], MX[zz])
            grad = jnp.concatenate([main, tail], axis=1).astype(BF)
            GB[p_at, pl.ds(2 * j, 2)] = grad.reshape(2, 2, SHARD, 768)
            return carry

        lax.fori_loop(0, 2, grad_step, 0)

    def block_rows():
        got(OR, er.at[2])
        out = OUTP[...] + OR[...].astype(F32) + nv[5:6, :]
        BO[z] = (XC[...] + BR[...] + nv[4:5, :] + out).astype(BF)
        line_start(blocks_of(BO), 0)

    reduce((2, 1), (1, 3), (3, 0))

    def backward_step(i, carry):
        group_backward(zk(3 - i), 4 + i)
        for j in range(4):
            @pl.when(i == j)
            def _():
                if j == 0:
                    reduce((0, 4), (2, 2), (3, 1))
                    block_rows()
                else:
                    reduce((0, 4 + j), (1, 3 + j), (2, 2 + j), (3, 1 + j))
                    line_step(blocks_of(BO), 0, j)
        return carry

    lax.fori_loop(0, 4, backward_step, 0)

    g_one = GONE[...]
    gain1 = col_sum(g_one * N1[...])
    shift1 = col_sum(g_one)
    back = norm_back(g_one, nv[0:1, :], N1[...], RS1[...])
    b_high, b_low = split_two(back)
    back = dot(ET[...], b_high) + dot(ET[...], b_low)
    IG[z] = (GMID[...] + back).astype(BF)
    line_start(blocks_of(IG), 1)
    reduce((1, 7), (2, 6), (3, 5))
    local(BO, bo_out, 2).start()

    def table_step(ri, carry):
        at = pl.ds(pl.multiple_of(ri * ROWP, ROWP), ROWP)
        pick = hot(iota((WPAD, ZL), 1) == iota((WPAD, ZL), 0) + (WIN - 1 - ri) * ROWP)
        sums = dot(DS[:, at, :].reshape(4 * HG * ROWP, WPAD), pick)
        for t in range(3):
            DZ[t] += sums[:, t * 128 : t * 128 + 128]
        return carry

    lax.fori_loop(0, WIN, table_step, 0)
    line_step(blocks_of(IG), 1, 1)
    reduce((2, 7), (3, 6))

    def table_sum(ci, total):
        rows = jnp.concatenate([DZ[t, pl.ds(ci, 4 * HG, stride=ROWP), :] for t in range(3)], axis=1)
        high, low = split_two(rows)
        parts = dot_nt(jnp.concatenate([high, low], axis=0), offset_hot(ci))
        return total + parts[0:24] + parts[24:48]

    total = lax.fori_loop(0, WIN, table_sum, jnp.zeros((4 * HG, TABL), F32))
    for zz in range(4):
        SMO[zz, 0:HG, 0:TABL] = total[zz * HG : zz * HG + HG]
        for j, row in enumerate((gain1, shift1, gain2, shift2, bias_b, bias_o)):
            SMO[zz, 9 + j : 10 + j, :] = row
    for k in (1, 2, 3):
        send(SMO.at[zx[k]], SMR.at[k], qs.at[k], qr.at[k], dev_z[k])
    line_step(blocks_of(IG), 1, 2)
    reduce((3, 7))
    small = SMO[z]
    for k in (1, 2, 3):
        got(SMR.at[k], qr.at[k])
        small = small + SMR[k]
    for j, dev in enumerate((dev_s, dev_x, dev_y)):
        SMT[j] = small
        send(SMT.at[j], SMS.at[j], qs.at[4 + j], qr.at[4 + j], dev)
        got(SMS.at[j], qr.at[4 + j])
        small = small + SMS[j]
    sm_out[...] = small

    for p in far:
        got(RZ.at[p], rs_r.at[p, 3])
    g_u[...] += RZ[2].astype(F32)
    g_d[...] += RZ[3].astype(F32)
    g_a[...] += RZ[4].astype(F32) + RZ[5].astype(F32) + RZ[6].astype(F32)
    local(g_u, gu_out, 3).start()
    local(g_d, gd_out, 4).start()
    local(g_a, ga_out, 5).start()
    line_step(blocks_of(IG), 1, 3)
    local(IG, ig_out, 6).start()

    item = G.at[0, 0, 0]
    for k in (1, 2, 3):
        sent(SMI, ms.at[k])
        sent(SMO.at[0], qs.at[k])
        sent(SMO.at[0], qs.at[3 + k])
    sent(item, zs.at[6])
    sent(item, zs.at[7])
    sent(G2S, es.at[0])
    sent(G2S, es.at[1])
    sent(OS, es.at[2])
    line_drain(blocks_of(BO), 0)
    line_drain(blocks_of(IG), 1)
    line_drain(own_items, 2)
    for k in range(8):
        for j in range(7):
            sent(item, gs.at[k, j])
    for p in range(8):
        sent(RBS.at[p], rs_s.at[p, 0])
        sent(T1.at[p], rs_s.at[p, 1])
        sent(T2.at[p], rs_s.at[p, 2])
    for p in far:
        sent(ZB.at[p], rs_s.at[p, 3])
    for j, (src, dst) in enumerate(((BO, bo_out), (g_u, gu_out), (g_d, gd_out), (g_a, ga_out), (IG, ig_out))):
        local(src, dst, 2 + j).wait()


def vm(shape, dtype=F32):
    return pltpu.VMEM(shape, dtype)


def main_call(args):
    f32 = lambda *s: jax.ShapeDtypeStruct(s, F32)
    bf = lambda *s: jax.ShapeDtypeStruct(s, BF)
    dma = lambda *s: pltpu.SemaphoreType.DMA(s)
    vspec = pl.BlockSpec(memory_space=pltpu.VMEM)
    specs = [vspec] * len(args)
    specs[2] = pl.BlockSpec(memory_space=pltpu.SMEM)
    hbm = pl.BlockSpec(memory_space=pl.ANY)
    specs[0] = specs[1] = hbm
    scratch = [
        vm((8, 4, 2, SHARD, 768), BF),
        vm((8, 4, 2, SHARD, 768), BF),
        vm((8, 4, SHARD, 768), BF),
        vm((8, 2, SHARD, 768), BF),
        vm((8, 2, SHARD, 768), BF),
        vm((8, SHARD, 768), BF),
        vm((8, SHARD, 768), BF),
        vm((8, SHARD, 768), BF),
        vm((8, SHARD, 768), BF),
        vm((4 * HG, WPAD, WPAD)),
        vm((3, 32 * ROWP, 128)),
        vm((4, WPAD, 768), BF),
        vm((4, WPAD, 256), BF),
        vm((4 * HG, WPAD, WPAD), BF),
        vm((3, 4 * HG * ROWP, 128)),
        vm((WPAD, 768), BF),
        vm((WPAD, 768)),
        vm((WPAD, 1)),
        vm((WTOK, 768)),
        vm((WTOK, 768)),
        vm((WTOK, 768)),
        vm((WTOK, 1)),
        vm((2, WTOK, 768), BF),
        vm((2, WTOK, 768), BF),
        vm((2, 2, WTOK, FQ), BF),
        vm((2, 2, WTOK, FQ), BF),
        vm((WTOK, 768)),
        vm((WTOK, 768), BF),
        vm((WTOK, 768), BF),
        vm((WTOK, 768)),
        vm((WTOK, 768), BF),
        vm((WTOK, 768), BF),
        vm((WTOK, 768)),
        vm((WPAD, 768), BF),
        vm((WTOK, WPAD), BF),
        vm((WPAD, 768)),
        vm((4, WTOK, 768), BF),
        vm((4, WTOK, 768), BF),
        vm((8, 768)),
        vm((4, 8, 768)),
        vm((4, 16, 768)),
        vm((4, 16, 768)),
        vm((3, 16, 768)),
        vm((3, 16, 768)),
        vm((WPAD, 768), BF),
        vm((TOK, 768), BF),
        vm((TOK, 768), BF),
        vm((SHARD, 768)),
        vm((SHARD, 768)),
        vm((SHARD, 768)),
        dma(8, 7), dma(8, 7),
        dma(8), dma(8),
        dma(4), dma(4),
        dma(3), dma(3),
        dma(8, 4), dma(8, 4),
        dma(3, 4, 2), dma(3, 4),
        dma(8), dma(8),
        dma(12),
    ]
    return pl.pallas_call(
        main_kernel,
        out_shape=(
            f32(SHARD, 768), f32(SHARD, 768), f32(SHARD, 768), f32(16, 768),
            bf(4, WTOK, 768), bf(4, WTOK, 768),
        ),
        in_specs=specs,
        out_specs=tuple([hbm] * 3 + [vspec] + [hbm] * 2),
        scratch_shapes=scratch,
        compiler_params=pltpu.CompilerParams(
            collective_id=0, has_side_effects=True, vmem_limit_bytes=62 * 2**20
        ),
        cost_estimate=pl.CostEstimate(flops=7 * 10**9, bytes_accessed=10**7, transcendentals=10**6),
    )(*args)


def last_kernel(n_in, n_out, *refs):
    given, made = refs[:n_in], refs[n_in : n_in + n_out]
    held = refs[n_in + n_out : 2 * n_in + n_out]
    done = refs[2 * n_in + n_out : 2 * (n_in + n_out)]
    in_sem, out_sem = refs[2 * (n_in + n_out) :]
    g_a, g_u, g_d, sm, bo, ig = range(6)

    def load(j):
        return pltpu.make_async_copy(given[j], held[j], in_sem.at[j])

    def store(j):
        return pltpu.make_async_copy(done[j], made[j], out_sem.at[j])

    order = [ig, bo, g_u, 12, 13, 14, g_d, 15, 16, 17, g_a, 6, 7, 8, 9, 10, 11, sm] + list(range(18, 30))
    for j in order:
        load(j).start()

    def wait(*js):
        for j in js:
            load(j).wait()

    token = iota((TOK, 1), 0)
    row = lax.shift_right_logical(token * 2731, 16)
    col = token - row * SIDE
    row = jnp.where(row >= SHIFT, row - SHIFT, row + SIDE - SHIFT)
    col = jnp.where(col >= SHIFT, col - SHIFT, col + SIDE - SHIFT)
    wr, wc = (row >= WIN).astype(jnp.int32), (col >= WIN).astype(jnp.int32)
    at = (wr * 2 + wc) * WTOK + (row - WIN * wr) * WIN + col - WIN * wc
    back = hot(at == iota((TOK, TOK), 1))
    wait(ig)
    done[1][0] = dot(back, held[ig][...].reshape(TOK, 768))
    store(1).start()
    wait(bo)
    done[0][0] = dot(back, held[bo][...].reshape(TOK, 768)).astype(BF)
    store(0).start()

    def adam(param, out, at, grad, low, vector=False):
        w, f, s = (held[param + j][at] for j in range(3))
        rate, decay = (RATE_VECTOR, 0.0) if vector else (RATE_MATRIX, DECAY_MATRIX)
        moment, square, updated = adam_update(w, f, s, grad, rate, decay)
        done[out][at], done[out + 1][at], done[out + 2][at] = moment, square, updated
        if low:
            done[out + 3][at] = updated.astype(BF)

    def finish(out, count):
        for j in range(out, out + count):
            store(j).start()

    whole = slice(None)
    wait(g_u, 12, 13, 14)
    adam(12, 10, whole, held[g_u][...], True)
    finish(10, 4)
    wait(g_d, 15, 16, 17)
    adam(15, 14, whole, held[g_d][...], True)
    finish(14, 4)
    wait(g_a, 6, 7, 8)
    for j, lane in ((0, 0), (1, 384), (2, 192)):
        adam(6, 2, j, held[g_a][:, lane : lane + 192], True)
    finish(2, 4)
    eye = jnp.where(iota((SHARD, SHARD), 0) == iota((SHARD, SHARD), 1), 1.0, 0.0)
    turned = lax.dot_general(
        held[g_a][:, 576:768], eye, (((0,), (0,)), ((), ())),
        precision=lax.Precision.HIGHEST, preferred_element_type=F32,
    )
    wait(9, 10, 11)
    adam(9, 6, whole, turned, True)
    finish(6, 4)
    small = held[sm]
    wait(sm, *range(18, 30))
    adam(18, 18, whole, small[9:15, :], False, True)
    for j in (0, 1):
        adam(21, 21, slice(j, j + 1), small[6:7, 192 * j : 192 * j + 192], False, True)
    adam(24, 24, whole, small[8:9, :].reshape(FQ), False, True)
    adam(27, 27, whole, small[0:HG, 0:529], False, True)
    finish(18, 12)
    for j in range(n_out):
        store(j).wait()


def last_call(sums, params):
    hbm = pl.BlockSpec(memory_space=pl.ANY)
    like = lambda a, t=F32: jax.ShapeDtypeStruct(a.shape, t)
    outs = [jax.ShapeDtypeStruct((1, TOK, 768), BF), jax.ShapeDtypeStruct((1, TOK, 768), F32)]
    for j in range(0, 12, 3):
        outs += [like(params[j])] * 3 + [like(params[j], BF)]
    for j in range(12, 24, 3):
        outs += [like(params[j])] * 3
    ins = list(sums) + list(params)
    return pl.pallas_call(
        functools.partial(last_kernel, len(ins), len(outs)),
        out_shape=tuple(outs),
        in_specs=[hbm] * len(ins),
        out_specs=tuple([hbm] * len(outs)),
        scratch_shapes=[vm(a.shape, a.dtype) for a in ins + outs]
        + [pltpu.SemaphoreType.DMA((len(ins),)), pltpu.SemaphoreType.DMA((len(outs),))],
        compiler_params=pltpu.CompilerParams(vmem_limit_bytes=62 * 2**20),
        cost_estimate=pl.CostEstimate(flops=10**9, bytes_accessed=15 * 10**6, transcendentals=10**6),
    )(*ins)


def on_device_windows(images, cotangent, image_mask, *params):
    params = list(params)
    turned = (9, 10, 11, 21, 22, 23)
    for j in turned:
        params[j] = params[j].T
    (in_w, _, _, out_w, _, _, up_w, _, _, dn_w, _, _, nv, _, _, hb, _, _, ub, _, _, tab, _, _) = params
    sums = main_call(
        (
            images.reshape(TOK, D), cotangent.reshape(TOK, D), image_mask,
            in_w, out_w, up_w, dn_w, nv, hb, ub, tab,
        )
    )
    outs = list(last_call(sums, params))
    for j in (14, 15, 16, 17, 27, 28, 29):
        outs[j] = outs[j].T
    return tuple(outs)


def solution(mesh):
    shape = mesh.shape
    windows = shape["dp"] == 8 and shape["tensor"] == 4
    return jax.shard_map(
        on_device_windows if windows else on_device,
        mesh=mesh,
        in_specs=(
            P("dp", None, None),
            P("dp", None, None),
            P("dp"),
            P(None, "dp", "tensor"),
            P(None, "dp", "tensor"),
            P(None, "dp", "tensor"),
            P("tensor", "dp"),
            P("tensor", "dp"),
            P("tensor", "dp"),
            P("dp", "tensor"),
            P("dp", "tensor"),
            P("dp", "tensor"),
            P("tensor", "dp"),
            P("tensor", "dp"),
            P("tensor", "dp"),
            P(),
            P(),
            P(),
            P(None, "tensor"),
            P(None, "tensor"),
            P(None, "tensor"),
            P("tensor"),
            P("tensor"),
            P("tensor"),
            P(None, "tensor"),
            P(None, "tensor"),
            P(None, "tensor"),
        ),
        out_specs=(
            P("dp", None, None),
            P("dp", None, None),
            P(None, "dp", "tensor"),
            P(None, "dp", "tensor"),
            P(None, "dp", "tensor"),
            P(None, "dp", "tensor"),
            P("tensor", "dp"),
            P("tensor", "dp"),
            P("tensor", "dp"),
            P("tensor", "dp"),
            P("dp", "tensor"),
            P("dp", "tensor"),
            P("dp", "tensor"),
            P("dp", "tensor"),
            P("tensor", "dp"),
            P("tensor", "dp"),
            P("tensor", "dp"),
            P("tensor", "dp"),
            P(),
            P(),
            P(),
            P(None, "tensor"),
            P(None, "tensor"),
            P(None, "tensor"),
            P("tensor"),
            P("tensor"),
            P("tensor"),
            P(None, "tensor"),
            P(None, "tensor"),
            P(None, "tensor"),
        ),
        check_vma=False,
    )
```

```python
import functools
from functools import partial

import jax
import jax.numpy as jnp
from jax import lax
from jax.experimental import pallas as pl
from jax.experimental.pallas import tpu as pltpu
from jax.sharding import PartitionSpec as P

D = 768
HEAD_DIM = 32
WIN = 12
SIDE = 24
STEP = 7
SHIFT = 6


NORM_EPS = 1e-05
FILL_VALUE = -100.0
BETA_ONE = 0.5
BETA_TWO = 0.5
ADAM_EPS = 1e-08
RATE_MATRIX = 0.05
RATE_VECTOR = 0.3
DECAY_MATRIX = 0.05


def layer_norm(values, gain_in, offset_in):
    center = values - jnp.mean(values, axis=-1, keepdims=True)
    spread = jnp.mean(center * center, axis=-1, keepdims=True)
    return center * lax.rsqrt(spread + NORM_EPS) * gain_in + offset_in


def adam_update(weight, first_old, second_old, gradient, rate_of, decay_of):
    moment = BETA_ONE * first_old + (1.0 - BETA_ONE) * gradient
    square = BETA_TWO * second_old + (1.0 - BETA_TWO) * gradient * gradient
    moment_fix = moment / (1.0 - BETA_ONE**STEP)
    square_fix = square / (1.0 - BETA_TWO**STEP)
    updated = weight * (1.0 - rate_of * decay_of) - rate_of * moment_fix / (
        jnp.sqrt(square_fix) + ADAM_EPS
    )
    return (moment, square, updated)


def dot_plain(left_side, right_side):
    return jnp.dot(left_side, right_side, preferred_element_type=jnp.float32)


def dot_back(left_side, right_side):
    return lax.dot_general(
        left_side, right_side, (((1,), (1,)), ((), ())), preferred_element_type=jnp.float32
    )


def dot_rows(left_side, right_side):
    return lax.dot_general(
        left_side, right_side, (((0,), (0,)), ((), ())), preferred_element_type=jnp.float32
    )


def to_heads(token_rows, images_here, heads_here):
    blocks = SIDE // WIN
    grid_view = token_rows.reshape(images_here, SIDE, SIDE, heads_here * HEAD_DIM)
    grid_view = jnp.roll(grid_view, (-SHIFT, -SHIFT), (1, 2))
    grid_view = grid_view.reshape(
        images_here, blocks, WIN, blocks, WIN, heads_here, HEAD_DIM
    ).transpose(0, 1, 3, 2, 4, 5, 6)
    return grid_view.reshape(images_here, blocks * blocks, WIN * WIN, heads_here, HEAD_DIM)


def from_heads(windows, images_here):
    blocks = SIDE // WIN
    channels = windows.shape[3] * windows.shape[4]
    grid_view = windows.reshape(images_here, blocks, blocks, WIN, WIN, channels).transpose(
        0, 1, 3, 2, 4, 5
    )
    grid_view = jnp.roll(
        grid_view.reshape(images_here, SIDE, SIDE, channels), (SHIFT, SHIFT), (1, 2)
    )
    return grid_view.reshape(images_here * SIDE * SIDE, channels)


def window_fill():
    blocks = SIDE // WIN
    cell_ids = jnp.arange(SIDE, dtype=jnp.int32)
    band_of = (cell_ids >= SIDE - WIN).astype(jnp.int32) + (cell_ids >= SIDE - SHIFT).astype(
        jnp.int32
    )
    region = band_of[:, None] * 3 + band_of[None, :]
    labels = (
        region.reshape(blocks, WIN, blocks, WIN)
        .transpose(0, 2, 1, 3)
        .reshape(blocks * blocks, WIN * WIN)
    )
    return jnp.where(labels[:, :, None] != labels[:, None, :], FILL_VALUE, 0.0).astype(jnp.float32)


def offset_onehot():
    places = jnp.arange(WIN, dtype=jnp.int32)
    spans = jnp.arange(2 * WIN - 1, dtype=jnp.int32)
    return (places[:, None, None] - places[None, :, None] + WIN - 1 == spans[None, None, :]).astype(
        jnp.float32
    )


def window_scores(query_win, key_win, bias_add, fill_add):
    scores = jnp.einsum(
        "inqhd,inkhd->inhqk", query_win, key_win, preferred_element_type=jnp.float32
    ) * HEAD_DIM ** (-0.5)
    return scores + bias_add[None, None] + fill_add[None, :, None]


def on_device(
    images,
    cotangent,
    image_mask,
    in_weight,
    in_first,
    in_second,
    out_weight,
    out_first,
    out_second,
    up_weight,
    up_first,
    up_second,
    down_weight,
    down_first,
    down_second,
    norm_vector,
    norm_first,
    norm_second,
    head_bias,
    head_first,
    head_second,
    up_bias,
    bias_first,
    bias_second,
    position_table,
    table_first,
    table_second,
):
    lowtype = jnp.bfloat16
    highest = lax.Precision.HIGHEST
    whole_in, whole_out, whole_up, whole_down = (
        lax.all_gather(in_weight.astype(lowtype), "dp", axis=1, tiled=True),
        lax.all_gather(out_weight.astype(lowtype), "dp", axis=1, tiled=True),
        lax.all_gather(up_weight.astype(lowtype), "dp", axis=0, tiled=True),
        lax.all_gather(down_weight.astype(lowtype), "dp", axis=1, tiled=True),
    )
    images_here = images.shape[0]
    heads_here = whole_in.shape[2] // HEAD_DIM
    span_count = 2 * WIN - 1
    token_rows = images.reshape(-1, D).astype(jnp.float32)
    normed_one, norm_one_back = jax.vjp(layer_norm, token_rows, norm_vector[0], norm_vector[1])
    low_one = normed_one.astype(lowtype)
    query_rows = (dot_plain(low_one, whole_in[0]) + head_bias[0]).astype(lowtype)
    key_rows = dot_plain(low_one, whole_in[1]).astype(lowtype)
    value_rows = (dot_plain(low_one, whole_in[2]) + head_bias[1]).astype(lowtype)
    query_win = to_heads(query_rows, images_here, heads_here)
    key_win = to_heads(key_rows, images_here, heads_here)
    value_win = to_heads(value_rows, images_here, heads_here)
    onehot = offset_onehot()
    table_view = position_table.reshape(span_count, span_count, heads_here)
    bias_add = jnp.einsum(
        "xya,zwb,abh->hxzyw", onehot, onehot, table_view, precision=highest
    ).reshape(heads_here, WIN * WIN, WIN * WIN)
    fill_add = window_fill()
    scores = window_scores(query_win, key_win, bias_add, fill_add)
    row_top = jnp.max(scores, axis=-1, keepdims=True)
    weights_raw = jnp.exp(scores - row_top)
    row_total = jnp.sum(weights_raw, axis=-1, keepdims=True)
    log_total = row_top + jnp.log(row_total)
    prob_low = (weights_raw / row_total).astype(lowtype)
    mixed_win = jnp.einsum(
        "inhqk,inkhd->inqhd", prob_low, value_win, preferred_element_type=jnp.float32
    ).astype(lowtype)
    mixed_rows = from_heads(mixed_win, images_here)
    branch_share = lax.psum_scatter(
        dot_plain(mixed_rows, whole_out), "tensor", scatter_dimension=0, tiled=True
    )
    branch = lax.all_gather(branch_share, "tensor", axis=0, tiled=True) + norm_vector[4]
    middle = token_rows + branch
    normed_two, norm_two_back = jax.vjp(layer_norm, middle, norm_vector[2], norm_vector[3])
    low_two = normed_two.astype(lowtype)
    hidden = dot_plain(low_two, whole_up) + up_bias
    active, gelu_back = jax.vjp(partial(jax.nn.gelu, approximate=True), hidden)
    active_low = active.astype(lowtype)
    output_share = lax.psum_scatter(
        dot_plain(active_low, whole_down).astype(jnp.bfloat16),
        "tensor",
        scatter_dimension=0,
        tiled=True,
    ).astype(jnp.float32)
    output = (
        lax.all_gather(output_share.astype(jnp.bfloat16), "tensor", axis=0, tiled=True).astype(
            output_share.dtype
        )
        + norm_vector[5]
    )
    block_out = (middle + output).astype(lowtype).reshape(images.shape)
    keep_rows = jnp.repeat(image_mask.astype(jnp.float32), SIDE * SIDE)[:, None]
    grad_out = cotangent.reshape(-1, D).astype(jnp.float32) * keep_rows
    grad_low = grad_out.astype(lowtype)
    down_grad = dot_rows(active_low, grad_low)
    grad_hidden = gelu_back(dot_back(grad_low, whole_down))[0].astype(lowtype)
    up_grad = dot_rows(low_two, grad_hidden)
    bias_grad = jnp.sum(grad_hidden.astype(jnp.float32), axis=0)
    two_share = lax.psum_scatter(
        dot_back(grad_hidden, whole_up), "tensor", scatter_dimension=0, tiled=True
    )
    grad_two = lax.all_gather(two_share, "tensor", axis=0, tiled=True)
    grad_norm_two, gain_two, offset_two = norm_two_back(grad_two)
    grad_middle = grad_out + grad_norm_two
    grad_branch = grad_middle.astype(lowtype)
    out_grad = dot_rows(mixed_rows, grad_branch)
    grad_mixed = dot_back(grad_branch, whole_out).astype(lowtype)
    grad_win = to_heads(grad_mixed, images_here, heads_here)
    scores_again = window_scores(query_win, key_win, bias_add, fill_add)
    probs = jnp.exp(scores_again - log_total)
    grad_probs = jnp.einsum(
        "inqhd,inkhd->inhqk", grad_win, value_win, preferred_element_type=jnp.float32
    )
    grad_value = jnp.einsum(
        "inhqk,inqhd->inkhd", probs.astype(lowtype), grad_win, preferred_element_type=jnp.float32
    ).astype(lowtype)
    grad_scores = (
        probs * (grad_probs - jnp.sum(grad_probs * probs, axis=-1, keepdims=True))
    ).astype(lowtype)
    grad_query = (
        jnp.einsum("inhqk,inkhd->inqhd", grad_scores, key_win, preferred_element_type=jnp.float32)
        * HEAD_DIM ** (-0.5)
    ).astype(lowtype)
    grad_key = (
        jnp.einsum("inhqk,inqhd->inkhd", grad_scores, query_win, preferred_element_type=jnp.float32)
        * HEAD_DIM ** (-0.5)
    ).astype(lowtype)
    score_sums = jnp.sum(grad_scores.astype(jnp.float32), axis=(0, 1)).reshape(
        heads_here, WIN, WIN, WIN, WIN
    )
    table_grad = jnp.einsum(
        "xya,zwb,hxzyw->abh", onehot, onehot, score_sums, precision=highest
    ).reshape(span_count * span_count, heads_here)
    query_back = from_heads(grad_query, images_here)
    key_back = from_heads(grad_key, images_here)
    value_back = from_heads(grad_value, images_here)
    in_grad = jnp.stack(
        [dot_rows(low_one, query_back), dot_rows(low_one, key_back), dot_rows(low_one, value_back)]
    )
    head_grad = jnp.stack(
        [
            jnp.sum(query_back.astype(jnp.float32), axis=0),
            jnp.sum(value_back.astype(jnp.float32), axis=0),
        ]
    )
    grad_one_terms = (
        dot_back(query_back, whole_in[0])
        + dot_back(key_back, whole_in[1])
        + dot_back(value_back, whole_in[2])
    )
    one_share = lax.psum_scatter(
        grad_one_terms.astype(jnp.bfloat16), "tensor", scatter_dimension=0, tiled=True
    ).astype(jnp.float32)
    grad_one = lax.all_gather(one_share.astype(jnp.bfloat16), "tensor", axis=0, tiled=True).astype(
        one_share.dtype
    )
    grad_norm_one, gain_one, offset_one = norm_one_back(grad_one)
    image_grad = (grad_middle + grad_norm_one).reshape(images.shape)
    norm_grad = jnp.stack(
        [
            gain_one,
            offset_one,
            gain_two,
            offset_two,
            jnp.sum(grad_branch.astype(jnp.float32), axis=0),
            jnp.sum(grad_low.astype(jnp.float32), axis=0),
        ]
    )
    summed = lax.psum(
        (in_grad, out_grad, up_grad, down_grad, norm_grad, head_grad, bias_grad, table_grad), "dp"
    )
    position = lax.axis_index("dp")
    in_total = lax.dynamic_slice_in_dim(
        summed[0], position * in_weight.shape[1], in_weight.shape[1], 1
    )
    out_total = lax.dynamic_slice_in_dim(
        summed[1], position * out_weight.shape[1], out_weight.shape[1], 1
    )
    up_total = lax.dynamic_slice_in_dim(
        summed[2], position * up_weight.shape[0], up_weight.shape[0], 0
    )
    down_total = lax.dynamic_slice_in_dim(
        summed[3], position * down_weight.shape[1], down_weight.shape[1], 1
    )
    norm_total, head_total, bias_total, table_total = (summed[4], summed[5], summed[6], summed[7])
    in_moment, in_square, in_updated = adam_update(
        in_weight, in_first, in_second, in_total, RATE_MATRIX, DECAY_MATRIX
    )
    out_moment, out_square, out_updated = adam_update(
        out_weight, out_first, out_second, out_total, RATE_MATRIX, DECAY_MATRIX
    )
    up_moment, up_square, up_updated = adam_update(
        up_weight, up_first, up_second, up_total, RATE_MATRIX, DECAY_MATRIX
    )
    down_moment, down_square, down_updated = adam_update(
        down_weight, down_first, down_second, down_total, RATE_MATRIX, DECAY_MATRIX
    )
    norm_moment, norm_square, norm_updated = adam_update(
        norm_vector, norm_first, norm_second, norm_total, RATE_VECTOR, 0.0
    )
    head_moment, head_square, head_updated = adam_update(
        head_bias, head_first, head_second, head_total, RATE_VECTOR, 0.0
    )
    bias_moment, bias_square, bias_updated = adam_update(
        up_bias, bias_first, bias_second, bias_total, RATE_VECTOR, 0.0
    )
    table_moment, table_square, table_updated = adam_update(
        position_table, table_first, table_second, table_total, RATE_VECTOR, 0.0
    )
    return (
        block_out,
        image_grad,
        in_moment,
        in_square,
        in_updated,
        in_updated.astype(lowtype),
        out_moment,
        out_square,
        out_updated,
        out_updated.astype(lowtype),
        up_moment,
        up_square,
        up_updated,
        up_updated.astype(lowtype),
        down_moment,
        down_square,
        down_updated,
        down_updated.astype(lowtype),
        norm_moment,
        norm_square,
        norm_updated,
        head_moment,
        head_square,
        head_updated,
        bias_moment,
        bias_square,
        bias_updated,
        table_moment,
        table_square,
        table_updated,
    )


MESH = pl.DeviceIdType.MESH
TOK = SIDE * SIDE
WTOK = WIN * WIN
ROWP = 16
WPAD = WIN * ROWP
FQ = 768
SHARD = 96
HG = 6
TABL = 640
TABS = 768
ZL = 384
SCALE = HEAD_DIM ** (-0.5)
F32 = jnp.float32
BF = jnp.bfloat16


def dot(a, b):
    return lax.dot_general(a, b, (((1,), (0,)), ((), ())), preferred_element_type=F32)


def dot_nt(a, b):
    return lax.dot_general(a, b, (((1,), (1,)), ((), ())), preferred_element_type=F32)


def dot_tn(a, b):
    return lax.dot_general(a, b, (((0,), (0,)), ((), ())), preferred_element_type=F32)


def iota(shape, axis):
    return lax.broadcasted_iota(jnp.int32, shape, axis)


def div12(i):
    return lax.shift_right_logical(i * 171, 11)


def hot(condition):
    return jnp.where(condition, 1.0, 0.0).astype(BF)


def split_two(v):
    high = v.astype(BF)
    return high, (v - high.astype(F32)).astype(BF)


def split_three(v):
    high, _ = split_two(v)
    rest = v - high.astype(F32)
    mid, low = split_two(rest)
    return high, mid, low


def token_of(row, col, win):
    r = row + WIN * (win // 2) + SHIFT
    c = col + WIN * (win % 2) + SHIFT
    r = jnp.where(r >= SIDE, r - SIDE, r)
    c = jnp.where(c >= SIDE, c - SIDE, c)
    return r * SIDE + c


def padded_rows(win):
    i = iota((WPAD, 1), 0)
    col = jnp.bitwise_and(i, ROWP - 1)
    token = token_of(lax.shift_right_logical(i, 4), col, win)
    token = jnp.where(col < WIN, token, -1)
    return hot(token == iota((WPAD, TOK), 1))


def window_rows():
    i = iota((TOK, 1), 0)
    win = sum((i >= j * WTOK).astype(jnp.int32) for j in (1, 2, 3))
    place = i - WTOK * win
    row = div12(place)
    down, across = (win >= 2).astype(jnp.int32), win - 2 * (win >= 2).astype(jnp.int32)
    r = row + WIN * down + SHIFT
    c = place - WIN * row + WIN * across + SHIFT
    r = jnp.where(r >= SIDE, r - SIDE, r)
    c = jnp.where(c >= SIDE, c - SIDE, c)
    return hot(r * SIDE + c == iota((TOK, TOK), 1))


def pad_hot():
    j = iota((WPAD, WTOK), 1)
    return hot(iota((WPAD, WTOK), 0) == j + 4 * div12(j))


def pad_hot_t():
    j = iota((WTOK, WPAD), 0)
    return hot(iota((WTOK, WPAD), 1) == j + 4 * div12(j))


def stride_hot():
    lane = iota((1, TABS), 1)
    row, col = lax.shift_right_logical(lane, 5), jnp.bitwise_and(lane, 31)
    entry = jnp.where((col < 23) & (row < 23), row * 23 + col, -1)
    return hot(iota((TABL, TABS), 0) == entry)


def offset_hot():
    lane = iota((1, ZL), 1)
    cj = jnp.bitwise_and(lane, ROWP - 1)
    u = lax.shift_right_logical(lane, 4)
    entry = jnp.where((cj < WIN) & (u < 23), (22 - u) * 32 + 11 - cj, -1)
    return hot(iota((TABS, ZL), 0) == entry)


def mask_head(tile, lane0):
    lane = iota((1, 128), 1)
    return jnp.where((lane >= lane0) & (lane < lane0 + HEAD_DIM), tile, jnp.zeros_like(tile))


def norm_stats(values):
    center = values - jnp.mean(values, axis=-1, keepdims=True)
    spread = jnp.mean(center * center, axis=-1, keepdims=True)
    rs = lax.rsqrt(spread + NORM_EPS)
    return center * rs, rs


def norm_back(grad, gain, normal, rs):
    e = grad * gain
    return rs * (
        e
        - jnp.mean(e, axis=-1, keepdims=True)
        - normal * jnp.mean(e * normal, axis=-1, keepdims=True)
    )


def col_sum(v):
    return jnp.sum(v, axis=0, keepdims=True)


def main_kernel(
    img_in, cot_in, msk, wi_in, wo_in, wu_in, wd_in, nv_in, hb_in, ub_in, tab_in,
    ga_out, gu_out, gd_out, sm_out, bo_out, ig_out,
    G, GB, RBS, T1, R1, T2, R2, ZB, RZ,
    PB, ZT, QVK, MX, DS, DZ, LOW1, N1, RS1, XC, BR, N2H, RS2, N2, GL, ACT, GH, ACT1, GH1,
    G2P, G2S, G2R, OS, OR, GMID, GBP, ET, GONE, BO, IG,
    SMI, SMG, SMO, SMR, SMT, SMS, FULL, LOW1T, GBPT, img, cot, w_in, w_out, w_up, w_dn, nv, hb, ub, tab, g_a, g_u, g_d,
    gs, gr, zs, zr, ms, mr, es, er, rs_s, rs_r, os_s, os_r, qs, qr, ls,
):
    def local(src, dst, j):
        return pltpu.make_async_copy(src, dst, ls.at[j])

    given = (
        (wi_in, w_in), (wo_in, w_out), (hb_in, hb), (ub_in, ub), (tab_in, tab), (img_in, img),
        (nv_in, nv), (wu_in, w_up), (wd_in, w_dn), (cot_in, cot),
    )
    for j, (src, dst) in enumerate(given):
        local(src, dst, j).start()

    def ready(*js):
        for j in js:
            local(*given[j], j).wait()
    d = lax.axis_index("dp")
    z = lax.axis_index("tensor")
    chip = d // 2
    c = d % 2
    chip_x = chip + 1 - 2 * (chip % 2)
    chip_y = (chip + 2) % 4
    chip_d = 3 - chip
    first = (1 - c) * chip_y + c * chip_x
    second = (1 - c) * chip_x + c * chip_y
    zx = [z, z + 1 - 2 * (z % 2), (z + 2) % 4, 3 - z]
    half = z // 2
    near = [z, zx[1], 2 - half, 3 - 3 * half]
    dev_s = (chip * 2 + 1 - c, z)
    dev_x = (chip_x * 2 + c, z)
    dev_y = (chip_y * 2 + c, z)
    dev_d = (chip_d * 2 + c, z)
    dev_1 = (first * 2 + c, z)
    dev_2 = (second * 2 + c, z)
    dev_z = [None] + [(d, zx[k]) for k in (1, 2, 3)]

    def copy(src, dst, ssem, rsem, dev):
        return pltpu.make_async_remote_copy(
            src_ref=src, dst_ref=dst, send_sem=ssem, recv_sem=rsem, device_id=dev, device_id_type=MESH
        )

    def send(src, dst, ssem, rsem, dev):
        copy(src, dst, ssem, rsem, dev).start()

    def got(dst, rsem):
        copy(dst, dst, rsem, rsem, dev_s).wait_recv()

    def sent(src, ssem):
        copy(src, src, ssem, ssem, dev_s).wait_send()

    def blocks_of(ref):
        return lambda block: ref.at[block]

    def own_items(block):
        return G.at[block, chip, c]

    dev_up = (d, (z + 1) % 4)
    dev_dn = (d, (z + 3) % 4)

    def line_send(buf, which, j, block, live_up, live_dn):
        def go(ok, side, dev):
            @pl.when(ok)
            def _():
                send(buf(block), buf(block), os_s.at[which, j, side], os_r.at[which, block], dev)

        go(live_up, 0, dev_up)
        go(live_dn, 1, dev_dn)

    def line_start(buf, which):
        line_send(buf, which, 0, z, z < 3, z > 0)

    def line_step(buf, which, j):
        below, above = (z + 4 - j) % 4, (z + j) % 4

        @pl.when(z >= j)
        def _():
            got(buf(below), os_r.at[which, below])

            @pl.when(z < 3)
            def _():
                send(buf(below), buf(below), os_s.at[which, j, 0], os_r.at[which, below], dev_up)

        @pl.when(z + j <= 3)
        def _():
            got(buf(above), os_r.at[which, above])

            @pl.when(z > 0)
            def _():
                send(buf(above), buf(above), os_s.at[which, j, 1], os_r.at[which, above], dev_dn)

    def line_drain(buf, which):
        for j in range(4):
            @pl.when((z >= j) & (z < 3))
            def _():
                sent(buf(0), os_s.at[which, j, 0])

            @pl.when((z + j <= 3) & (z > 0))
            def _():
                sent(buf(0), os_s.at[which, j, 1])

    def slot(k):
        return near[k] if k < 4 else k

    def s0(k):
        s = slot(k)
        if k in (6, 7):
            got(G.at[s, chip, c], zr.at[k])
        item = G.at[s, chip, c]
        send(item, item, gs.at[k, 0], gr.at[k, 0], dev_x)
        send(item, item, gs.at[k, 1], gr.at[k, 1], dev_y)
        send(item, item, gs.at[k, 3], gr.at[k, 3], dev_s)

    def s1(k):
        s = slot(k)
        got(G.at[s, chip_x, c], gr.at[k, 0])
        got(G.at[s, chip_y, c], gr.at[k, 1])
        item = G.at[s, second, c]
        send(item, item, gs.at[k, 2], gr.at[k, 2], dev_1)
        item = G.at[s, chip_x, c]
        send(item, item, gs.at[k, 4], gr.at[k, 4], dev_s)
        item = G.at[s, chip_y, c]
        send(item, item, gs.at[k, 5], gr.at[k, 5], dev_s)

    def s2(k):
        s = slot(k)
        got(G.at[s, chip_d, c], gr.at[k, 2])
        item = G.at[s, chip_d, c]
        send(item, item, gs.at[k, 6], gr.at[k, 6], dev_s)

    def s3(k):
        s = slot(k)
        for j, from_chip in ((3, chip), (4, chip_x), (5, chip_y), (6, chip_d)):
            got(G.at[s, from_chip, 1 - c], gr.at[k, j])

    def gather_step(t):
        if t == 0:
            line_start(own_items, 2)
        if 1 <= t <= 3:
            line_step(own_items, 2, t)
        if t in (3, 4):
            k = t + 3
            send(G.at[k - 2, chip, c], G.at[k, chip, c], zs.at[k], zr.at[k], dev_z[2])
        if t <= 7:
            s0(t)
        if 1 <= t <= 8:
            s1(t - 1)
        if 2 <= t <= 9:
            s2(t - 2)

    far = {2: 1, 3: 2, 4: 1}

    def r0(p):
        send(GB.at[p, :, 1 - c], RBS.at[p], rs_s.at[p, 0], rs_r.at[p, 0], dev_s)

    def r1(p):
        got(RBS.at[p], rs_r.at[p, 0])
        T1[p, 0] = (GB[p, chip_d, c].astype(F32) + RBS[p, chip_d].astype(F32)).astype(BF)
        T1[p, 1] = (GB[p, first, c].astype(F32) + RBS[p, first].astype(F32)).astype(BF)
        send(T1.at[p], R1.at[p], rs_s.at[p, 1], rs_r.at[p, 1], dev_1)

    def r2(p):
        got(R1.at[p], rs_r.at[p, 1])
        T2[p] = (
            GB[p, second, c].astype(F32) + RBS[p, second].astype(F32) + R1[p, 0].astype(F32)
        ).astype(BF)
        send(T2.at[p], R2.at[p], rs_s.at[p, 2], rs_r.at[p, 2], dev_2)

    def r3(p):
        got(R2.at[p], rs_r.at[p, 2])
        own = (
            GB[p, chip, c].astype(F32)
            + RBS[p, chip].astype(F32)
            + R1[p, 1].astype(F32)
            + R2[p].astype(F32)
        )
        if p == 3:
            got(RZ.at[2], rs_r.at[2, 3])
            own = own + RZ[2].astype(F32)
        if p in far:
            ZB[p] = own.astype(BF)
            send(ZB.at[p], RZ.at[p], rs_s.at[p, 3], rs_r.at[p, 3], dev_z[far[p]])
        elif p == 0:
            g_u[...] = own
        elif p == 1:
            g_d[...] = own
        else:
            g_a[...] = own

    def reduce(*steps):
        for step, p in steps:
            (r0, r1, r2, r3)[step](p)

    barrier = pltpu.get_barrier_semaphore()
    for dev in (dev_s, dev_x, dev_y, dev_d, dev_z[1], dev_z[2], dev_z[3]):
        pl.semaphore_signal(barrier, inc=1, device_id=dev, device_id_type=MESH)

    ready(0, 1)
    shard = jnp.concatenate([w_in[0], w_in[2], w_in[1], w_out[...].T], axis=1)
    G[z, chip, c] = shard.astype(BF)
    pl.semaphore_wait(barrier, 7)
    gather_step(0)

    SMI[...] = jnp.zeros_like(SMI)
    ready(2, 3, 4)
    SMI[0:HG, 0:529] = tab[...]
    SMI[6:7, 0:192] = hb[0:1, :]
    SMI[6:7, 192:384] = hb[1:2, :]
    SMI[7:8, :] = ub[...].reshape(1, FQ)
    for k in (1, 2, 3):
        send(SMI, SMG.at[z], ms.at[k], mr.at[k], dev_z[k])
    SMG[z] = SMI[...]

    ready(5, 6)
    xp = dot(padded_rows(z), img[...])
    normal, rs = norm_stats(xp)
    N1[...] = normal
    RS1[...] = rs
    LOW1[...] = (normal * nv[0:1, :] + nv[1:2, :]).astype(BF)
    ready(7, 8)
    G[4, chip, c] = w_up[...].astype(BF)
    G[5, chip, c] = w_dn[...].astype(BF)
    gather_step(1)
    ET[...] = pad_hot_t()
    LOW1T[...] = LOW1[...].T
    XC[...] = dot(ET[...], xp.astype(BF))
    BR[...] = jnp.zeros_like(BR)
    ZT[...] = jnp.zeros_like(ZT)
    DZ[...] = jnp.zeros_like(DZ)
    SMO[...] = jnp.zeros_like(SMO)

    for k in (1, 2, 3):
        got(SMG.at[zx[k]], mr.at[k])
    table = SMG[:, :, 0:TABL].reshape(32, TABL)
    stride = stride_hot()
    table = sum(dot(part, stride) for part in split_three(table))
    for ci in range(WIN):
        turned = table if ci == 0 else pltpu.roll(table, TABS - ci, 1)
        GB[ci // 8, ci % 8 // 2, ci % 2] = jnp.concatenate(split_three(turned), axis=0)
    offset = offset_hot()
    for first_ci, rows in ((0, GB[0].reshape(768, 768)), (8, GB[1, 0:2].reshape(384, 768))):
        spread = dot(rows, offset)
        for j in range(spread.shape[0] // SHARD):
            part = spread[j * SHARD : j * SHARD + SHARD]
            part = part[0:32] + part[32:64] + part[64:96]
            for t in range(3):
                ZT[t, pl.ds(first_ci + j, 32, stride=ROWP), :] = part[:, t * 128 : t * 128 + 128]

    qi = iota((WPAD, 1), 0)
    kj = iota((1, WPAD), 1)
    q_r, q_c = lax.shift_right_logical(qi, 4), jnp.bitwise_and(qi, ROWP - 1)
    k_r, k_c = lax.shift_right_logical(kj, 4), jnp.bitwise_and(kj, ROWP - 1)
    cut_r = ((q_r >= SHIFT) != (k_r >= SHIFT)) & (z // 2 == 1)
    cut_c = ((q_c >= SHIFT) != (k_c >= SHIFT)) & (z % 2 == 1)
    fill = jnp.where(cut_r | cut_c, FILL_VALUE, 0.0)
    GONE[:, 0:WPAD] = jnp.where(k_c < WIN, fill, -1e30)

    def bias_step(zz, carry):
        at = pl.ds(pl.multiple_of(zz * 8 * ROWP, 8 * ROWP), HG * ROWP)
        rows = jnp.concatenate([ZT[t, at, :] for t in range(3)], axis=1)
        for ri in range(WIN):
            left = (WIN - 1 - ri) * ROWP
            block = rows[:, left : left + WPAD].reshape(HG, ROWP, WPAD)
            fill = GONE[ri * ROWP : ri * ROWP + ROWP, 0:WPAD]
            PB[pl.ds(zz * HG, HG), ri * ROWP : ri * ROWP + ROWP, :] = block + fill[None]
        return carry

    lax.fori_loop(0, 4, bias_step, 0)
    GONE[...] = jnp.zeros_like(GONE)
    gather_step(2)

    def zk(k):
        return (z // 2 + k // 2) % 2 * 2 + (z % 2 + k % 2) % 2

    def near_of(k):
        across = (1 - half) * k + half * (3 - k)
        beside = z + (1 - 2 * (z % 2)) * k
        far_half = k // 2
        return far_half * across + (1 - far_half) * beside

    def group_forward(zz):
        whole = G[zz].reshape(768, 768)
        qvk = (dot(LOW1[...], whole) + SMG[zz, 6:7, :]).astype(BF)
        QVK[zz] = qvk
        mixed = [None, None]
        for e in range(HG):
            ta, la, tb, lb = e // 4, 32 * (e % 4), (e + 2) // 4, 32 * ((e + 2) % 4)
            q_t = qvk[:, ta * 128 : ta * 128 + 128]
            k_t = qvk[:, 384 + ta * 128 : 512 + ta * 128]
            v_t = qvk[:, 128 + tb * 128 : 256 + tb * 128]
            s = dot_nt(mask_head(q_t, la), k_t) * SCALE + PB[zz * HG + e]
            p = jnp.exp(s - jnp.max(s, axis=-1, keepdims=True))
            p = p * (1.0 / jnp.sum(p, axis=-1, keepdims=True))
            PB[zz * HG + e] = p
            add = dot(p.astype(BF), mask_head(v_t, lb))
            mixed[tb] = add if mixed[tb] is None else mixed[tb] + add
        mixed = jnp.concatenate(mixed, axis=1).astype(BF)
        MX[zz] = mixed
        BR[...] += dot_nt(dot(ET[...], mixed).astype(BF), whole[:, 512:768])

    def forward_step(k, carry):
        for j in range(4):
            @pl.when(k == j)
            def _():
                if j > 0:
                    gather_step(j + 2)
                s3(j)

        group_forward(near_of(k))
        return carry

    lax.fori_loop(0, 4, forward_step, 0)

    gather_step(6)
    normal, rs = norm_stats(XC[...] + BR[...] + nv[4:5, :])
    N2H[...] = normal
    RS2[...] = rs
    N2[z] = (normal * nv[2:3, :] + nv[3:4, :]).astype(BF)
    line_start(blocks_of(N2), 3)

    def ff_quarter(w, q, act, gh):
        zq = (z // 2 + q) % 2 * 2 + z % 2

        def ff_step(n, carry):
            at = pl.ds(pl.multiple_of(n * 256, 256), 256)
            up = G[4 + 2 * q, :, :, :, at].reshape(768, 256)
            down = G[5 + 2 * q, :, :, :, at].reshape(768, 256)
            u = dot(N2[w], up) + SMG[zq, 7:8, at]
            u2 = u * u
            th = jnp.tanh(0.7978845608028654 * (u + 0.044715 * (u2 * u)))
            half_up = 0.5 * (1.0 + th)
            act[:, at] = (u * half_up).astype(BF)
            slope = half_up + 0.5 * u * (1.0 - th * th) * (
                0.7978845608028654 * (1.0 + 3 * 0.044715 * u2)
            )
            gh[:, at] = (dot(GL[w], down) * slope).astype(BF)
            return carry

        lax.fori_loop(0, 3, ff_step, 0)

    def ff_own(w):
        ff_quarter(w, 0, ACT.at[w], GH.at[w])

    def ff_other(b):
        ff_quarter(zx[b], 1, ACT1.at[b], GH1.at[b])

    def ff_two(b):
        return dot_nt(GH[zx[b]], G[4].reshape(768, 768)) + dot_nt(GH1[b], G[6].reshape(768, 768))

    def ff_out(b):
        return dot_nt(ACT[zx[b]], G[5].reshape(768, 768)) + dot_nt(ACT1[b], G[7].reshape(768, 768))

    def ff_grad(p):
        left, right = (N2, GH) if p == 0 else (GL, ACT)

        def grad_step(j, carry):
            at = pl.ds(pl.multiple_of(j * 384, 384), 384)
            rows = left[:, :, at].reshape(TOK, 384)
            grad = dot_tn(rows, right[...].reshape(TOK, 768))
            GB[p, pl.ds(2 * j, 2)] = grad.astype(BF).reshape(2, 2, SHARD, 768)
            return carry

        lax.fori_loop(0, 2, grad_step, 0)

    ready(9)
    rows = dot(window_rows(), cot[...]) * msk[0].astype(F32)
    GL[...] = rows.astype(BF).reshape(4, WTOK, 768)
    gather_step(7)
    s3(4)
    s3(5)
    ff_own(z)
    line_step(blocks_of(N2), 3, 1)
    gather_step(8)
    ff_own(zx[1])
    gather_step(9)
    s3(6)
    s3(7)
    ff_other(1)
    G2S[...] = ff_two(1).astype(BF)
    send(G2S, G2R, es.at[1], er.at[1], dev_z[1])
    line_step(blocks_of(N2), 3, 2)
    OS[...] = ff_out(1).astype(BF)
    send(OS, OR, es.at[2], er.at[2], dev_z[1])
    ff_other(0)
    G2P[...] = ff_two(0)

    got(G2R, er.at[1])
    g2 = G2P[...] + G2R[...].astype(F32)
    g_out = GL[z].astype(F32)
    gain2 = col_sum(g2 * N2H[...])
    shift2 = col_sum(g2)
    g_mid = g_out + norm_back(g2, nv[2:3, :], N2H[...], RS2[...])
    GMID[...] = g_mid
    g_branch = g_mid.astype(BF)
    GBP[...] = dot(pad_hot(), g_branch).astype(BF)
    GBPT[...] = GBP[...].T
    bias_b = col_sum(g_branch.astype(F32))
    bias_o = col_sum(g_out)

    def group_backward(zz, p_at):
        whole = G[zz].reshape(768, 768)
        d_out = dot(GBP[...], whole[:, 512:768]).astype(BF)
        qvk = QVK[zz]
        dq, dk, dv = [None, None], [None, None], [None, None]

        def add(parts, t, v):
            parts[t] = v if parts[t] is None else parts[t] + v

        for e in range(HG):
            ta, la, tb, lb = e // 4, 32 * (e % 4), (e + 2) // 4, 32 * ((e + 2) % 4)
            q_t = qvk[:, ta * 128 : ta * 128 + 128]
            k_t = qvk[:, 384 + ta * 128 : 512 + ta * 128]
            v_t = qvk[:, 128 + tb * 128 : 256 + tb * 128]
            p = PB[zz * HG + e]
            d_o = mask_head(d_out[:, tb * 128 : tb * 128 + 128], lb)
            dp = dot_nt(d_o, v_t)
            add(dv, tb, dot_tn(p.astype(BF), d_o))
            ds = (p * (dp - jnp.sum(dp * p, axis=-1, keepdims=True))).astype(BF)
            DS[zz * HG + e] = ds
            add(dq, ta, dot(ds, mask_head(k_t, la)))
            add(dk, ta, dot_tn(ds, mask_head(q_t, la)))
        dq = [v * SCALE for v in dq]
        dk = [v * SCALE for v in dk]
        full = jnp.concatenate(
            [dq[0], dq[1] + dv[0], dv[1], dk[0], dk[1], jnp.zeros_like(dk[1])], axis=1
        ).astype(BF)
        GONE[...] += dot_nt(full[:, 0:640], whole[:, 0:640])
        SMO[zz, 6:7, :] = col_sum(full.astype(F32))
        FULL[...] = full

        def grad_step(j, carry):
            at = pl.ds(pl.multiple_of(j * 384, 384), 384)
            rows = LOW1T[at, :]
            main = dot(rows, FULL[:, 0:512])
            tail = dot(rows, FULL[:, 512:768]) + dot(GBPT[at, :], MX[zz])
            grad = jnp.concatenate([main, tail], axis=1).astype(BF)
            GB[p_at, pl.ds(2 * j, 2)] = grad.reshape(2, 2, SHARD, 768)
            return carry

        lax.fori_loop(0, 2, grad_step, 0)

    def block_rows():
        got(OR, er.at[2])
        out = ff_out(0) + OR[...].astype(F32) + nv[5:6, :]
        BO[z] = (XC[...] + BR[...] + nv[4:5, :] + out).astype(BF)
        line_start(blocks_of(BO), 0)

    def backward_step(i, carry):
        group_backward(zk(3 - i), 2 + i)
        for j in range(4):
            @pl.when(i == j)
            def _():
                if j == 0:
                    reduce((0, 2))
                    block_rows()
                    line_step(blocks_of(N2), 3, 3)
                if j == 1:
                    reduce((0, 3), (1, 2))
                if j == 2:
                    reduce((0, 4), (1, 3), (2, 2))
                    line_step(blocks_of(BO), 0, 1)
                if j == 3:
                    reduce((0, 5), (1, 4), (3, 2))
        return carry

    lax.fori_loop(0, 4, backward_step, 0)

    g_one = GONE[...]
    gain1 = col_sum(g_one * N1[...])
    shift1 = col_sum(g_one)
    back = norm_back(g_one, nv[0:1, :], N1[...], RS1[...])
    b_high, b_low = split_two(back)
    back = dot(ET[...], b_high) + dot(ET[...], b_low)
    IG[z] = (GMID[...] + back).astype(BF)
    line_start(blocks_of(IG), 1)

    def leave(w, ok):
        @pl.when(ok)
        def _():
            local(IG.at[w], ig_out.at[w], 14 + w).start()

    leave(z, z >= 0)
    reduce((2, 3), (1, 5))
    line_step(blocks_of(BO), 0, 2)

    ff_own(zx[2])
    ff_own(zx[3])
    reduce((3, 3))
    ff_grad(0)
    reduce((0, 0), (2, 4))
    line_step(blocks_of(IG), 1, 1)
    leave((z + 4 - 1) % 4, z >= 1)
    leave((z + 1) % 4, z + 1 <= 3)
    ff_grad(1)
    reduce((0, 1), (1, 0), (3, 4), (2, 5))
    SMO[z, 8:9, :] = col_sum(GH[...].reshape(TOK, 768).astype(F32))

    def table_step(ri, carry):
        at = pl.ds(pl.multiple_of(ri * ROWP, ROWP), ROWP)
        pick = hot(iota((WPAD, ZL), 1) == iota((WPAD, ZL), 0) + (WIN - 1 - ri) * ROWP)
        sums = dot(DS[:, at, :].reshape(4 * HG * ROWP, WPAD), pick)
        for t in range(3):
            DZ[t] += sums[:, t * 128 : t * 128 + 128]
        return carry

    lax.fori_loop(0, WIN, table_step, 0)
    reduce((1, 1), (3, 5))
    line_step(blocks_of(BO), 0, 3)
    local(BO, bo_out, 10).start()

    rows = [
        jnp.concatenate([DZ[t, pl.ds(ci, 4 * HG, stride=ROWP), :] for t in range(3)], axis=1)
        for ci in range(WIN)
    ]
    offset = offset_hot()
    sums = sum(dot_nt(part, offset) for part in split_two(jnp.concatenate(rows, axis=0)))
    total = sums[0 : 4 * HG]
    for ci in range(1, WIN):
        total = total + pltpu.roll(sums[ci * 4 * HG : (ci + 1) * 4 * HG], ci, 1)
    stride = stride_hot()
    total = sum(dot_nt(part, stride) for part in split_two(total))
    for zz in range(4):
        SMO[zz, 0:HG, 0:TABL] = total[zz * HG : zz * HG + HG]
        for j, row in enumerate((gain1, shift1, gain2, shift2, bias_b, bias_o)):
            SMO[zz, 9 + j : 10 + j, :] = row
    for k in (1, 2, 3):
        send(SMO.at[zx[k]], SMR.at[k], qs.at[k], qr.at[k], dev_z[k])
    reduce((2, 0))
    line_step(blocks_of(IG), 1, 2)
    leave((z + 4 - 2) % 4, z >= 2)
    leave((z + 2) % 4, z + 2 <= 3)
    small = SMO[z]
    for k in (1, 2, 3):
        got(SMR.at[k], qr.at[k])
        small = small + SMR[k]
    SMT[0] = small
    send(SMT.at[0], SMS.at[0], qs.at[4], qr.at[4], dev_s)
    reduce((2, 1))
    got(SMS.at[0], qr.at[4])
    small = small + SMS[0]
    SMT[1] = small
    for j, dev in enumerate((dev_x, dev_y, dev_d)):
        send(SMT.at[1], SMS.at[1 + j], qs.at[5 + j], qr.at[5 + j], dev)
    reduce((3, 0))
    local(g_u, gu_out, 11).start()
    for j in range(3):
        got(SMS.at[1 + j], qr.at[5 + j])
        small = small + SMS[1 + j]
    reduce((3, 1))
    local(g_d, gd_out, 12).start()
    sm_out[...] = small

    for p in (3, 4):
        got(RZ.at[p], rs_r.at[p, 3])
    g_a[...] += RZ[3].astype(F32) + RZ[4].astype(F32)
    local(g_a, ga_out, 13).start()
    line_step(blocks_of(IG), 1, 3)
    leave((z + 4 - 3) % 4, z >= 3)
    leave((z + 3) % 4, z + 3 <= 3)

    item = G.at[0, 0, 0]
    for k in (1, 2, 3):
        sent(SMI, ms.at[k])
        sent(SMO.at[0], qs.at[k])
        sent(SMO.at[0], qs.at[4 + k])
    sent(item, zs.at[6])
    sent(item, zs.at[7])
    line_drain(blocks_of(N2), 3)
    sent(G2S, es.at[1])
    sent(OS, es.at[2])
    sent(SMO.at[0], qs.at[4])
    line_drain(blocks_of(BO), 0)
    line_drain(blocks_of(IG), 1)
    line_drain(own_items, 2)
    for k in range(8):
        for j in range(7):
            sent(item, gs.at[k, j])
    for p in range(6):
        sent(RBS.at[p], rs_s.at[p, 0])
        sent(T1.at[p], rs_s.at[p, 1])
        sent(T2.at[p], rs_s.at[p, 2])
    for p in far:
        sent(ZB.at[p], rs_s.at[p, 3])
    for w in range(4):
        local(IG.at[w], ig_out.at[w], 14 + w).wait()
    for j, (src, dst) in enumerate(((BO, bo_out), (g_u, gu_out), (g_d, gd_out), (g_a, ga_out))):
        local(src, dst, 10 + j).wait()


def vm(shape, dtype=F32):
    return pltpu.VMEM(shape, dtype)


def main_call(args):
    f32 = lambda *s: jax.ShapeDtypeStruct(s, F32)
    bf = lambda *s: jax.ShapeDtypeStruct(s, BF)
    dma = lambda *s: pltpu.SemaphoreType.DMA(s)
    vspec = pl.BlockSpec(memory_space=pltpu.VMEM)
    hbm = pl.BlockSpec(memory_space=pl.ANY)
    specs = [hbm] * len(args)
    specs[2] = pl.BlockSpec(memory_space=pltpu.SMEM)
    scratch = [
        vm((8, 4, 2, SHARD, 768), BF),
        vm((6, 4, 2, SHARD, 768), BF),
        vm((6, 4, SHARD, 768), BF),
        vm((6, 2, SHARD, 768), BF),
        vm((6, 2, SHARD, 768), BF),
        vm((6, SHARD, 768), BF),
        vm((6, SHARD, 768), BF),
        vm((6, SHARD, 768), BF),
        vm((6, SHARD, 768), BF),
        vm((4 * HG, WPAD, WPAD)),
        vm((3, 32 * ROWP, 128)),
        vm((4, WPAD, 768), BF),
        vm((4, WPAD, 256), BF),
        vm((4 * HG, WPAD, WPAD), BF),
        vm((3, 4 * HG * ROWP, 128)),
        vm((WPAD, 768), BF),
        vm((WPAD, 768)),
        vm((WPAD, 1)),
        vm((WTOK, 768)),
        vm((WTOK, 768)),
        vm((WTOK, 768)),
        vm((WTOK, 1)),
        vm((4, WTOK, 768), BF),
        vm((4, WTOK, 768), BF),
        vm((4, WTOK, FQ), BF),
        vm((4, WTOK, FQ), BF),
        vm((2, WTOK, FQ), BF),
        vm((2, WTOK, FQ), BF),
        vm((WTOK, 768)),
        vm((WTOK, 768), BF),
        vm((WTOK, 768), BF),
        vm((WTOK, 768), BF),
        vm((WTOK, 768), BF),
        vm((WTOK, 768)),
        vm((WPAD, 768), BF),
        vm((WTOK, WPAD), BF),
        vm((WPAD, 768)),
        vm((4, WTOK, 768), BF),
        vm((4, WTOK, 768), BF),
        vm((8, 768)),
        vm((4, 8, 768)),
        vm((4, 16, 768)),
        vm((4, 16, 768)),
        vm((2, 16, 768)),
        vm((4, 16, 768)),
        vm((WPAD, 768), BF),
        vm((768, WPAD), BF),
        vm((768, WPAD), BF),
        vm((TOK, 768), BF),
        vm((TOK, 768), BF),
        vm((3, SHARD, 192)),
        vm((192, SHARD)),
        vm((SHARD, 768)),
        vm((SHARD, 768)),
        vm((6, 768)),
        vm((2, 192)),
        vm((FQ,)),
        vm((HG, 529)),
        vm((SHARD, 768)),
        vm((SHARD, 768)),
        vm((SHARD, 768)),
        dma(8, 7), dma(8, 7),
        dma(8), dma(8),
        dma(4), dma(4),
        dma(3), dma(3),
        dma(8, 4), dma(8, 4),
        dma(4, 4, 2), dma(4, 4),
        dma(8), dma(8),
        dma(18),
    ]
    return pl.pallas_call(
        main_kernel,
        out_shape=(
            f32(SHARD, 768), f32(SHARD, 768), f32(SHARD, 768), f32(16, 768),
            bf(4, WTOK, 768), bf(4, WTOK, 768),
        ),
        in_specs=specs,
        out_specs=tuple([hbm] * 3 + [vspec] + [hbm] * 2),
        scratch_shapes=scratch,
        compiler_params=pltpu.CompilerParams(
            collective_id=0, has_side_effects=True, vmem_limit_bytes=62 * 2**20
        ),
        cost_estimate=pl.CostEstimate(flops=7 * 10**9, bytes_accessed=10**7, transcendentals=10**6),
    )(*args)


def last_kernel(n_in, n_out, *refs):
    given, made = refs[:n_in], refs[n_in : n_in + n_out]
    held = refs[n_in + n_out : 2 * n_in + n_out]
    done = refs[2 * n_in + n_out : 2 * (n_in + n_out)]
    in_sem, out_sem = refs[2 * (n_in + n_out) :]
    g_a, g_u, g_d, sm, bo, ig = range(6)

    def load(j):
        return pltpu.make_async_copy(given[j], held[j], in_sem.at[j])

    def store(j):
        return pltpu.make_async_copy(done[j], made[j], out_sem.at[j])

    order = [ig, bo, g_u, 12, 13, 14, g_d, 15, 16, 17, g_a, 6, 7, 8, 9, 10, 11, sm] + list(range(18, 30))
    for j in order:
        load(j).start()

    def wait(*js):
        for j in js:
            load(j).wait()

    token = iota((TOK, 1), 0)
    row = lax.shift_right_logical(token * 2731, 16)
    col = token - row * SIDE
    row = jnp.where(row >= SHIFT, row - SHIFT, row + SIDE - SHIFT)
    col = jnp.where(col >= SHIFT, col - SHIFT, col + SIDE - SHIFT)
    wr, wc = (row >= WIN).astype(jnp.int32), (col >= WIN).astype(jnp.int32)
    at = (wr * 2 + wc) * WTOK + (row - WIN * wr) * WIN + col - WIN * wc
    back = hot(at == iota((TOK, TOK), 1))
    wait(ig)
    done[1][0] = dot(back, held[ig][...].reshape(TOK, 768))
    store(1).start()
    wait(bo)
    done[0][0] = dot(back, held[bo][...].reshape(TOK, 768)).astype(BF)
    store(0).start()

    def adam(param, out, at, grad, low, vector=False):
        w, f, s = (held[param + j][at] for j in range(3))
        rate, decay = (RATE_VECTOR, 0.0) if vector else (RATE_MATRIX, DECAY_MATRIX)
        moment, square, updated = adam_update(w, f, s, grad, rate, decay)
        done[out][at], done[out + 1][at], done[out + 2][at] = moment, square, updated
        if low:
            done[out + 3][at] = updated.astype(BF)

    def finish(out, count):
        for j in range(out, out + count):
            store(j).start()

    whole = slice(None)
    wait(g_u, 12, 13, 14)
    adam(12, 10, whole, held[g_u][...], True)
    finish(10, 4)
    wait(g_d, 15, 16, 17)
    adam(15, 14, whole, held[g_d][...], True)
    finish(14, 4)
    wait(g_a, 6, 7, 8)
    for j, lane in ((0, 0), (1, 384), (2, 192)):
        adam(6, 2, j, held[g_a][:, lane : lane + 192], True)
    finish(2, 4)
    eye = jnp.where(iota((SHARD, SHARD), 0) == iota((SHARD, SHARD), 1), 1.0, 0.0)
    turned = lax.dot_general(
        held[g_a][:, 576:768], eye, (((0,), (0,)), ((), ())),
        precision=lax.Precision.HIGHEST, preferred_element_type=F32,
    )
    wait(9, 10, 11)
    adam(9, 6, whole, turned, True)
    finish(6, 4)
    small = held[sm]
    wait(sm, *range(18, 30))
    adam(18, 18, whole, small[9:15, :], False, True)
    for j in (0, 1):
        adam(21, 21, slice(j, j + 1), small[6:7, 192 * j : 192 * j + 192], False, True)
    adam(24, 24, whole, small[8:9, :].reshape(FQ), False, True)
    adam(27, 27, whole, small[0:HG, 0:529], False, True)
    finish(18, 12)
    for j in range(n_out):
        store(j).wait()


def last_call(sums, params):
    hbm = pl.BlockSpec(memory_space=pl.ANY)
    like = lambda a, t=F32: jax.ShapeDtypeStruct(a.shape, t)
    outs = [jax.ShapeDtypeStruct((1, TOK, 768), BF), jax.ShapeDtypeStruct((1, TOK, 768), F32)]
    for j in range(0, 12, 3):
        outs += [like(params[j])] * 3 + [like(params[j], BF)]
    for j in range(12, 24, 3):
        outs += [like(params[j])] * 3
    ins = list(sums) + list(params)
    return pl.pallas_call(
        functools.partial(last_kernel, len(ins), len(outs)),
        out_shape=tuple(outs),
        in_specs=[hbm] * len(ins),
        out_specs=tuple([hbm] * len(outs)),
        scratch_shapes=[vm(a.shape, a.dtype) for a in ins + outs]
        + [pltpu.SemaphoreType.DMA((len(ins),)), pltpu.SemaphoreType.DMA((len(outs),))],
        compiler_params=pltpu.CompilerParams(vmem_limit_bytes=62 * 2**20),
        cost_estimate=pl.CostEstimate(flops=10**9, bytes_accessed=15 * 10**6, transcendentals=10**6),
    )(*ins)


def on_device_windows(images, cotangent, image_mask, *params):
    params = list(params)
    turned = (9, 10, 11, 21, 22, 23)
    for j in turned:
        params[j] = params[j].T
    (in_w, _, _, out_w, _, _, up_w, _, _, dn_w, _, _, nv, _, _, hb, _, _, ub, _, _, tab, _, _) = params
    sums = main_call(
        (
            images.reshape(TOK, D), cotangent.reshape(TOK, D), image_mask,
            in_w, out_w, up_w, dn_w, nv, hb, ub, tab,
        )
    )
    outs = list(last_call(sums, params))
    for j in (14, 15, 16, 17, 27, 28, 29):
        outs[j] = outs[j].T
    return tuple(outs)


def solution(mesh):
    shape = mesh.shape
    windows = shape["dp"] == 8 and shape["tensor"] == 4
    return jax.shard_map(
        on_device_windows if windows else on_device,
        mesh=mesh,
        in_specs=(
            P("dp", None, None),
            P("dp", None, None),
            P("dp"),
            P(None, "dp", "tensor"),
            P(None, "dp", "tensor"),
            P(None, "dp", "tensor"),
            P("tensor", "dp"),
            P("tensor", "dp"),
            P("tensor", "dp"),
            P("dp", "tensor"),
            P("dp", "tensor"),
            P("dp", "tensor"),
            P("tensor", "dp"),
            P("tensor", "dp"),
            P("tensor", "dp"),
            P(),
            P(),
            P(),
            P(None, "tensor"),
            P(None, "tensor"),
            P(None, "tensor"),
            P("tensor"),
            P("tensor"),
            P("tensor"),
            P(None, "tensor"),
            P(None, "tensor"),
            P(None, "tensor"),
        ),
        out_specs=(
            P("dp", None, None),
            P("dp", None, None),
            P(None, "dp", "tensor"),
            P(None, "dp", "tensor"),
            P(None, "dp", "tensor"),
            P(None, "dp", "tensor"),
            P("tensor", "dp"),
            P("tensor", "dp"),
            P("tensor", "dp"),
            P("tensor", "dp"),
            P("dp", "tensor"),
            P("dp", "tensor"),
            P("dp", "tensor"),
            P("dp", "tensor"),
            P("tensor", "dp"),
            P("tensor", "dp"),
            P("tensor", "dp"),
            P("tensor", "dp"),
            P(),
            P(),
            P(),
            P(None, "tensor"),
            P(None, "tensor"),
            P(None, "tensor"),
            P("tensor"),
            P("tensor"),
            P("tensor"),
            P(None, "tensor"),
            P(None, "tensor"),
            P(None, "tensor"),
        ),
        check_vma=False,
    )
```

```python
import functools
from functools import partial

import jax
import jax.numpy as jnp
from jax import lax
from jax.experimental import pallas as pl
from jax.experimental.pallas import tpu as pltpu
from jax.sharding import PartitionSpec as P

D = 768
HEAD_DIM = 32
WIN = 12
SIDE = 24
STEP = 7
SHIFT = 6


NORM_EPS = 1e-05
FILL_VALUE = -100.0
BETA_ONE = 0.5
BETA_TWO = 0.5
ADAM_EPS = 1e-08
RATE_MATRIX = 0.05
RATE_VECTOR = 0.3
DECAY_MATRIX = 0.05


def layer_norm(values, gain_in, offset_in):
    center = values - jnp.mean(values, axis=-1, keepdims=True)
    spread = jnp.mean(center * center, axis=-1, keepdims=True)
    return center * lax.rsqrt(spread + NORM_EPS) * gain_in + offset_in


def adam_update(weight, first_old, second_old, gradient, rate_of, decay_of):
    moment = BETA_ONE * first_old + (1.0 - BETA_ONE) * gradient
    square = BETA_TWO * second_old + (1.0 - BETA_TWO) * gradient * gradient
    moment_fix = moment / (1.0 - BETA_ONE**STEP)
    square_fix = square / (1.0 - BETA_TWO**STEP)
    updated = weight * (1.0 - rate_of * decay_of) - rate_of * moment_fix / (
        jnp.sqrt(square_fix) + ADAM_EPS
    )
    return (moment, square, updated)


def dot_plain(left_side, right_side):
    return jnp.dot(left_side, right_side, preferred_element_type=jnp.float32)


def dot_back(left_side, right_side):
    return lax.dot_general(
        left_side, right_side, (((1,), (1,)), ((), ())), preferred_element_type=jnp.float32
    )


def dot_rows(left_side, right_side):
    return lax.dot_general(
        left_side, right_side, (((0,), (0,)), ((), ())), preferred_element_type=jnp.float32
    )


def to_heads(token_rows, images_here, heads_here):
    blocks = SIDE // WIN
    grid_view = token_rows.reshape(images_here, SIDE, SIDE, heads_here * HEAD_DIM)
    grid_view = jnp.roll(grid_view, (-SHIFT, -SHIFT), (1, 2))
    grid_view = grid_view.reshape(
        images_here, blocks, WIN, blocks, WIN, heads_here, HEAD_DIM
    ).transpose(0, 1, 3, 2, 4, 5, 6)
    return grid_view.reshape(images_here, blocks * blocks, WIN * WIN, heads_here, HEAD_DIM)


def from_heads(windows, images_here):
    blocks = SIDE // WIN
    channels = windows.shape[3] * windows.shape[4]
    grid_view = windows.reshape(images_here, blocks, blocks, WIN, WIN, channels).transpose(
        0, 1, 3, 2, 4, 5
    )
    grid_view = jnp.roll(
        grid_view.reshape(images_here, SIDE, SIDE, channels), (SHIFT, SHIFT), (1, 2)
    )
    return grid_view.reshape(images_here * SIDE * SIDE, channels)


def window_fill():
    blocks = SIDE // WIN
    cell_ids = jnp.arange(SIDE, dtype=jnp.int32)
    band_of = (cell_ids >= SIDE - WIN).astype(jnp.int32) + (cell_ids >= SIDE - SHIFT).astype(
        jnp.int32
    )
    region = band_of[:, None] * 3 + band_of[None, :]
    labels = (
        region.reshape(blocks, WIN, blocks, WIN)
        .transpose(0, 2, 1, 3)
        .reshape(blocks * blocks, WIN * WIN)
    )
    return jnp.where(labels[:, :, None] != labels[:, None, :], FILL_VALUE, 0.0).astype(jnp.float32)


def offset_onehot():
    places = jnp.arange(WIN, dtype=jnp.int32)
    spans = jnp.arange(2 * WIN - 1, dtype=jnp.int32)
    return (places[:, None, None] - places[None, :, None] + WIN - 1 == spans[None, None, :]).astype(
        jnp.float32
    )


def window_scores(query_win, key_win, bias_add, fill_add):
    scores = jnp.einsum(
        "inqhd,inkhd->inhqk", query_win, key_win, preferred_element_type=jnp.float32
    ) * HEAD_DIM ** (-0.5)
    return scores + bias_add[None, None] + fill_add[None, :, None]


def on_device(
    images,
    cotangent,
    image_mask,
    in_weight,
    in_first,
    in_second,
    out_weight,
    out_first,
    out_second,
    up_weight,
    up_first,
    up_second,
    down_weight,
    down_first,
    down_second,
    norm_vector,
    norm_first,
    norm_second,
    head_bias,
    head_first,
    head_second,
    up_bias,
    bias_first,
    bias_second,
    position_table,
    table_first,
    table_second,
):
    lowtype = jnp.bfloat16
    highest = lax.Precision.HIGHEST
    whole_in, whole_out, whole_up, whole_down = (
        lax.all_gather(in_weight.astype(lowtype), "dp", axis=1, tiled=True),
        lax.all_gather(out_weight.astype(lowtype), "dp", axis=1, tiled=True),
        lax.all_gather(up_weight.astype(lowtype), "dp", axis=0, tiled=True),
        lax.all_gather(down_weight.astype(lowtype), "dp", axis=1, tiled=True),
    )
    images_here = images.shape[0]
    heads_here = whole_in.shape[2] // HEAD_DIM
    span_count = 2 * WIN - 1
    token_rows = images.reshape(-1, D).astype(jnp.float32)
    normed_one, norm_one_back = jax.vjp(layer_norm, token_rows, norm_vector[0], norm_vector[1])
    low_one = normed_one.astype(lowtype)
    query_rows = (dot_plain(low_one, whole_in[0]) + head_bias[0]).astype(lowtype)
    key_rows = dot_plain(low_one, whole_in[1]).astype(lowtype)
    value_rows = (dot_plain(low_one, whole_in[2]) + head_bias[1]).astype(lowtype)
    query_win = to_heads(query_rows, images_here, heads_here)
    key_win = to_heads(key_rows, images_here, heads_here)
    value_win = to_heads(value_rows, images_here, heads_here)
    onehot = offset_onehot()
    table_view = position_table.reshape(span_count, span_count, heads_here)
    bias_add = jnp.einsum(
        "xya,zwb,abh->hxzyw", onehot, onehot, table_view, precision=highest
    ).reshape(heads_here, WIN * WIN, WIN * WIN)
    fill_add = window_fill()
    scores = window_scores(query_win, key_win, bias_add, fill_add)
    row_top = jnp.max(scores, axis=-1, keepdims=True)
    weights_raw = jnp.exp(scores - row_top)
    row_total = jnp.sum(weights_raw, axis=-1, keepdims=True)
    log_total = row_top + jnp.log(row_total)
    prob_low = (weights_raw / row_total).astype(lowtype)
    mixed_win = jnp.einsum(
        "inhqk,inkhd->inqhd", prob_low, value_win, preferred_element_type=jnp.float32
    ).astype(lowtype)
    mixed_rows = from_heads(mixed_win, images_here)
    branch_share = lax.psum_scatter(
        dot_plain(mixed_rows, whole_out), "tensor", scatter_dimension=0, tiled=True
    )
    branch = lax.all_gather(branch_share, "tensor", axis=0, tiled=True) + norm_vector[4]
    middle = token_rows + branch
    normed_two, norm_two_back = jax.vjp(layer_norm, middle, norm_vector[2], norm_vector[3])
    low_two = normed_two.astype(lowtype)
    hidden = dot_plain(low_two, whole_up) + up_bias
    active, gelu_back = jax.vjp(partial(jax.nn.gelu, approximate=True), hidden)
    active_low = active.astype(lowtype)
    output_share = lax.psum_scatter(
        dot_plain(active_low, whole_down).astype(jnp.bfloat16),
        "tensor",
        scatter_dimension=0,
        tiled=True,
    ).astype(jnp.float32)
    output = (
        lax.all_gather(output_share.astype(jnp.bfloat16), "tensor", axis=0, tiled=True).astype(
            output_share.dtype
        )
        + norm_vector[5]
    )
    block_out = (middle + output).astype(lowtype).reshape(images.shape)
    keep_rows = jnp.repeat(image_mask.astype(jnp.float32), SIDE * SIDE)[:, None]
    grad_out = cotangent.reshape(-1, D).astype(jnp.float32) * keep_rows
    grad_low = grad_out.astype(lowtype)
    down_grad = dot_rows(active_low, grad_low)
    grad_hidden = gelu_back(dot_back(grad_low, whole_down))[0].astype(lowtype)
    up_grad = dot_rows(low_two, grad_hidden)
    bias_grad = jnp.sum(grad_hidden.astype(jnp.float32), axis=0)
    two_share = lax.psum_scatter(
        dot_back(grad_hidden, whole_up), "tensor", scatter_dimension=0, tiled=True
    )
    grad_two = lax.all_gather(two_share, "tensor", axis=0, tiled=True)
    grad_norm_two, gain_two, offset_two = norm_two_back(grad_two)
    grad_middle = grad_out + grad_norm_two
    grad_branch = grad_middle.astype(lowtype)
    out_grad = dot_rows(mixed_rows, grad_branch)
    grad_mixed = dot_back(grad_branch, whole_out).astype(lowtype)
    grad_win = to_heads(grad_mixed, images_here, heads_here)
    scores_again = window_scores(query_win, key_win, bias_add, fill_add)
    probs = jnp.exp(scores_again - log_total)
    grad_probs = jnp.einsum(
        "inqhd,inkhd->inhqk", grad_win, value_win, preferred_element_type=jnp.float32
    )
    grad_value = jnp.einsum(
        "inhqk,inqhd->inkhd", probs.astype(lowtype), grad_win, preferred_element_type=jnp.float32
    ).astype(lowtype)
    grad_scores = (
        probs * (grad_probs - jnp.sum(grad_probs * probs, axis=-1, keepdims=True))
    ).astype(lowtype)
    grad_query = (
        jnp.einsum("inhqk,inkhd->inqhd", grad_scores, key_win, preferred_element_type=jnp.float32)
        * HEAD_DIM ** (-0.5)
    ).astype(lowtype)
    grad_key = (
        jnp.einsum("inhqk,inqhd->inkhd", grad_scores, query_win, preferred_element_type=jnp.float32)
        * HEAD_DIM ** (-0.5)
    ).astype(lowtype)
    score_sums = jnp.sum(grad_scores.astype(jnp.float32), axis=(0, 1)).reshape(
        heads_here, WIN, WIN, WIN, WIN
    )
    table_grad = jnp.einsum(
        "xya,zwb,hxzyw->abh", onehot, onehot, score_sums, precision=highest
    ).reshape(span_count * span_count, heads_here)
    query_back = from_heads(grad_query, images_here)
    key_back = from_heads(grad_key, images_here)
    value_back = from_heads(grad_value, images_here)
    in_grad = jnp.stack(
        [dot_rows(low_one, query_back), dot_rows(low_one, key_back), dot_rows(low_one, value_back)]
    )
    head_grad = jnp.stack(
        [
            jnp.sum(query_back.astype(jnp.float32), axis=0),
            jnp.sum(value_back.astype(jnp.float32), axis=0),
        ]
    )
    grad_one_terms = (
        dot_back(query_back, whole_in[0])
        + dot_back(key_back, whole_in[1])
        + dot_back(value_back, whole_in[2])
    )
    one_share = lax.psum_scatter(
        grad_one_terms.astype(jnp.bfloat16), "tensor", scatter_dimension=0, tiled=True
    ).astype(jnp.float32)
    grad_one = lax.all_gather(one_share.astype(jnp.bfloat16), "tensor", axis=0, tiled=True).astype(
        one_share.dtype
    )
    grad_norm_one, gain_one, offset_one = norm_one_back(grad_one)
    image_grad = (grad_middle + grad_norm_one).reshape(images.shape)
    norm_grad = jnp.stack(
        [
            gain_one,
            offset_one,
            gain_two,
            offset_two,
            jnp.sum(grad_branch.astype(jnp.float32), axis=0),
            jnp.sum(grad_low.astype(jnp.float32), axis=0),
        ]
    )
    summed = lax.psum(
        (in_grad, out_grad, up_grad, down_grad, norm_grad, head_grad, bias_grad, table_grad), "dp"
    )
    position = lax.axis_index("dp")
    in_total = lax.dynamic_slice_in_dim(
        summed[0], position * in_weight.shape[1], in_weight.shape[1], 1
    )
    out_total = lax.dynamic_slice_in_dim(
        summed[1], position * out_weight.shape[1], out_weight.shape[1], 1
    )
    up_total = lax.dynamic_slice_in_dim(
        summed[2], position * up_weight.shape[0], up_weight.shape[0], 0
    )
    down_total = lax.dynamic_slice_in_dim(
        summed[3], position * down_weight.shape[1], down_weight.shape[1], 1
    )
    norm_total, head_total, bias_total, table_total = (summed[4], summed[5], summed[6], summed[7])
    in_moment, in_square, in_updated = adam_update(
        in_weight, in_first, in_second, in_total, RATE_MATRIX, DECAY_MATRIX
    )
    out_moment, out_square, out_updated = adam_update(
        out_weight, out_first, out_second, out_total, RATE_MATRIX, DECAY_MATRIX
    )
    up_moment, up_square, up_updated = adam_update(
        up_weight, up_first, up_second, up_total, RATE_MATRIX, DECAY_MATRIX
    )
    down_moment, down_square, down_updated = adam_update(
        down_weight, down_first, down_second, down_total, RATE_MATRIX, DECAY_MATRIX
    )
    norm_moment, norm_square, norm_updated = adam_update(
        norm_vector, norm_first, norm_second, norm_total, RATE_VECTOR, 0.0
    )
    head_moment, head_square, head_updated = adam_update(
        head_bias, head_first, head_second, head_total, RATE_VECTOR, 0.0
    )
    bias_moment, bias_square, bias_updated = adam_update(
        up_bias, bias_first, bias_second, bias_total, RATE_VECTOR, 0.0
    )
    table_moment, table_square, table_updated = adam_update(
        position_table, table_first, table_second, table_total, RATE_VECTOR, 0.0
    )
    return (
        block_out,
        image_grad,
        in_moment,
        in_square,
        in_updated,
        in_updated.astype(lowtype),
        out_moment,
        out_square,
        out_updated,
        out_updated.astype(lowtype),
        up_moment,
        up_square,
        up_updated,
        up_updated.astype(lowtype),
        down_moment,
        down_square,
        down_updated,
        down_updated.astype(lowtype),
        norm_moment,
        norm_square,
        norm_updated,
        head_moment,
        head_square,
        head_updated,
        bias_moment,
        bias_square,
        bias_updated,
        table_moment,
        table_square,
        table_updated,
    )


MESH = pl.DeviceIdType.MESH
TOK = SIDE * SIDE
WTOK = WIN * WIN
ROWP = 16
WPAD = WIN * ROWP
FQ = 768
SHARD = 96
HG = 6
TABL = 640
TABS = 768
ZL = 384
SCALE = HEAD_DIM ** (-0.5)
F32 = jnp.float32
BF = jnp.bfloat16


def dot(a, b):
    return lax.dot_general(a, b, (((1,), (0,)), ((), ())), preferred_element_type=F32)


def dot_nt(a, b):
    return lax.dot_general(a, b, (((1,), (1,)), ((), ())), preferred_element_type=F32)


def dot_tn(a, b):
    return lax.dot_general(a, b, (((0,), (0,)), ((), ())), preferred_element_type=F32)


def iota(shape, axis):
    return lax.broadcasted_iota(jnp.int32, shape, axis)


def div12(i):
    return lax.shift_right_logical(i * 171, 11)


def hot(condition):
    return jnp.where(condition, 1.0, 0.0).astype(BF)


def split_two(v):
    high = v.astype(BF)
    return high, (v - high.astype(F32)).astype(BF)


def split_three(v):
    high, _ = split_two(v)
    rest = v - high.astype(F32)
    mid, low = split_two(rest)
    return high, mid, low


def token_of(row, col, win):
    r = row + WIN * (win // 2) + SHIFT
    c = col + WIN * (win % 2) + SHIFT
    r = jnp.where(r >= SIDE, r - SIDE, r)
    c = jnp.where(c >= SIDE, c - SIDE, c)
    return r * SIDE + c


def padded_rows(win):
    i = iota((WPAD, 1), 0)
    col = jnp.bitwise_and(i, ROWP - 1)
    token = token_of(lax.shift_right_logical(i, 4), col, win)
    token = jnp.where(col < WIN, token, -1)
    return hot(token == iota((WPAD, TOK), 1))


def window_rows():
    i = iota((TOK, 1), 0)
    win = sum((i >= j * WTOK).astype(jnp.int32) for j in (1, 2, 3))
    place = i - WTOK * win
    row = div12(place)
    down, across = (win >= 2).astype(jnp.int32), win - 2 * (win >= 2).astype(jnp.int32)
    r = row + WIN * down + SHIFT
    c = place - WIN * row + WIN * across + SHIFT
    r = jnp.where(r >= SIDE, r - SIDE, r)
    c = jnp.where(c >= SIDE, c - SIDE, c)
    return hot(r * SIDE + c == iota((TOK, TOK), 1))


def token_rows():
    token = iota((TOK, 1), 0)
    row = lax.shift_right_logical(token * 2731, 16)
    col = token - row * SIDE
    row = jnp.where(row >= SHIFT, row - SHIFT, row + SIDE - SHIFT)
    col = jnp.where(col >= SHIFT, col - SHIFT, col + SIDE - SHIFT)
    wr, wc = (row >= WIN).astype(jnp.int32), (col >= WIN).astype(jnp.int32)
    at = (wr * 2 + wc) * WTOK + (row - WIN * wr) * WIN + col - WIN * wc
    return hot(at == iota((TOK, TOK), 1))


def pad_hot():
    j = iota((WPAD, WTOK), 1)
    return hot(iota((WPAD, WTOK), 0) == j + 4 * div12(j))


def pad_hot_t():
    j = iota((WTOK, WPAD), 0)
    return hot(iota((WTOK, WPAD), 1) == j + 4 * div12(j))


def stride_hot():
    lane = iota((1, TABS), 1)
    row, col = lax.shift_right_logical(lane, 5), jnp.bitwise_and(lane, 31)
    entry = jnp.where((col < 23) & (row < 23), row * 23 + col, -1)
    return hot(iota((TABL, TABS), 0) == entry)


def offset_hot():
    lane = iota((1, ZL), 1)
    cj = jnp.bitwise_and(lane, ROWP - 1)
    u = lax.shift_right_logical(lane, 4)
    entry = jnp.where((cj < WIN) & (u < 23), (22 - u) * 32 + 11 - cj, -1)
    return hot(iota((TABS, ZL), 0) == entry)


def mask_head(tile, lane0):
    lane = iota((1, 128), 1)
    return jnp.where((lane >= lane0) & (lane < lane0 + HEAD_DIM), tile, jnp.zeros_like(tile))


def norm_stats(values):
    center = values - jnp.mean(values, axis=-1, keepdims=True)
    spread = jnp.mean(center * center, axis=-1, keepdims=True)
    rs = lax.rsqrt(spread + NORM_EPS)
    return center * rs, rs


def norm_back(grad, gain, normal, rs):
    e = grad * gain
    return rs * (
        e
        - jnp.mean(e, axis=-1, keepdims=True)
        - normal * jnp.mean(e * normal, axis=-1, keepdims=True)
    )


def col_sum(v):
    return jnp.sum(v, axis=0, keepdims=True)


def main_kernel(
    img_in, cot_in, msk, wi_in, wo_in, wu_in, wd_in, nv_in, hb_in, ub_in, tab_in,
    ga_out, gu_out, gd_out, sm_out, bo_out, ig_out,
    G, GB, RBS, T1, R1, T2, R2, ZB, RZ,
    PB, ZT, QVK, MX, DS, DZ, LOW1, N1, RS1, XC, BR, N2H, RS2, N2, GL, ACT, GH, ACT1, GH1,
    G2P, G2S, G2R, OS, OR, GMID, GBP, ET, GONE, BO, IG,
    SMI, SMG, SMO, SMR, SMT, SMS, FULL, LOW1T, GBPT, BOT, OUTP, img, cot, w_in, w_out, w_up, w_dn, nv, hb, ub, tab, g_a, g_u, g_d,
    gs, gr, zs, zr, ms, mr, es, er, rs_s, rs_r, os_s, os_r, qs, qr, ls,
):
    def local(src, dst, j):
        return pltpu.make_async_copy(src, dst, ls.at[j])

    given = (
        (wi_in, w_in), (wo_in, w_out), (hb_in, hb), (ub_in, ub), (tab_in, tab), (img_in, img),
        (nv_in, nv), (wu_in, w_up), (wd_in, w_dn), (cot_in, cot),
    )
    for j, (src, dst) in enumerate(given):
        local(src, dst, j).start()

    def ready(*js):
        for j in js:
            local(*given[j], j).wait()
    d = lax.axis_index("dp")
    z = lax.axis_index("tensor")
    chip = d // 2
    c = d % 2
    chip_x = chip + 1 - 2 * (chip % 2)
    chip_y = (chip + 2) % 4
    chip_d = 3 - chip
    first = (1 - c) * chip_y + c * chip_x
    second = (1 - c) * chip_x + c * chip_y
    zx = [z, z + 1 - 2 * (z % 2), (z + 2) % 4, 3 - z]
    half = z // 2
    near = [z, zx[1], 2 - half, 3 - 3 * half]
    dev_s = (chip * 2 + 1 - c, z)
    dev_x = (chip_x * 2 + c, z)
    dev_y = (chip_y * 2 + c, z)
    dev_d = (chip_d * 2 + c, z)
    dev_1 = (first * 2 + c, z)
    dev_2 = (second * 2 + c, z)
    dev_z = [None] + [(d, zx[k]) for k in (1, 2, 3)]

    def copy(src, dst, ssem, rsem, dev):
        return pltpu.make_async_remote_copy(
            src_ref=src, dst_ref=dst, send_sem=ssem, recv_sem=rsem, device_id=dev, device_id_type=MESH
        )

    def send(src, dst, ssem, rsem, dev):
        copy(src, dst, ssem, rsem, dev).start()

    def got(dst, rsem):
        copy(dst, dst, rsem, rsem, dev_s).wait_recv()

    def sent(src, ssem):
        copy(src, src, ssem, ssem, dev_s).wait_send()

    def blocks_of(ref):
        return lambda block: ref.at[block]

    def own_items(block):
        return G.at[block, chip, c]

    dev_up = (d, (z + 1) % 4)
    dev_dn = (d, (z + 3) % 4)

    def line_send(buf, which, j, block, live_up, live_dn):
        def go(ok, side, dev):
            @pl.when(ok)
            def _():
                send(buf(block), buf(block), os_s.at[which, j, side], os_r.at[which, block], dev)

        go(live_up, 0, dev_up)
        go(live_dn, 1, dev_dn)

    def line_start(buf, which):
        line_send(buf, which, 0, z, z < 3, z > 0)

    def line_step(buf, which, j):
        below, above = (z + 4 - j) % 4, (z + j) % 4

        @pl.when(z >= j)
        def _():
            got(buf(below), os_r.at[which, below])

            @pl.when(z < 3)
            def _():
                send(buf(below), buf(below), os_s.at[which, j, 0], os_r.at[which, below], dev_up)

        @pl.when(z + j <= 3)
        def _():
            got(buf(above), os_r.at[which, above])

            @pl.when(z > 0)
            def _():
                send(buf(above), buf(above), os_s.at[which, j, 1], os_r.at[which, above], dev_dn)

    def line_drain(buf, which):
        for j in range(4):
            @pl.when((z >= j) & (z < 3))
            def _():
                sent(buf(0), os_s.at[which, j, 0])

            @pl.when((z + j <= 3) & (z > 0))
            def _():
                sent(buf(0), os_s.at[which, j, 1])

    def slot(k):
        return near[k] if k < 4 else k

    def s0(k):
        s = slot(k)
        if k in (6, 7):
            got(G.at[s, chip, c], zr.at[k])
        item = G.at[s, chip, c]
        send(item, item, gs.at[k, 0], gr.at[k, 0], dev_x)
        send(item, item, gs.at[k, 1], gr.at[k, 1], dev_y)
        send(item, item, gs.at[k, 3], gr.at[k, 3], dev_s)

    def s1(k):
        s = slot(k)
        got(G.at[s, chip_x, c], gr.at[k, 0])
        got(G.at[s, chip_y, c], gr.at[k, 1])
        item = G.at[s, second, c]
        send(item, item, gs.at[k, 2], gr.at[k, 2], dev_1)
        item = G.at[s, chip_x, c]
        send(item, item, gs.at[k, 4], gr.at[k, 4], dev_s)
        item = G.at[s, chip_y, c]
        send(item, item, gs.at[k, 5], gr.at[k, 5], dev_s)

    def s2(k):
        s = slot(k)
        got(G.at[s, chip_d, c], gr.at[k, 2])
        item = G.at[s, chip_d, c]
        send(item, item, gs.at[k, 6], gr.at[k, 6], dev_s)

    def s3(k):
        s = slot(k)
        for j, from_chip in ((3, chip), (4, chip_x), (5, chip_y), (6, chip_d)):
            got(G.at[s, from_chip, 1 - c], gr.at[k, j])

    def gather_step(t):
        if t == 0:
            line_start(own_items, 2)
        if 1 <= t <= 3:
            line_step(own_items, 2, t)
        if t in (3, 4):
            k = t + 3
            send(G.at[k - 2, chip, c], G.at[k, chip, c], zs.at[k], zr.at[k], dev_z[2])
        if t <= 7:
            s0(t)
        if 1 <= t <= 8:
            s1(t - 1)
        if 2 <= t <= 9:
            s2(t - 2)

    far = {2: 1, 3: 2, 4: 1}

    def r0(p):
        send(GB.at[p, :, 1 - c], RBS.at[p], rs_s.at[p, 0], rs_r.at[p, 0], dev_s)

    def r1(p):
        got(RBS.at[p], rs_r.at[p, 0])
        T1[p, 0] = (GB[p, chip_d, c].astype(F32) + RBS[p, chip_d].astype(F32)).astype(BF)
        send(T1.at[p, 0], R1.at[p, 0], rs_s.at[p, 1], rs_r.at[p, 1], dev_1)
        T1[p, 1] = (GB[p, first, c].astype(F32) + RBS[p, first].astype(F32)).astype(BF)
        send(T1.at[p, 1], R1.at[p, 1], rs_s.at[p, 4], rs_r.at[p, 4], dev_1)

    def r2(p):
        got(R1.at[p, 0], rs_r.at[p, 1])
        T2[p] = (
            GB[p, second, c].astype(F32) + RBS[p, second].astype(F32) + R1[p, 0].astype(F32)
        ).astype(BF)
        send(T2.at[p], R2.at[p], rs_s.at[p, 2], rs_r.at[p, 2], dev_2)

    def r3(p):
        got(R1.at[p, 1], rs_r.at[p, 4])
        got(R2.at[p], rs_r.at[p, 2])
        own = (
            GB[p, chip, c].astype(F32)
            + RBS[p, chip].astype(F32)
            + R1[p, 1].astype(F32)
            + R2[p].astype(F32)
        )
        if p == 3:
            got(RZ.at[2], rs_r.at[2, 3])
            own = own + RZ[2].astype(F32)
        if p in far:
            ZB[p] = own.astype(BF)
            send(ZB.at[p], RZ.at[p], rs_s.at[p, 3], rs_r.at[p, 3], dev_z[far[p]])
        elif p == 0:
            g_u[...] = own
        elif p == 1:
            g_d[...] = own
        else:
            g_a[...] = own

    def reduce(*steps):
        for step, p in steps:
            (r0, r1, r2, r3)[step](p)

    barrier = pltpu.get_barrier_semaphore()
    for dev in (dev_s, dev_x, dev_y, dev_d, dev_z[1], dev_z[2], dev_z[3]):
        pl.semaphore_signal(barrier, inc=1, device_id=dev, device_id_type=MESH)

    ready(0, 1)
    shard = jnp.concatenate([w_in[0], w_in[2], w_in[1], w_out[...].T], axis=1)
    G[z, chip, c] = shard.astype(BF)
    pl.semaphore_wait(barrier, 7)
    gather_step(0)

    SMI[...] = jnp.zeros_like(SMI)
    ready(2, 3, 4)
    SMI[0:HG, 0:529] = tab[...]
    SMI[6:7, 0:192] = hb[0:1, :]
    SMI[6:7, 192:384] = hb[1:2, :]
    SMI[7:8, :] = ub[...].reshape(1, FQ)
    for k in (1, 2, 3):
        send(SMI, SMG.at[z], ms.at[k], mr.at[k], dev_z[k])
    SMG[z] = SMI[...]

    ready(5, 6)
    xp = dot(padded_rows(z), img[...])
    normal, rs = norm_stats(xp)
    N1[...] = normal
    RS1[...] = rs
    LOW1[...] = (normal * nv[0:1, :] + nv[1:2, :]).astype(BF)
    ready(7, 8)
    G[4, chip, c] = w_up[...].astype(BF)
    G[5, chip, c] = w_dn[...].astype(BF)
    gather_step(1)
    ET[...] = pad_hot_t()
    LOW1T[...] = LOW1[...].T
    XC[...] = dot(ET[...], xp.astype(BF))
    BR[...] = jnp.zeros_like(BR)
    ZT[...] = jnp.zeros_like(ZT)
    DZ[...] = jnp.zeros_like(DZ)
    SMO[...] = jnp.zeros_like(SMO)

    for k in (1, 2, 3):
        got(SMG.at[zx[k]], mr.at[k])
    table = SMG[:, :, 0:TABL].reshape(32, TABL)
    stride = stride_hot()
    table = sum(dot(part, stride) for part in split_three(table))
    for ci in range(WIN):
        turned = table if ci == 0 else pltpu.roll(table, TABS - ci, 1)
        GB[ci // 8, ci % 8 // 2, ci % 2] = jnp.concatenate(split_three(turned), axis=0)
    offset = offset_hot()
    for first_ci, rows in ((0, GB[0].reshape(768, 768)), (8, GB[1, 0:2].reshape(384, 768))):
        spread = dot(rows, offset)
        for j in range(spread.shape[0] // SHARD):
            part = spread[j * SHARD : j * SHARD + SHARD]
            part = part[0:32] + part[32:64] + part[64:96]
            for t in range(3):
                ZT[t, pl.ds(first_ci + j, 32, stride=ROWP), :] = part[:, t * 128 : t * 128 + 128]

    qi = iota((WPAD, 1), 0)
    kj = iota((1, WPAD), 1)
    q_r, q_c = lax.shift_right_logical(qi, 4), jnp.bitwise_and(qi, ROWP - 1)
    k_r, k_c = lax.shift_right_logical(kj, 4), jnp.bitwise_and(kj, ROWP - 1)
    cut_r = ((q_r >= SHIFT) != (k_r >= SHIFT)) & (z // 2 == 1)
    cut_c = ((q_c >= SHIFT) != (k_c >= SHIFT)) & (z % 2 == 1)
    fill = jnp.where(cut_r | cut_c, FILL_VALUE, 0.0)
    GONE[:, 0:WPAD] = jnp.where(k_c < WIN, fill, -1e30)

    def bias_step(zz, carry):
        at = pl.ds(pl.multiple_of(zz * 8 * ROWP, 8 * ROWP), HG * ROWP)
        rows = jnp.concatenate([ZT[t, at, :] for t in range(3)], axis=1)
        for ri in range(WIN):
            left = (WIN - 1 - ri) * ROWP
            block = rows[:, left : left + WPAD].reshape(HG, ROWP, WPAD)
            fill = GONE[ri * ROWP : ri * ROWP + ROWP, 0:WPAD]
            PB[pl.ds(zz * HG, HG), ri * ROWP : ri * ROWP + ROWP, :] = block + fill[None]
        return carry

    lax.fori_loop(0, 4, bias_step, 0)
    GONE[...] = jnp.zeros_like(GONE)
    gather_step(2)

    def zk(k):
        return (z // 2 + k // 2) % 2 * 2 + (z % 2 + k % 2) % 2

    def near_of(k):
        across = (1 - half) * k + half * (3 - k)
        beside = z + (1 - 2 * (z % 2)) * k
        far_half = k // 2
        return far_half * across + (1 - far_half) * beside

    def group_forward(zz):
        whole = G[zz].reshape(768, 768)
        qvk = (dot(LOW1[...], whole) + SMG[zz, 6:7, :]).astype(BF)
        QVK[zz] = qvk
        mixed = [None, None]
        for e in range(HG):
            ta, la, tb, lb = e // 4, 32 * (e % 4), (e + 2) // 4, 32 * ((e + 2) % 4)
            q_t = qvk[:, ta * 128 : ta * 128 + 128]
            k_t = qvk[:, 384 + ta * 128 : 512 + ta * 128]
            v_t = qvk[:, 128 + tb * 128 : 256 + tb * 128]
            s = dot_nt(mask_head(q_t, la), k_t) * SCALE + PB[zz * HG + e]
            p = jnp.exp(s - jnp.max(s, axis=-1, keepdims=True))
            p = p * (1.0 / jnp.sum(p, axis=-1, keepdims=True))
            PB[zz * HG + e] = p
            add = dot(p.astype(BF), mask_head(v_t, lb))
            mixed[tb] = add if mixed[tb] is None else mixed[tb] + add
        mixed = jnp.concatenate(mixed, axis=1).astype(BF)
        MX[zz] = mixed
        BR[...] += dot_nt(dot(ET[...], mixed).astype(BF), whole[:, 512:768])

    def forward_step(k, carry):
        for j in range(4):
            @pl.when(k == j)
            def _():
                if j > 0:
                    gather_step(j + 2)
                s3(j)

        group_forward(near_of(k))
        return carry

    lax.fori_loop(0, 4, forward_step, 0)

    gather_step(6)
    normal, rs = norm_stats(XC[...] + BR[...] + nv[4:5, :])
    N2H[...] = normal
    RS2[...] = rs
    N2[z] = (normal * nv[2:3, :] + nv[3:4, :]).astype(BF)
    line_start(blocks_of(N2), 3)

    def ff_quarter(w, q, act, gh):
        zq = (z // 2 + q) % 2 * 2 + z % 2

        def ff_step(n, carry):
            at = pl.ds(pl.multiple_of(n * 256, 256), 256)
            up = G[4 + 2 * q, :, :, :, at].reshape(768, 256)
            down = G[5 + 2 * q, :, :, :, at].reshape(768, 256)
            u = dot(N2[w], up) + SMG[zq, 7:8, at]
            u2 = u * u
            th = jnp.tanh(0.7978845608028654 * (u + 0.044715 * (u2 * u)))
            half_up = 0.5 * (1.0 + th)
            act[:, at] = (u * half_up).astype(BF)
            slope = half_up + 0.5 * u * (1.0 - th * th) * (
                0.7978845608028654 * (1.0 + 3 * 0.044715 * u2)
            )
            gh[:, at] = (dot(GL[w], down) * slope).astype(BF)
            return carry

        lax.fori_loop(0, 3, ff_step, 0)

    def ff_own(w):
        ff_quarter(w, 0, ACT.at[w], GH.at[w])

    def ff_other(b):
        ff_quarter(zx[b], 1, ACT1.at[b], GH1.at[b])

    def ff_two(b):
        return dot_nt(GH[zx[b]], G[4].reshape(768, 768)) + dot_nt(GH1[b], G[6].reshape(768, 768))

    def ff_out(b):
        return dot_nt(ACT[zx[b]], G[5].reshape(768, 768)) + dot_nt(ACT1[b], G[7].reshape(768, 768))

    def ff_grad(p):
        left, right = (N2, GH) if p == 0 else (GL, ACT)

        def grad_step(j, carry):
            at = pl.ds(pl.multiple_of(j * 384, 384), 384)
            rows = left[:, :, at].reshape(TOK, 384)
            grad = dot_tn(rows, right[...].reshape(TOK, 768))
            GB[p, pl.ds(2 * j, 2)] = grad.astype(BF).reshape(2, 2, SHARD, 768)
            return carry

        lax.fori_loop(0, 2, grad_step, 0)

    ready(9)
    rows = dot(window_rows(), cot[...]) * msk[0].astype(F32)
    GL[...] = rows.astype(BF).reshape(4, WTOK, 768)
    gather_step(7)
    s3(4)
    s3(5)
    ff_own(z)
    line_step(blocks_of(N2), 3, 1)
    gather_step(8)
    ff_own(zx[1])
    gather_step(9)
    line_step(blocks_of(N2), 3, 2)
    s3(6)
    s3(7)
    ff_other(1)
    G2S[...] = ff_two(1).astype(BF)
    send(G2S, G2R, es.at[1], er.at[1], dev_z[1])
    ff_other(0)
    G2P[...] = ff_two(0)
    OS[...] = ff_out(1).astype(BF)
    send(OS, OR, es.at[2], er.at[2], dev_z[1])
    OUTP[...] = ff_out(0)
    line_step(blocks_of(N2), 3, 3)
    ff_own(zx[2])
    ff_own(zx[3])

    got(G2R, er.at[1])
    g2 = G2P[...] + G2R[...].astype(F32)
    g_out = GL[z].astype(F32)
    gain2 = col_sum(g2 * N2H[...])
    shift2 = col_sum(g2)
    g_mid = g_out + norm_back(g2, nv[2:3, :], N2H[...], RS2[...])
    GMID[...] = g_mid
    g_branch = g_mid.astype(BF)
    GBP[...] = dot(pad_hot(), g_branch).astype(BF)
    GBPT[...] = GBP[...].T
    bias_b = col_sum(g_branch.astype(F32))
    bias_o = col_sum(g_out)

    def group_backward(zz, p_at):
        whole = G[zz].reshape(768, 768)
        d_out = dot(GBP[...], whole[:, 512:768]).astype(BF)
        qvk = QVK[zz]
        dq, dk, dv = [None, None], [None, None], [None, None]

        def add(parts, t, v):
            parts[t] = v if parts[t] is None else parts[t] + v

        for e in range(HG):
            ta, la, tb, lb = e // 4, 32 * (e % 4), (e + 2) // 4, 32 * ((e + 2) % 4)
            q_t = qvk[:, ta * 128 : ta * 128 + 128]
            k_t = qvk[:, 384 + ta * 128 : 512 + ta * 128]
            v_t = qvk[:, 128 + tb * 128 : 256 + tb * 128]
            p = PB[zz * HG + e]
            d_o = mask_head(d_out[:, tb * 128 : tb * 128 + 128], lb)
            dp = dot_nt(d_o, v_t)
            add(dv, tb, dot_tn(p.astype(BF), d_o))
            ds = (p * (dp - jnp.sum(dp * p, axis=-1, keepdims=True))).astype(BF)
            DS[zz * HG + e] = ds
            add(dq, ta, dot(ds, mask_head(k_t, la)))
            add(dk, ta, dot_tn(ds, mask_head(q_t, la)))
        dq = [v * SCALE for v in dq]
        dk = [v * SCALE for v in dk]
        full = jnp.concatenate(
            [dq[0], dq[1] + dv[0], dv[1], dk[0], dk[1], jnp.zeros_like(dk[1])], axis=1
        ).astype(BF)
        GONE[...] += dot_nt(full[:, 0:640], whole[:, 0:640])
        SMO[zz, 6:7, :] = col_sum(full.astype(F32))
        FULL[...] = full

        def grad_step(j, carry):
            at = pl.ds(pl.multiple_of(j * 384, 384), 384)
            rows = LOW1T[at, :]
            main = dot(rows, FULL[:, 0:512])
            tail = dot(rows, FULL[:, 512:768]) + dot(GBPT[at, :], MX[zz])
            grad = jnp.concatenate([main, tail], axis=1).astype(BF)
            GB[p_at, pl.ds(2 * j, 2)] = grad.reshape(2, 2, SHARD, 768)
            return carry

        lax.fori_loop(0, 2, grad_step, 0)

    def block_rows():
        got(OR, er.at[2])
        out = OUTP[...] + OR[...].astype(F32) + nv[5:6, :]
        BO[z] = (XC[...] + BR[...] + nv[4:5, :] + out).astype(BF)
        line_start(blocks_of(BO), 0)

    def backward_step(i, carry):
        group_backward(zk(3 - i), 2 + i)
        for j in range(4):
            @pl.when(i == j)
            def _():
                if j == 0:
                    reduce((0, 2))
                    block_rows()
                if j == 1:
                    reduce((0, 3), (1, 2))
                if j == 2:
                    reduce((0, 4), (1, 3), (2, 2))
                    line_step(blocks_of(BO), 0, 1)
                if j == 3:
                    reduce((0, 5), (1, 4), (3, 2))
                    line_step(blocks_of(BO), 0, 2)
        return carry

    lax.fori_loop(0, 4, backward_step, 0)

    g_one = GONE[...]
    gain1 = col_sum(g_one * N1[...])
    shift1 = col_sum(g_one)
    back = norm_back(g_one, nv[0:1, :], N1[...], RS1[...])
    b_high, b_low = split_two(back)
    back = dot(ET[...], b_high) + dot(ET[...], b_low)
    IG[z] = (GMID[...] + back).astype(BF)
    line_start(blocks_of(IG), 1)

    def leave(w, ok):
        @pl.when(ok)
        def _():
            local(IG.at[w], ig_out.at[w], 14 + w).start()

    leave(z, z >= 0)
    reduce((2, 3), (1, 5))
    ff_grad(0)
    reduce((0, 0), (3, 3))
    ff_grad(1)
    reduce((0, 1), (1, 0), (2, 4))
    SMO[z, 8:9, :] = col_sum(GH[...].reshape(TOK, 768).astype(F32))
    def table_step(ri, carry):
        at = pl.ds(pl.multiple_of(ri * ROWP, ROWP), ROWP)
        pick = hot(iota((WPAD, ZL), 1) == iota((WPAD, ZL), 0) + (WIN - 1 - ri) * ROWP)
        sums = dot(DS[:, at, :].reshape(4 * HG * ROWP, WPAD), pick)
        for t in range(3):
            DZ[t] += sums[:, t * 128 : t * 128 + 128]
        return carry

    lax.fori_loop(0, WIN, table_step, 0)
    rows = [
        jnp.concatenate([DZ[t, pl.ds(ci, 4 * HG, stride=ROWP), :] for t in range(3)], axis=1)
        for ci in range(WIN)
    ]
    offset = offset_hot()
    sums = sum(dot_nt(part, offset) for part in split_two(jnp.concatenate(rows, axis=0)))
    total = sums[0 : 4 * HG]
    for ci in range(1, WIN):
        total = total + pltpu.roll(sums[ci * 4 * HG : (ci + 1) * 4 * HG], ci, 1)
    stride = stride_hot()
    total = sum(dot_nt(part, stride) for part in split_two(total))
    for zz in range(4):
        SMO[zz, 0:HG, 0:TABL] = total[zz * HG : zz * HG + HG]
        for j, row in enumerate((gain1, shift1, gain2, shift2, bias_b, bias_o)):
            SMO[zz, 9 + j : 10 + j, :] = row
    for k in (1, 2, 3):
        send(SMO.at[zx[k]], SMR.at[k], qs.at[k], qr.at[k], dev_z[k])
    line_step(blocks_of(IG), 1, 1)
    leave((z + 4 - 1) % 4, z >= 1)
    leave((z + 1) % 4, z + 1 <= 3)
    reduce((1, 1), (3, 4), (2, 5))
    line_step(blocks_of(BO), 0, 3)
    BOT[...] = dot(token_rows(), BO[...].reshape(TOK, 768)).astype(BF)
    local(BOT, bo_out, 10).start()
    small = SMO[z]
    for k in (1, 2, 3):
        got(SMR.at[k], qr.at[k])
        small = small + SMR[k]
    SMT[0] = small
    send(SMT.at[0], SMS.at[0], qs.at[4], qr.at[4], dev_s)
    reduce((2, 0), (3, 5))
    got(SMS.at[0], qr.at[4])
    small = small + SMS[0]
    SMT[1] = small
    for j, dev in enumerate((dev_x, dev_y, dev_d)):
        send(SMT.at[1], SMS.at[1 + j], qs.at[5 + j], qr.at[5 + j], dev)
    line_step(blocks_of(IG), 1, 2)
    leave((z + 4 - 2) % 4, z >= 2)
    leave((z + 2) % 4, z + 2 <= 3)
    reduce((2, 1), (3, 0))
    local(g_u, gu_out, 11).start()
    for j in range(3):
        got(SMS.at[1 + j], qr.at[5 + j])
        small = small + SMS[1 + j]
    sm_out[...] = small
    reduce((3, 1))
    local(g_d, gd_out, 12).start()

    for p in (3, 4):
        got(RZ.at[p], rs_r.at[p, 3])
    g_a[...] += RZ[3].astype(F32) + RZ[4].astype(F32)
    local(g_a, ga_out, 13).start()
    line_step(blocks_of(IG), 1, 3)
    leave((z + 4 - 3) % 4, z >= 3)
    leave((z + 3) % 4, z + 3 <= 3)

    item = G.at[0, 0, 0]
    for k in (1, 2, 3):
        sent(SMI, ms.at[k])
        sent(SMO.at[0], qs.at[k])
        sent(SMO.at[0], qs.at[4 + k])
    sent(item, zs.at[6])
    sent(item, zs.at[7])
    line_drain(blocks_of(N2), 3)
    sent(G2S, es.at[1])
    sent(OS, es.at[2])
    sent(SMO.at[0], qs.at[4])
    line_drain(blocks_of(BO), 0)
    line_drain(blocks_of(IG), 1)
    line_drain(own_items, 2)
    for k in range(8):
        for j in range(7):
            sent(item, gs.at[k, j])
    for p in range(6):
        sent(RBS.at[p], rs_s.at[p, 0])
        sent(T1.at[p, 0], rs_s.at[p, 1])
        sent(T1.at[p, 1], rs_s.at[p, 4])
        sent(T2.at[p], rs_s.at[p, 2])
    for p in far:
        sent(ZB.at[p], rs_s.at[p, 3])
    for w in range(4):
        local(IG.at[w], ig_out.at[w], 14 + w).wait()
    for j, (src, dst) in enumerate(((BOT, bo_out), (g_u, gu_out), (g_d, gd_out), (g_a, ga_out))):
        local(src, dst, 10 + j).wait()


def vm(shape, dtype=F32):
    return pltpu.VMEM(shape, dtype)


def main_call(args):
    f32 = lambda *s: jax.ShapeDtypeStruct(s, F32)
    bf = lambda *s: jax.ShapeDtypeStruct(s, BF)
    dma = lambda *s: pltpu.SemaphoreType.DMA(s)
    vspec = pl.BlockSpec(memory_space=pltpu.VMEM)
    hbm = pl.BlockSpec(memory_space=pl.ANY)
    specs = [hbm] * len(args)
    specs[2] = pl.BlockSpec(memory_space=pltpu.SMEM)
    scratch = [
        vm((8, 4, 2, SHARD, 768), BF),
        vm((6, 4, 2, SHARD, 768), BF),
        vm((6, 4, SHARD, 768), BF),
        vm((6, 2, SHARD, 768), BF),
        vm((6, 2, SHARD, 768), BF),
        vm((6, SHARD, 768), BF),
        vm((6, SHARD, 768), BF),
        vm((6, SHARD, 768), BF),
        vm((6, SHARD, 768), BF),
        vm((4 * HG, WPAD, WPAD)),
        vm((3, 32 * ROWP, 128)),
        vm((4, WPAD, 768), BF),
        vm((4, WPAD, 256), BF),
        vm((4 * HG, WPAD, WPAD), BF),
        vm((3, 4 * HG * ROWP, 128)),
        vm((WPAD, 768), BF),
        vm((WPAD, 768)),
        vm((WPAD, 1)),
        vm((WTOK, 768)),
        vm((WTOK, 768)),
        vm((WTOK, 768)),
        vm((WTOK, 1)),
        vm((4, WTOK, 768), BF),
        vm((4, WTOK, 768), BF),
        vm((4, WTOK, FQ), BF),
        vm((4, WTOK, FQ), BF),
        vm((2, WTOK, FQ), BF),
        vm((2, WTOK, FQ), BF),
        vm((WTOK, 768)),
        vm((WTOK, 768), BF),
        vm((WTOK, 768), BF),
        vm((WTOK, 768), BF),
        vm((WTOK, 768), BF),
        vm((WTOK, 768)),
        vm((WPAD, 768), BF),
        vm((WTOK, WPAD), BF),
        vm((WPAD, 768)),
        vm((4, WTOK, 768), BF),
        vm((4, WTOK, 768), BF),
        vm((8, 768)),
        vm((4, 8, 768)),
        vm((4, 16, 768)),
        vm((4, 16, 768)),
        vm((2, 16, 768)),
        vm((4, 16, 768)),
        vm((WPAD, 768), BF),
        vm((768, WPAD), BF),
        vm((768, WPAD), BF),
        vm((TOK, 768), BF),
        vm((WTOK, 768)),
        vm((TOK, 768), BF),
        vm((TOK, 768), BF),
        vm((3, SHARD, 192)),
        vm((192, SHARD)),
        vm((SHARD, 768)),
        vm((SHARD, 768)),
        vm((6, 768)),
        vm((2, 192)),
        vm((FQ,)),
        vm((HG, 529)),
        vm((SHARD, 768)),
        vm((SHARD, 768)),
        vm((SHARD, 768)),
        dma(8, 7), dma(8, 7),
        dma(8), dma(8),
        dma(4), dma(4),
        dma(3), dma(3),
        dma(6, 5), dma(6, 5),
        dma(4, 4, 2), dma(4, 4),
        dma(8), dma(8),
        dma(18),
    ]
    return pl.pallas_call(
        main_kernel,
        out_shape=(
            f32(SHARD, 768), f32(SHARD, 768), f32(SHARD, 768), f32(16, 768),
            bf(TOK, 768), bf(4, WTOK, 768),
        ),
        in_specs=specs,
        out_specs=tuple([hbm] * 3 + [vspec] + [hbm] * 2),
        scratch_shapes=scratch,
        compiler_params=pltpu.CompilerParams(
            collective_id=0, has_side_effects=True, vmem_limit_bytes=62 * 2**20
        ),
        cost_estimate=pl.CostEstimate(flops=7 * 10**9, bytes_accessed=10**7, transcendentals=10**6),
    )(*args)


def last_kernel(n_in, n_out, *refs):
    given, made = refs[:n_in], refs[n_in : n_in + n_out]
    held = refs[n_in + n_out : 2 * n_in + n_out]
    done = refs[2 * n_in + n_out : 2 * (n_in + n_out)]
    in_sem, out_sem = refs[2 * (n_in + n_out) :]
    g_a, g_u, g_d, sm, bo, ig = range(6)

    def load(j):
        return pltpu.make_async_copy(given[j], held[j], in_sem.at[j])

    def store(j):
        return pltpu.make_async_copy(done[j], made[j], out_sem.at[j])

    order = [ig, bo, g_u, 12, 13, 14, g_d, 15, 16, 17, g_a, 6, 7, 8, 9, 10, 11, sm] + list(range(18, 30))
    for j in order:
        load(j).start()

    def wait(*js):
        for j in js:
            load(j).wait()

    back = token_rows()
    wait(ig)
    done[1][0] = dot(back, held[ig][...].reshape(TOK, 768))
    store(1).start()
    wait(bo)
    pltpu.make_async_copy(held[bo], made[0].at[0], out_sem.at[0]).start()

    def adam(param, out, at, grad, low, vector=False):
        w, f, s = (held[param + j][at] for j in range(3))
        rate, decay = (RATE_VECTOR, 0.0) if vector else (RATE_MATRIX, DECAY_MATRIX)
        moment, square, updated = adam_update(w, f, s, grad, rate, decay)
        done[out][at], done[out + 1][at], done[out + 2][at] = moment, square, updated
        if low:
            done[out + 3][at] = updated.astype(BF)

    def finish(out, count):
        for j in range(out, out + count):
            store(j).start()

    whole = slice(None)
    wait(g_u, 12, 13, 14)
    adam(12, 10, whole, held[g_u][...], True)
    finish(10, 4)
    wait(g_d, 15, 16, 17)
    adam(15, 14, whole, held[g_d][...], True)
    finish(14, 4)
    wait(g_a, 6, 7, 8)
    for j, lane in ((0, 0), (1, 384), (2, 192)):
        adam(6, 2, j, held[g_a][:, lane : lane + 192], True)
    finish(2, 4)
    eye = jnp.where(iota((SHARD, SHARD), 0) == iota((SHARD, SHARD), 1), 1.0, 0.0)
    turned = lax.dot_general(
        held[g_a][:, 576:768], eye, (((0,), (0,)), ((), ())),
        precision=lax.Precision.HIGHEST, preferred_element_type=F32,
    )
    wait(9, 10, 11)
    adam(9, 6, whole, turned, True)
    finish(6, 4)
    small = held[sm]
    wait(sm, *range(18, 30))
    adam(18, 18, whole, small[9:15, :], False, True)
    for j in (0, 1):
        adam(21, 21, slice(j, j + 1), small[6:7, 192 * j : 192 * j + 192], False, True)
    adam(24, 24, whole, small[8:9, :].reshape(FQ), False, True)
    adam(27, 27, whole, small[0:HG, 0:529], False, True)
    finish(18, 12)
    pltpu.make_async_copy(held[bo], made[0].at[0], out_sem.at[0]).wait()
    for j in range(1, n_out):
        store(j).wait()


def last_call(sums, params):
    hbm = pl.BlockSpec(memory_space=pl.ANY)
    like = lambda a, t=F32: jax.ShapeDtypeStruct(a.shape, t)
    outs = [jax.ShapeDtypeStruct((1, TOK, 768), BF), jax.ShapeDtypeStruct((1, TOK, 768), F32)]
    for j in range(0, 12, 3):
        outs += [like(params[j])] * 3 + [like(params[j], BF)]
    for j in range(12, 24, 3):
        outs += [like(params[j])] * 3
    ins = list(sums) + list(params)
    return pl.pallas_call(
        functools.partial(last_kernel, len(ins), len(outs)),
        out_shape=tuple(outs),
        in_specs=[hbm] * len(ins),
        out_specs=tuple([hbm] * len(outs)),
        scratch_shapes=[vm(a.shape, a.dtype) for a in ins + outs]
        + [pltpu.SemaphoreType.DMA((len(ins),)), pltpu.SemaphoreType.DMA((len(outs),))],
        compiler_params=pltpu.CompilerParams(vmem_limit_bytes=62 * 2**20),
        cost_estimate=pl.CostEstimate(flops=10**9, bytes_accessed=15 * 10**6, transcendentals=10**6),
    )(*ins)


def on_device_windows(images, cotangent, image_mask, *params):
    params = list(params)
    turned = (9, 10, 11, 21, 22, 23)
    for j in turned:
        params[j] = params[j].T
    (in_w, _, _, out_w, _, _, up_w, _, _, dn_w, _, _, nv, _, _, hb, _, _, ub, _, _, tab, _, _) = params
    sums = main_call(
        (
            images.reshape(TOK, D), cotangent.reshape(TOK, D), image_mask,
            in_w, out_w, up_w, dn_w, nv, hb, ub, tab,
        )
    )
    outs = list(last_call(sums, params))
    for j in (14, 15, 16, 17, 27, 28, 29):
        outs[j] = outs[j].T
    return tuple(outs)


def solution(mesh):
    shape = mesh.shape
    windows = shape["dp"] == 8 and shape["tensor"] == 4
    return jax.shard_map(
        on_device_windows if windows else on_device,
        mesh=mesh,
        in_specs=(
            P("dp", None, None),
            P("dp", None, None),
            P("dp"),
            P(None, "dp", "tensor"),
            P(None, "dp", "tensor"),
            P(None, "dp", "tensor"),
            P("tensor", "dp"),
            P("tensor", "dp"),
            P("tensor", "dp"),
            P("dp", "tensor"),
            P("dp", "tensor"),
            P("dp", "tensor"),
            P("tensor", "dp"),
            P("tensor", "dp"),
            P("tensor", "dp"),
            P(),
            P(),
            P(),
            P(None, "tensor"),
            P(None, "tensor"),
            P(None, "tensor"),
            P("tensor"),
            P("tensor"),
            P("tensor"),
            P(None, "tensor"),
            P(None, "tensor"),
            P(None, "tensor"),
        ),
        out_specs=(
            P("dp", None, None),
            P("dp", None, None),
            P(None, "dp", "tensor"),
            P(None, "dp", "tensor"),
            P(None, "dp", "tensor"),
            P(None, "dp", "tensor"),
            P("tensor", "dp"),
            P("tensor", "dp"),
            P("tensor", "dp"),
            P("tensor", "dp"),
            P("dp", "tensor"),
            P("dp", "tensor"),
            P("dp", "tensor"),
            P("dp", "tensor"),
            P("tensor", "dp"),
            P("tensor", "dp"),
            P("tensor", "dp"),
            P("tensor", "dp"),
            P(),
            P(),
            P(),
            P(None, "tensor"),
            P(None, "tensor"),
            P(None, "tensor"),
            P("tensor"),
            P("tensor"),
            P("tensor"),
            P(None, "tensor"),
            P(None, "tensor"),
            P(None, "tensor"),
        ),
        check_vma=False,
    )
```

```python
import functools
from functools import partial

import jax
import jax.numpy as jnp
from jax import lax
from jax.experimental import pallas as pl
from jax.experimental.pallas import tpu as pltpu
from jax.sharding import PartitionSpec as P

D = 768
HEAD_DIM = 32
WIN = 12
SIDE = 24
STEP = 7
SHIFT = 6


NORM_EPS = 1e-05
FILL_VALUE = -100.0
BETA_ONE = 0.5
BETA_TWO = 0.5
ADAM_EPS = 1e-08
RATE_MATRIX = 0.05
RATE_VECTOR = 0.3
DECAY_MATRIX = 0.05


def layer_norm(values, gain_in, offset_in):
    center = values - jnp.mean(values, axis=-1, keepdims=True)
    spread = jnp.mean(center * center, axis=-1, keepdims=True)
    return center * lax.rsqrt(spread + NORM_EPS) * gain_in + offset_in


def adam_update(weight, first_old, second_old, gradient, rate_of, decay_of):
    moment = BETA_ONE * first_old + (1.0 - BETA_ONE) * gradient
    square = BETA_TWO * second_old + (1.0 - BETA_TWO) * gradient * gradient
    moment_fix = moment / (1.0 - BETA_ONE**STEP)
    square_fix = square / (1.0 - BETA_TWO**STEP)
    updated = weight * (1.0 - rate_of * decay_of) - rate_of * moment_fix / (
        jnp.sqrt(square_fix) + ADAM_EPS
    )
    return (moment, square, updated)


def dot_plain(left_side, right_side):
    return jnp.dot(left_side, right_side, preferred_element_type=jnp.float32)


def dot_back(left_side, right_side):
    return lax.dot_general(
        left_side, right_side, (((1,), (1,)), ((), ())), preferred_element_type=jnp.float32
    )


def dot_rows(left_side, right_side):
    return lax.dot_general(
        left_side, right_side, (((0,), (0,)), ((), ())), preferred_element_type=jnp.float32
    )


def to_heads(token_rows, images_here, heads_here):
    blocks = SIDE // WIN
    grid_view = token_rows.reshape(images_here, SIDE, SIDE, heads_here * HEAD_DIM)
    grid_view = jnp.roll(grid_view, (-SHIFT, -SHIFT), (1, 2))
    grid_view = grid_view.reshape(
        images_here, blocks, WIN, blocks, WIN, heads_here, HEAD_DIM
    ).transpose(0, 1, 3, 2, 4, 5, 6)
    return grid_view.reshape(images_here, blocks * blocks, WIN * WIN, heads_here, HEAD_DIM)


def from_heads(windows, images_here):
    blocks = SIDE // WIN
    channels = windows.shape[3] * windows.shape[4]
    grid_view = windows.reshape(images_here, blocks, blocks, WIN, WIN, channels).transpose(
        0, 1, 3, 2, 4, 5
    )
    grid_view = jnp.roll(
        grid_view.reshape(images_here, SIDE, SIDE, channels), (SHIFT, SHIFT), (1, 2)
    )
    return grid_view.reshape(images_here * SIDE * SIDE, channels)


def window_fill():
    blocks = SIDE // WIN
    cell_ids = jnp.arange(SIDE, dtype=jnp.int32)
    band_of = (cell_ids >= SIDE - WIN).astype(jnp.int32) + (cell_ids >= SIDE - SHIFT).astype(
        jnp.int32
    )
    region = band_of[:, None] * 3 + band_of[None, :]
    labels = (
        region.reshape(blocks, WIN, blocks, WIN)
        .transpose(0, 2, 1, 3)
        .reshape(blocks * blocks, WIN * WIN)
    )
    return jnp.where(labels[:, :, None] != labels[:, None, :], FILL_VALUE, 0.0).astype(jnp.float32)


def offset_onehot():
    places = jnp.arange(WIN, dtype=jnp.int32)
    spans = jnp.arange(2 * WIN - 1, dtype=jnp.int32)
    return (places[:, None, None] - places[None, :, None] + WIN - 1 == spans[None, None, :]).astype(
        jnp.float32
    )


def window_scores(query_win, key_win, bias_add, fill_add):
    scores = jnp.einsum(
        "inqhd,inkhd->inhqk", query_win, key_win, preferred_element_type=jnp.float32
    ) * HEAD_DIM ** (-0.5)
    return scores + bias_add[None, None] + fill_add[None, :, None]


def on_device(
    images,
    cotangent,
    image_mask,
    in_weight,
    in_first,
    in_second,
    out_weight,
    out_first,
    out_second,
    up_weight,
    up_first,
    up_second,
    down_weight,
    down_first,
    down_second,
    norm_vector,
    norm_first,
    norm_second,
    head_bias,
    head_first,
    head_second,
    up_bias,
    bias_first,
    bias_second,
    position_table,
    table_first,
    table_second,
):
    lowtype = jnp.bfloat16
    highest = lax.Precision.HIGHEST
    whole_in, whole_out, whole_up, whole_down = (
        lax.all_gather(in_weight.astype(lowtype), "dp", axis=1, tiled=True),
        lax.all_gather(out_weight.astype(lowtype), "dp", axis=1, tiled=True),
        lax.all_gather(up_weight.astype(lowtype), "dp", axis=0, tiled=True),
        lax.all_gather(down_weight.astype(lowtype), "dp", axis=1, tiled=True),
    )
    images_here = images.shape[0]
    heads_here = whole_in.shape[2] // HEAD_DIM
    span_count = 2 * WIN - 1
    token_rows = images.reshape(-1, D).astype(jnp.float32)
    normed_one, norm_one_back = jax.vjp(layer_norm, token_rows, norm_vector[0], norm_vector[1])
    low_one = normed_one.astype(lowtype)
    query_rows = (dot_plain(low_one, whole_in[0]) + head_bias[0]).astype(lowtype)
    key_rows = dot_plain(low_one, whole_in[1]).astype(lowtype)
    value_rows = (dot_plain(low_one, whole_in[2]) + head_bias[1]).astype(lowtype)
    query_win = to_heads(query_rows, images_here, heads_here)
    key_win = to_heads(key_rows, images_here, heads_here)
    value_win = to_heads(value_rows, images_here, heads_here)
    onehot = offset_onehot()
    table_view = position_table.reshape(span_count, span_count, heads_here)
    bias_add = jnp.einsum(
        "xya,zwb,abh->hxzyw", onehot, onehot, table_view, precision=highest
    ).reshape(heads_here, WIN * WIN, WIN * WIN)
    fill_add = window_fill()
    scores = window_scores(query_win, key_win, bias_add, fill_add)
    row_top = jnp.max(scores, axis=-1, keepdims=True)
    weights_raw = jnp.exp(scores - row_top)
    row_total = jnp.sum(weights_raw, axis=-1, keepdims=True)
    log_total = row_top + jnp.log(row_total)
    prob_low = (weights_raw / row_total).astype(lowtype)
    mixed_win = jnp.einsum(
        "inhqk,inkhd->inqhd", prob_low, value_win, preferred_element_type=jnp.float32
    ).astype(lowtype)
    mixed_rows = from_heads(mixed_win, images_here)
    branch_share = lax.psum_scatter(
        dot_plain(mixed_rows, whole_out), "tensor", scatter_dimension=0, tiled=True
    )
    branch = lax.all_gather(branch_share, "tensor", axis=0, tiled=True) + norm_vector[4]
    middle = token_rows + branch
    normed_two, norm_two_back = jax.vjp(layer_norm, middle, norm_vector[2], norm_vector[3])
    low_two = normed_two.astype(lowtype)
    hidden = dot_plain(low_two, whole_up) + up_bias
    active, gelu_back = jax.vjp(partial(jax.nn.gelu, approximate=True), hidden)
    active_low = active.astype(lowtype)
    output_share = lax.psum_scatter(
        dot_plain(active_low, whole_down).astype(jnp.bfloat16),
        "tensor",
        scatter_dimension=0,
        tiled=True,
    ).astype(jnp.float32)
    output = (
        lax.all_gather(output_share.astype(jnp.bfloat16), "tensor", axis=0, tiled=True).astype(
            output_share.dtype
        )
        + norm_vector[5]
    )
    block_out = (middle + output).astype(lowtype).reshape(images.shape)
    keep_rows = jnp.repeat(image_mask.astype(jnp.float32), SIDE * SIDE)[:, None]
    grad_out = cotangent.reshape(-1, D).astype(jnp.float32) * keep_rows
    grad_low = grad_out.astype(lowtype)
    down_grad = dot_rows(active_low, grad_low)
    grad_hidden = gelu_back(dot_back(grad_low, whole_down))[0].astype(lowtype)
    up_grad = dot_rows(low_two, grad_hidden)
    bias_grad = jnp.sum(grad_hidden.astype(jnp.float32), axis=0)
    two_share = lax.psum_scatter(
        dot_back(grad_hidden, whole_up), "tensor", scatter_dimension=0, tiled=True
    )
    grad_two = lax.all_gather(two_share, "tensor", axis=0, tiled=True)
    grad_norm_two, gain_two, offset_two = norm_two_back(grad_two)
    grad_middle = grad_out + grad_norm_two
    grad_branch = grad_middle.astype(lowtype)
    out_grad = dot_rows(mixed_rows, grad_branch)
    grad_mixed = dot_back(grad_branch, whole_out).astype(lowtype)
    grad_win = to_heads(grad_mixed, images_here, heads_here)
    scores_again = window_scores(query_win, key_win, bias_add, fill_add)
    probs = jnp.exp(scores_again - log_total)
    grad_probs = jnp.einsum(
        "inqhd,inkhd->inhqk", grad_win, value_win, preferred_element_type=jnp.float32
    )
    grad_value = jnp.einsum(
        "inhqk,inqhd->inkhd", probs.astype(lowtype), grad_win, preferred_element_type=jnp.float32
    ).astype(lowtype)
    grad_scores = (
        probs * (grad_probs - jnp.sum(grad_probs * probs, axis=-1, keepdims=True))
    ).astype(lowtype)
    grad_query = (
        jnp.einsum("inhqk,inkhd->inqhd", grad_scores, key_win, preferred_element_type=jnp.float32)
        * HEAD_DIM ** (-0.5)
    ).astype(lowtype)
    grad_key = (
        jnp.einsum("inhqk,inqhd->inkhd", grad_scores, query_win, preferred_element_type=jnp.float32)
        * HEAD_DIM ** (-0.5)
    ).astype(lowtype)
    score_sums = jnp.sum(grad_scores.astype(jnp.float32), axis=(0, 1)).reshape(
        heads_here, WIN, WIN, WIN, WIN
    )
    table_grad = jnp.einsum(
        "xya,zwb,hxzyw->abh", onehot, onehot, score_sums, precision=highest
    ).reshape(span_count * span_count, heads_here)
    query_back = from_heads(grad_query, images_here)
    key_back = from_heads(grad_key, images_here)
    value_back = from_heads(grad_value, images_here)
    in_grad = jnp.stack(
        [dot_rows(low_one, query_back), dot_rows(low_one, key_back), dot_rows(low_one, value_back)]
    )
    head_grad = jnp.stack(
        [
            jnp.sum(query_back.astype(jnp.float32), axis=0),
            jnp.sum(value_back.astype(jnp.float32), axis=0),
        ]
    )
    grad_one_terms = (
        dot_back(query_back, whole_in[0])
        + dot_back(key_back, whole_in[1])
        + dot_back(value_back, whole_in[2])
    )
    one_share = lax.psum_scatter(
        grad_one_terms.astype(jnp.bfloat16), "tensor", scatter_dimension=0, tiled=True
    ).astype(jnp.float32)
    grad_one = lax.all_gather(one_share.astype(jnp.bfloat16), "tensor", axis=0, tiled=True).astype(
        one_share.dtype
    )
    grad_norm_one, gain_one, offset_one = norm_one_back(grad_one)
    image_grad = (grad_middle + grad_norm_one).reshape(images.shape)
    norm_grad = jnp.stack(
        [
            gain_one,
            offset_one,
            gain_two,
            offset_two,
            jnp.sum(grad_branch.astype(jnp.float32), axis=0),
            jnp.sum(grad_low.astype(jnp.float32), axis=0),
        ]
    )
    summed = lax.psum(
        (in_grad, out_grad, up_grad, down_grad, norm_grad, head_grad, bias_grad, table_grad), "dp"
    )
    position = lax.axis_index("dp")
    in_total = lax.dynamic_slice_in_dim(
        summed[0], position * in_weight.shape[1], in_weight.shape[1], 1
    )
    out_total = lax.dynamic_slice_in_dim(
        summed[1], position * out_weight.shape[1], out_weight.shape[1], 1
    )
    up_total = lax.dynamic_slice_in_dim(
        summed[2], position * up_weight.shape[0], up_weight.shape[0], 0
    )
    down_total = lax.dynamic_slice_in_dim(
        summed[3], position * down_weight.shape[1], down_weight.shape[1], 1
    )
    norm_total, head_total, bias_total, table_total = (summed[4], summed[5], summed[6], summed[7])
    in_moment, in_square, in_updated = adam_update(
        in_weight, in_first, in_second, in_total, RATE_MATRIX, DECAY_MATRIX
    )
    out_moment, out_square, out_updated = adam_update(
        out_weight, out_first, out_second, out_total, RATE_MATRIX, DECAY_MATRIX
    )
    up_moment, up_square, up_updated = adam_update(
        up_weight, up_first, up_second, up_total, RATE_MATRIX, DECAY_MATRIX
    )
    down_moment, down_square, down_updated = adam_update(
        down_weight, down_first, down_second, down_total, RATE_MATRIX, DECAY_MATRIX
    )
    norm_moment, norm_square, norm_updated = adam_update(
        norm_vector, norm_first, norm_second, norm_total, RATE_VECTOR, 0.0
    )
    head_moment, head_square, head_updated = adam_update(
        head_bias, head_first, head_second, head_total, RATE_VECTOR, 0.0
    )
    bias_moment, bias_square, bias_updated = adam_update(
        up_bias, bias_first, bias_second, bias_total, RATE_VECTOR, 0.0
    )
    table_moment, table_square, table_updated = adam_update(
        position_table, table_first, table_second, table_total, RATE_VECTOR, 0.0
    )
    return (
        block_out,
        image_grad,
        in_moment,
        in_square,
        in_updated,
        in_updated.astype(lowtype),
        out_moment,
        out_square,
        out_updated,
        out_updated.astype(lowtype),
        up_moment,
        up_square,
        up_updated,
        up_updated.astype(lowtype),
        down_moment,
        down_square,
        down_updated,
        down_updated.astype(lowtype),
        norm_moment,
        norm_square,
        norm_updated,
        head_moment,
        head_square,
        head_updated,
        bias_moment,
        bias_square,
        bias_updated,
        table_moment,
        table_square,
        table_updated,
    )


MESH = pl.DeviceIdType.MESH
TOK = SIDE * SIDE
WTOK = WIN * WIN
ROWP = 16
WPAD = WIN * ROWP
FQ = 768
SHARD = 96
HG = 6
TABL = 640
TABS = 768
ZL = 384
SCALE = HEAD_DIM ** (-0.5)
F32 = jnp.float32
BF = jnp.bfloat16


def dot(a, b):
    return lax.dot_general(a, b, (((1,), (0,)), ((), ())), preferred_element_type=F32)


def dot_nt(a, b):
    return lax.dot_general(a, b, (((1,), (1,)), ((), ())), preferred_element_type=F32)


def dot_tn(a, b):
    return lax.dot_general(a, b, (((0,), (0,)), ((), ())), preferred_element_type=F32)


def iota(shape, axis):
    return lax.broadcasted_iota(jnp.int32, shape, axis)


def div12(i):
    return lax.shift_right_logical(i * 171, 11)


def hot(condition):
    return jnp.where(condition, 1.0, 0.0).astype(BF)


def split_two(v):
    high = v.astype(BF)
    return high, (v - high.astype(F32)).astype(BF)


def split_three(v):
    high, _ = split_two(v)
    rest = v - high.astype(F32)
    mid, low = split_two(rest)
    return high, mid, low


def token_of(row, col, win):
    r = row + WIN * (win // 2) + SHIFT
    c = col + WIN * (win % 2) + SHIFT
    r = jnp.where(r >= SIDE, r - SIDE, r)
    c = jnp.where(c >= SIDE, c - SIDE, c)
    return r * SIDE + c


def padded_rows(win):
    i = iota((WPAD, 1), 0)
    col = jnp.bitwise_and(i, ROWP - 1)
    token = token_of(lax.shift_right_logical(i, 4), col, win)
    token = jnp.where(col < WIN, token, -1)
    return hot(token == iota((WPAD, TOK), 1))


def window_rows():
    i = iota((TOK, 1), 0)
    win = sum((i >= j * WTOK).astype(jnp.int32) for j in (1, 2, 3))
    place = i - WTOK * win
    row = div12(place)
    down, across = (win >= 2).astype(jnp.int32), win - 2 * (win >= 2).astype(jnp.int32)
    r = row + WIN * down + SHIFT
    c = place - WIN * row + WIN * across + SHIFT
    r = jnp.where(r >= SIDE, r - SIDE, r)
    c = jnp.where(c >= SIDE, c - SIDE, c)
    return hot(r * SIDE + c == iota((TOK, TOK), 1))


def token_rows():
    token = iota((TOK, 1), 0)
    row = lax.shift_right_logical(token * 2731, 16)
    col = token - row * SIDE
    row = jnp.where(row >= SHIFT, row - SHIFT, row + SIDE - SHIFT)
    col = jnp.where(col >= SHIFT, col - SHIFT, col + SIDE - SHIFT)
    wr, wc = (row >= WIN).astype(jnp.int32), (col >= WIN).astype(jnp.int32)
    at = (wr * 2 + wc) * WTOK + (row - WIN * wr) * WIN + col - WIN * wc
    return hot(at == iota((TOK, TOK), 1))


def pad_hot():
    j = iota((WPAD, WTOK), 1)
    return hot(iota((WPAD, WTOK), 0) == j + 4 * div12(j))


def pad_hot_t():
    j = iota((WTOK, WPAD), 0)
    return hot(iota((WTOK, WPAD), 1) == j + 4 * div12(j))


def stride_hot():
    lane = iota((1, TABS), 1)
    row, col = lax.shift_right_logical(lane, 5), jnp.bitwise_and(lane, 31)
    entry = jnp.where((col < 23) & (row < 23), row * 23 + col, -1)
    return hot(iota((TABL, TABS), 0) == entry)


def offset_hot():
    lane = iota((1, ZL), 1)
    cj = jnp.bitwise_and(lane, ROWP - 1)
    u = lax.shift_right_logical(lane, 4)
    entry = jnp.where((cj < WIN) & (u < 23), (22 - u) * 32 + 11 - cj, -1)
    return hot(iota((TABS, ZL), 0) == entry)


def mask_head(tile, lane0):
    lane = iota((1, 128), 1)
    return jnp.where((lane >= lane0) & (lane < lane0 + HEAD_DIM), tile, jnp.zeros_like(tile))


def norm_stats(values):
    center = values - jnp.mean(values, axis=-1, keepdims=True)
    spread = jnp.mean(center * center, axis=-1, keepdims=True)
    rs = lax.rsqrt(spread + NORM_EPS)
    return center * rs, rs


def norm_back(grad, gain, normal, rs):
    e = grad * gain
    return rs * (
        e
        - jnp.mean(e, axis=-1, keepdims=True)
        - normal * jnp.mean(e * normal, axis=-1, keepdims=True)
    )


def col_sum(v):
    return jnp.sum(v, axis=0, keepdims=True)


def main_kernel(
    img_in, cot_in, msk, wi_in, wo_in, wu_in, wd_in, nv_in, hb_in, ub_in, tab_in,
    ga_out, gu_out, gd_out, sm_out, bo_out, ig_out,
    G, GB, RBS, T1, R1, T2, R2, ZB, RZ,
    PB, ZT, QVK, MX, DS, DZ, LOW1, N1, RS1, XC, BR, N2H, RS2, N2, GL, ACT, GH, ACT1, GH1,
    G2P, G2S, G2R, OS, OR, GMID, GBP, ET, GONE, BO, IG,
    SMI, SMG, SMO, SMR, SMT, SMS, FULL, LOW1T, GBPT, BOT, OUTP, img, cot, w_in, w_out, w_up, w_dn, nv, hb, ub, tab, g_a, g_u, g_d,
    gs, gr, zs, zr, ms, mr, es, er, rs_s, rs_r, os_s, os_r, qs, qr, ls,
):
    def local(src, dst, j):
        return pltpu.make_async_copy(src, dst, ls.at[j])

    given = (
        (wi_in, w_in), (wo_in, w_out), (hb_in, hb), (ub_in, ub), (tab_in, tab), (img_in, img),
        (nv_in, nv), (wu_in, w_up), (wd_in, w_dn), (cot_in, cot),
    )
    for j, (src, dst) in enumerate(given):
        local(src, dst, j).start()

    def ready(*js):
        for j in js:
            local(*given[j], j).wait()
    d = lax.axis_index("dp")
    z = lax.axis_index("tensor")
    chip = d // 2
    c = d % 2
    chip_x = chip + 1 - 2 * (chip % 2)
    chip_y = (chip + 2) % 4
    chip_d = 3 - chip
    first = (1 - c) * chip_y + c * chip_x
    second = (1 - c) * chip_x + c * chip_y
    zx = [z, z + 1 - 2 * (z % 2), (z + 2) % 4, 3 - z]
    half = z // 2
    near = [z, zx[1], 2 - half, 3 - 3 * half]
    dev_s = (chip * 2 + 1 - c, z)
    dev_x = (chip_x * 2 + c, z)
    dev_y = (chip_y * 2 + c, z)
    dev_d = (chip_d * 2 + c, z)
    dev_1 = (first * 2 + c, z)
    dev_2 = (second * 2 + c, z)
    dev_z = [None] + [(d, zx[k]) for k in (1, 2, 3)]

    def copy(src, dst, ssem, rsem, dev):
        return pltpu.make_async_remote_copy(
            src_ref=src, dst_ref=dst, send_sem=ssem, recv_sem=rsem, device_id=dev, device_id_type=MESH
        )

    def send(src, dst, ssem, rsem, dev):
        copy(src, dst, ssem, rsem, dev).start()

    def got(dst, rsem):
        copy(dst, dst, rsem, rsem, dev_s).wait_recv()

    def sent(src, ssem):
        copy(src, src, ssem, ssem, dev_s).wait_send()

    def blocks_of(ref):
        return lambda block: ref.at[block]

    def own_items(block):
        return G.at[block, chip, c]

    dev_up = (d, (z + 1) % 4)
    dev_dn = (d, (z + 3) % 4)

    def line_send(buf, which, j, block, live_up, live_dn):
        def go(ok, side, dev):
            @pl.when(ok)
            def _():
                send(buf(block), buf(block), os_s.at[which, j, side], os_r.at[which, block], dev)

        go(live_up, 0, dev_up)
        go(live_dn, 1, dev_dn)

    def line_start(buf, which):
        line_send(buf, which, 0, z, z < 3, z > 0)

    def line_step(buf, which, j):
        below, above = (z + 4 - j) % 4, (z + j) % 4

        @pl.when(z >= j)
        def _():
            got(buf(below), os_r.at[which, below])

            @pl.when(z < 3)
            def _():
                send(buf(below), buf(below), os_s.at[which, j, 0], os_r.at[which, below], dev_up)

        @pl.when(z + j <= 3)
        def _():
            got(buf(above), os_r.at[which, above])

            @pl.when(z > 0)
            def _():
                send(buf(above), buf(above), os_s.at[which, j, 1], os_r.at[which, above], dev_dn)

    def line_drain(buf, which):
        for j in range(4):
            @pl.when((z >= j) & (z < 3))
            def _():
                sent(buf(0), os_s.at[which, j, 0])

            @pl.when((z + j <= 3) & (z > 0))
            def _():
                sent(buf(0), os_s.at[which, j, 1])

    def slot(k):
        return near[k] if k < 4 else k

    def s0(k):
        s = slot(k)
        if k in (6, 7):
            got(G.at[s, chip, c], zr.at[k])
        item = G.at[s, chip, c]
        send(item, item, gs.at[k, 0], gr.at[k, 0], dev_x)
        send(item, item, gs.at[k, 1], gr.at[k, 1], dev_y)
        send(item, item, gs.at[k, 3], gr.at[k, 3], dev_s)

    def s1(k):
        s = slot(k)
        got(G.at[s, chip_x, c], gr.at[k, 0])
        got(G.at[s, chip_y, c], gr.at[k, 1])
        item = G.at[s, second, c]
        send(item, item, gs.at[k, 2], gr.at[k, 2], dev_1)
        item = G.at[s, chip_x, c]
        send(item, item, gs.at[k, 4], gr.at[k, 4], dev_s)
        item = G.at[s, chip_y, c]
        send(item, item, gs.at[k, 5], gr.at[k, 5], dev_s)

    def s2(k):
        s = slot(k)
        got(G.at[s, chip_d, c], gr.at[k, 2])
        item = G.at[s, chip_d, c]
        send(item, item, gs.at[k, 6], gr.at[k, 6], dev_s)

    def s3(k):
        s = slot(k)
        for j, from_chip in ((3, chip), (4, chip_x), (5, chip_y), (6, chip_d)):
            got(G.at[s, from_chip, 1 - c], gr.at[k, j])

    def gather_step(t):
        if t == 0:
            line_start(own_items, 2)
        if 1 <= t <= 3:
            line_step(own_items, 2, t)
        if t in (3, 4):
            k = t + 3
            send(G.at[k - 2, chip, c], G.at[k, chip, c], zs.at[k], zr.at[k], dev_z[2])
        if t <= 7:
            s0(t)
        if 1 <= t <= 8:
            s1(t - 1)
        if 2 <= t <= 9:
            s2(t - 2)

    far = {2: 1, 3: 2, 4: 1}

    def r0(p):
        send(GB.at[p, :, 1 - c], RBS.at[p], rs_s.at[p, 0], rs_r.at[p, 0], dev_s)

    def r1(p):
        got(RBS.at[p], rs_r.at[p, 0])
        T1[p, 0] = (GB[p, chip_d, c].astype(F32) + RBS[p, chip_d].astype(F32)).astype(BF)
        send(T1.at[p, 0], R1.at[p, 0], rs_s.at[p, 1], rs_r.at[p, 1], dev_1)
        T1[p, 1] = (GB[p, first, c].astype(F32) + RBS[p, first].astype(F32)).astype(BF)
        send(T1.at[p, 1], R1.at[p, 1], rs_s.at[p, 4], rs_r.at[p, 4], dev_1)

    def r2(p):
        got(R1.at[p, 0], rs_r.at[p, 1])
        T2[p] = (
            GB[p, second, c].astype(F32) + RBS[p, second].astype(F32) + R1[p, 0].astype(F32)
        ).astype(BF)
        send(T2.at[p], R2.at[p], rs_s.at[p, 2], rs_r.at[p, 2], dev_2)

    def r3(p):
        got(R1.at[p, 1], rs_r.at[p, 4])
        got(R2.at[p], rs_r.at[p, 2])
        own = (
            GB[p, chip, c].astype(F32)
            + RBS[p, chip].astype(F32)
            + R1[p, 1].astype(F32)
            + R2[p].astype(F32)
        )
        if p == 3:
            got(RZ.at[2], rs_r.at[2, 3])
            own = own + RZ[2].astype(F32)
        if p in far:
            ZB[p] = own.astype(BF)
            send(ZB.at[p], RZ.at[p], rs_s.at[p, 3], rs_r.at[p, 3], dev_z[far[p]])
        elif p == 0:
            g_u[...] = own
        elif p == 1:
            g_d[...] = own
        else:
            g_a[...] = own

    def reduce(*steps):
        for step, p in steps:
            (r0, r1, r2, r3)[step](p)

    barrier = pltpu.get_barrier_semaphore()
    for dev in (dev_s, dev_x, dev_y, dev_d, dev_z[1], dev_z[2], dev_z[3]):
        pl.semaphore_signal(barrier, inc=1, device_id=dev, device_id_type=MESH)

    ready(0, 1)
    shard = jnp.concatenate([w_in[0], w_in[2], w_in[1], w_out[...].T], axis=1)
    G[z, chip, c] = shard.astype(BF)
    pl.semaphore_wait(barrier, 7)
    gather_step(0)

    SMI[...] = jnp.zeros_like(SMI)
    ready(2, 3, 4)
    SMI[0:HG, 0:529] = tab[...]
    SMI[6:7, 0:192] = hb[0:1, :]
    SMI[6:7, 192:384] = hb[1:2, :]
    SMI[7:8, :] = ub[...].reshape(1, FQ)
    for k in (1, 2, 3):
        send(SMI, SMG.at[z], ms.at[k], mr.at[k], dev_z[k])
    SMG[z] = SMI[...]

    ready(5, 6)
    xp = dot(padded_rows(z), img[...])
    normal, rs = norm_stats(xp)
    N1[...] = normal
    RS1[...] = rs
    LOW1[...] = (normal * nv[0:1, :] + nv[1:2, :]).astype(BF)
    ready(7, 8)
    G[4, chip, c] = w_up[...].astype(BF)
    G[5, chip, c] = w_dn[...].astype(BF)
    gather_step(1)
    ET[...] = pad_hot_t()
    LOW1T[...] = LOW1[...].T
    XC[...] = dot(ET[...], xp.astype(BF))
    BR[...] = jnp.zeros_like(BR)
    ZT[...] = jnp.zeros_like(ZT)
    DZ[...] = jnp.zeros_like(DZ)
    SMO[...] = jnp.zeros_like(SMO)

    for k in (1, 2, 3):
        got(SMG.at[zx[k]], mr.at[k])
    table = SMG[:, :, 0:TABL].reshape(32, TABL)
    stride = stride_hot()
    table = sum(dot(part, stride) for part in split_three(table))
    for ci in range(WIN):
        turned = table if ci == 0 else pltpu.roll(table, TABS - ci, 1)
        GB[ci // 8, ci % 8 // 2, ci % 2] = jnp.concatenate(split_three(turned), axis=0)
    offset = offset_hot()
    for first_ci, rows in ((0, GB[0].reshape(768, 768)), (8, GB[1, 0:2].reshape(384, 768))):
        spread = dot(rows, offset)
        for j in range(spread.shape[0] // SHARD):
            part = spread[j * SHARD : j * SHARD + SHARD]
            part = part[0:32] + part[32:64] + part[64:96]
            for t in range(3):
                ZT[t, pl.ds(first_ci + j, 32, stride=ROWP), :] = part[:, t * 128 : t * 128 + 128]

    qi = iota((WPAD, 1), 0)
    kj = iota((1, WPAD), 1)
    q_r, q_c = lax.shift_right_logical(qi, 4), jnp.bitwise_and(qi, ROWP - 1)
    k_r, k_c = lax.shift_right_logical(kj, 4), jnp.bitwise_and(kj, ROWP - 1)
    cut_r = ((q_r >= SHIFT) != (k_r >= SHIFT)) & (z // 2 == 1)
    cut_c = ((q_c >= SHIFT) != (k_c >= SHIFT)) & (z % 2 == 1)
    fill = jnp.where(cut_r | cut_c, FILL_VALUE, 0.0)
    GONE[:, 0:WPAD] = jnp.where(k_c < WIN, fill, -1e30)

    def bias_step(zz, carry):
        at = pl.ds(pl.multiple_of(zz * 8 * ROWP, 8 * ROWP), HG * ROWP)
        rows = jnp.concatenate([ZT[t, at, :] for t in range(3)], axis=1)
        for ri in range(WIN):
            left = (WIN - 1 - ri) * ROWP
            block = rows[:, left : left + WPAD].reshape(HG, ROWP, WPAD)
            fill = GONE[ri * ROWP : ri * ROWP + ROWP, 0:WPAD]
            PB[pl.ds(zz * HG, HG), ri * ROWP : ri * ROWP + ROWP, :] = block + fill[None]
        return carry

    lax.fori_loop(0, 4, bias_step, 0)
    GONE[...] = jnp.zeros_like(GONE)
    gather_step(2)

    def zk(k):
        return (z // 2 + k // 2) % 2 * 2 + (z % 2 + k % 2) % 2

    def near_of(k):
        across = (1 - half) * k + half * (3 - k)
        beside = z + (1 - 2 * (z % 2)) * k
        far_half = k // 2
        return far_half * across + (1 - far_half) * beside

    def group_forward(zz):
        whole = G[zz].reshape(768, 768)
        qvk = (dot(LOW1[...], whole) + SMG[zz, 6:7, :]).astype(BF)
        QVK[zz] = qvk
        mixed = [None, None]
        for e in range(HG):
            ta, la, tb, lb = e // 4, 32 * (e % 4), (e + 2) // 4, 32 * ((e + 2) % 4)
            q_t = qvk[:, ta * 128 : ta * 128 + 128]
            k_t = qvk[:, 384 + ta * 128 : 512 + ta * 128]
            v_t = qvk[:, 128 + tb * 128 : 256 + tb * 128]
            s = dot_nt(mask_head(q_t, la), k_t) * SCALE + PB[zz * HG + e]
            p = jnp.exp(s - jnp.max(s, axis=-1, keepdims=True))
            p = p * (1.0 / jnp.sum(p, axis=-1, keepdims=True))
            PB[zz * HG + e] = p
            add = dot(p.astype(BF), mask_head(v_t, lb))
            mixed[tb] = add if mixed[tb] is None else mixed[tb] + add
        mixed = jnp.concatenate(mixed, axis=1).astype(BF)
        MX[zz] = mixed
        BR[...] += dot_nt(dot(ET[...], mixed).astype(BF), whole[:, 512:768])

    def forward_step(k, carry):
        for j in range(4):
            @pl.when(k == j)
            def _():
                if j > 0:
                    gather_step(j + 2)
                s3(j)

        group_forward(near_of(k))
        return carry

    lax.fori_loop(0, 4, forward_step, 0)

    gather_step(6)
    normal, rs = norm_stats(XC[...] + BR[...] + nv[4:5, :])
    N2H[...] = normal
    RS2[...] = rs
    N2[z] = (normal * nv[2:3, :] + nv[3:4, :]).astype(BF)
    line_start(blocks_of(N2), 3)

    def ff_quarter(w, q, act, gh):
        zq = (z // 2 + q) % 2 * 2 + z % 2

        def ff_step(n, carry):
            at = pl.ds(pl.multiple_of(n * 256, 256), 256)
            up = G[4 + 2 * q, :, :, :, at].reshape(768, 256)
            down = G[5 + 2 * q, :, :, :, at].reshape(768, 256)
            u = dot(N2[w], up) + SMG[zq, 7:8, at]
            u2 = u * u
            th = jnp.tanh(0.7978845608028654 * (u + 0.044715 * (u2 * u)))
            half_up = 0.5 * (1.0 + th)
            act[:, at] = (u * half_up).astype(BF)
            slope = half_up + 0.5 * u * (1.0 - th * th) * (
                0.7978845608028654 * (1.0 + 3 * 0.044715 * u2)
            )
            gh[:, at] = (dot(GL[w], down) * slope).astype(BF)
            return carry

        lax.fori_loop(0, 3, ff_step, 0)

    def ff_own(w):
        ff_quarter(w, 0, ACT.at[w], GH.at[w])

    def ff_other(b):
        ff_quarter(zx[b], 1, ACT1.at[b], GH1.at[b])

    def ff_two(b):
        return dot_nt(GH[zx[b]], G[4].reshape(768, 768)) + dot_nt(GH1[b], G[6].reshape(768, 768))

    def ff_out(b):
        return dot_nt(ACT[zx[b]], G[5].reshape(768, 768)) + dot_nt(ACT1[b], G[7].reshape(768, 768))

    def ff_grad(p):
        left, right = (N2, GH) if p == 0 else (GL, ACT)

        def grad_step(j, carry):
            at = pl.ds(pl.multiple_of(j * 384, 384), 384)
            rows = left[:, :, at].reshape(TOK, 384)
            grad = dot_tn(rows, right[...].reshape(TOK, 768))
            GB[p, pl.ds(2 * j, 2)] = grad.astype(BF).reshape(2, 2, SHARD, 768)
            return carry

        lax.fori_loop(0, 2, grad_step, 0)

    ready(9)
    rows = dot(window_rows(), cot[...]) * msk[0].astype(F32)
    GL[...] = rows.astype(BF).reshape(4, WTOK, 768)
    gather_step(7)
    s3(4)
    s3(5)
    ff_own(z)
    line_step(blocks_of(N2), 3, 1)
    gather_step(8)
    ff_own(zx[1])
    gather_step(9)
    line_step(blocks_of(N2), 3, 2)
    s3(6)
    s3(7)
    ff_other(1)
    G2S[...] = ff_two(1).astype(BF)
    send(G2S, G2R, es.at[1], er.at[1], dev_z[1])
    ff_other(0)
    G2P[...] = ff_two(0)
    OS[...] = ff_out(1).astype(BF)
    send(OS, OR, es.at[2], er.at[2], dev_z[1])
    OUTP[...] = ff_out(0)
    line_step(blocks_of(N2), 3, 3)
    ff_own(zx[2])
    ff_own(zx[3])

    got(G2R, er.at[1])
    g2 = G2P[...] + G2R[...].astype(F32)
    g_out = GL[z].astype(F32)
    gain2 = col_sum(g2 * N2H[...])
    shift2 = col_sum(g2)
    g_mid = g_out + norm_back(g2, nv[2:3, :], N2H[...], RS2[...])
    GMID[...] = g_mid
    g_branch = g_mid.astype(BF)
    GBP[...] = dot(pad_hot(), g_branch).astype(BF)
    GBPT[...] = GBP[...].T
    bias_b = col_sum(g_branch.astype(F32))
    bias_o = col_sum(g_out)

    def group_backward(zz, p_at):
        whole = G[zz].reshape(768, 768)
        d_out = dot(GBP[...], whole[:, 512:768]).astype(BF)
        qvk = QVK[zz]
        dq, dk, dv = [None, None], [None, None], [None, None]

        def add(parts, t, v):
            parts[t] = v if parts[t] is None else parts[t] + v

        for e in range(HG):
            ta, la, tb, lb = e // 4, 32 * (e % 4), (e + 2) // 4, 32 * ((e + 2) % 4)
            q_t = qvk[:, ta * 128 : ta * 128 + 128]
            k_t = qvk[:, 384 + ta * 128 : 512 + ta * 128]
            v_t = qvk[:, 128 + tb * 128 : 256 + tb * 128]
            p = PB[zz * HG + e]
            d_o = mask_head(d_out[:, tb * 128 : tb * 128 + 128], lb)
            dp = dot_nt(d_o, v_t)
            add(dv, tb, dot_tn(p.astype(BF), d_o))
            ds = (p * (dp - jnp.sum(dp * p, axis=-1, keepdims=True))).astype(BF)
            DS[zz * HG + e] = ds
            add(dq, ta, dot(ds, mask_head(k_t, la)))
            add(dk, ta, dot_tn(ds, mask_head(q_t, la)))
        dq = [v * SCALE for v in dq]
        dk = [v * SCALE for v in dk]
        full = jnp.concatenate(
            [dq[0], dq[1] + dv[0], dv[1], dk[0], dk[1], jnp.zeros_like(dk[1])], axis=1
        ).astype(BF)
        GONE[...] += dot_nt(full[:, 0:640], whole[:, 0:640])
        SMO[zz, 6:7, :] = col_sum(full.astype(F32))
        FULL[...] = full

        def grad_step(j, carry):
            at = pl.ds(pl.multiple_of(j * 384, 384), 384)
            rows = LOW1T[at, :]
            main = dot(rows, FULL[:, 0:512])
            tail = dot(rows, FULL[:, 512:768]) + dot(GBPT[at, :], MX[zz])
            grad = jnp.concatenate([main, tail], axis=1).astype(BF)
            GB[p_at, pl.ds(2 * j, 2)] = grad.reshape(2, 2, SHARD, 768)
            return carry

        lax.fori_loop(0, 2, grad_step, 0)

    def block_rows():
        got(OR, er.at[2])
        out = OUTP[...] + OR[...].astype(F32) + nv[5:6, :]
        BO[z] = (XC[...] + BR[...] + nv[4:5, :] + out).astype(BF)
        line_start(blocks_of(BO), 0)

    def backward_step(i, carry):
        group_backward(zk(3 - i), 2 + i)
        for j in range(4):
            @pl.when(i == j)
            def _():
                if j == 0:
                    reduce((0, 2))
                    block_rows()
                if j == 1:
                    reduce((0, 3), (1, 2))
                if j == 2:
                    reduce((0, 4), (1, 3), (2, 2))
                    line_step(blocks_of(BO), 0, 1)
                if j == 3:
                    reduce((0, 5), (1, 4), (3, 2))
                    line_step(blocks_of(BO), 0, 2)
        return carry

    lax.fori_loop(0, 4, backward_step, 0)

    g_one = GONE[...]
    gain1 = col_sum(g_one * N1[...])
    shift1 = col_sum(g_one)
    back = norm_back(g_one, nv[0:1, :], N1[...], RS1[...])
    b_high, b_low = split_two(back)
    back = dot(ET[...], b_high) + dot(ET[...], b_low)
    IG[z] = (GMID[...] + back).astype(BF)
    line_start(blocks_of(IG), 1)

    def leave(w, ok):
        @pl.when(ok)
        def _():
            local(IG.at[w], ig_out.at[w], 14 + w).start()

    leave(z, z >= 0)
    reduce((2, 3), (1, 5))
    ff_grad(0)
    reduce((0, 0), (3, 3))
    ff_grad(1)
    reduce((0, 1), (1, 0), (2, 4))
    SMO[z, 8:9, :] = col_sum(GH[...].reshape(TOK, 768).astype(F32))
    def table_step(ri, carry):
        at = pl.ds(pl.multiple_of(ri * ROWP, ROWP), ROWP)
        pick = hot(iota((WPAD, ZL), 1) == iota((WPAD, ZL), 0) + (WIN - 1 - ri) * ROWP)
        sums = dot(DS[:, at, :].reshape(4 * HG * ROWP, WPAD), pick)
        for t in range(3):
            DZ[t] += sums[:, t * 128 : t * 128 + 128]
        return carry

    line_step(blocks_of(IG), 1, 1)
    leave((z + 4 - 1) % 4, z >= 1)
    leave((z + 1) % 4, z + 1 <= 3)
    lax.fori_loop(0, WIN, table_step, 0)
    rows = [
        jnp.concatenate([DZ[t, pl.ds(ci, 4 * HG, stride=ROWP), :] for t in range(3)], axis=1)
        for ci in range(WIN)
    ]
    offset = offset_hot()
    sums = sum(dot_nt(part, offset) for part in split_two(jnp.concatenate(rows, axis=0)))
    total = sums[0 : 4 * HG]
    for ci in range(1, WIN):
        total = total + pltpu.roll(sums[ci * 4 * HG : (ci + 1) * 4 * HG], ci, 1)
    stride = stride_hot()
    total = sum(dot_nt(part, stride) for part in split_two(total))
    for zz in range(4):
        SMO[zz, 0:HG, 0:TABL] = total[zz * HG : zz * HG + HG]
        for j, row in enumerate((gain1, shift1, gain2, shift2, bias_b, bias_o)):
            SMO[zz, 9 + j : 10 + j, :] = row
    for k in (1, 2, 3):
        send(SMO.at[zx[k]], SMR.at[k], qs.at[k], qr.at[k], dev_z[k])
    reduce((1, 1), (3, 4), (2, 5))
    line_step(blocks_of(BO), 0, 3)
    BOT[...] = dot(token_rows(), BO[...].reshape(TOK, 768)).astype(BF)
    local(BOT, bo_out, 10).start()
    small = SMO[z]
    for k in (1, 2, 3):
        got(SMR.at[k], qr.at[k])
        small = small + SMR[k]
    SMT[0] = small
    send(SMT.at[0], SMS.at[0], qs.at[4], qr.at[4], dev_s)
    reduce((2, 0), (3, 5))
    got(SMS.at[0], qr.at[4])
    small = small + SMS[0]
    SMT[1] = small
    for j, dev in enumerate((dev_x, dev_y, dev_d)):
        send(SMT.at[1], SMS.at[1 + j], qs.at[5 + j], qr.at[5 + j], dev)
    line_step(blocks_of(IG), 1, 2)
    leave((z + 4 - 2) % 4, z >= 2)
    leave((z + 2) % 4, z + 2 <= 3)
    reduce((2, 1), (3, 0))
    local(g_u, gu_out, 11).start()
    for j in range(3):
        got(SMS.at[1 + j], qr.at[5 + j])
        small = small + SMS[1 + j]
    sm_out[...] = small
    reduce((3, 1))
    local(g_d, gd_out, 12).start()

    for p in (3, 4):
        got(RZ.at[p], rs_r.at[p, 3])
    g_a[...] += RZ[3].astype(F32) + RZ[4].astype(F32)
    local(g_a, ga_out, 13).start()
    line_step(blocks_of(IG), 1, 3)
    leave((z + 4 - 3) % 4, z >= 3)
    leave((z + 3) % 4, z + 3 <= 3)

    item = G.at[0, 0, 0]
    for k in (1, 2, 3):
        sent(SMI, ms.at[k])
        sent(SMO.at[0], qs.at[k])
        sent(SMO.at[0], qs.at[4 + k])
    sent(item, zs.at[6])
    sent(item, zs.at[7])
    line_drain(blocks_of(N2), 3)
    sent(G2S, es.at[1])
    sent(OS, es.at[2])
    sent(SMO.at[0], qs.at[4])
    line_drain(blocks_of(BO), 0)
    line_drain(blocks_of(IG), 1)
    line_drain(own_items, 2)
    for k in range(8):
        for j in range(7):
            sent(item, gs.at[k, j])
    for p in range(6):
        sent(RBS.at[p], rs_s.at[p, 0])
        sent(T1.at[p, 0], rs_s.at[p, 1])
        sent(T1.at[p, 1], rs_s.at[p, 4])
        sent(T2.at[p], rs_s.at[p, 2])
    for p in far:
        sent(ZB.at[p], rs_s.at[p, 3])
    for w in range(4):
        local(IG.at[w], ig_out.at[w], 14 + w).wait()
    for j, (src, dst) in enumerate(((BOT, bo_out), (g_u, gu_out), (g_d, gd_out), (g_a, ga_out))):
        local(src, dst, 10 + j).wait()


def vm(shape, dtype=F32):
    return pltpu.VMEM(shape, dtype)


def main_call(args):
    f32 = lambda *s: jax.ShapeDtypeStruct(s, F32)
    bf = lambda *s: jax.ShapeDtypeStruct(s, BF)
    dma = lambda *s: pltpu.SemaphoreType.DMA(s)
    vspec = pl.BlockSpec(memory_space=pltpu.VMEM)
    hbm = pl.BlockSpec(memory_space=pl.ANY)
    specs = [hbm] * len(args)
    specs[2] = pl.BlockSpec(memory_space=pltpu.SMEM)
    scratch = [
        vm((8, 4, 2, SHARD, 768), BF),
        vm((6, 4, 2, SHARD, 768), BF),
        vm((6, 4, SHARD, 768), BF),
        vm((6, 2, SHARD, 768), BF),
        vm((6, 2, SHARD, 768), BF),
        vm((6, SHARD, 768), BF),
        vm((6, SHARD, 768), BF),
        vm((6, SHARD, 768), BF),
        vm((6, SHARD, 768), BF),
        vm((4 * HG, WPAD, WPAD)),
        vm((3, 32 * ROWP, 128)),
        vm((4, WPAD, 768), BF),
        vm((4, WPAD, 256), BF),
        vm((4 * HG, WPAD, WPAD), BF),
        vm((3, 4 * HG * ROWP, 128)),
        vm((WPAD, 768), BF),
        vm((WPAD, 768)),
        vm((WPAD, 1)),
        vm((WTOK, 768)),
        vm((WTOK, 768)),
        vm((WTOK, 768)),
        vm((WTOK, 1)),
        vm((4, WTOK, 768), BF),
        vm((4, WTOK, 768), BF),
        vm((4, WTOK, FQ), BF),
        vm((4, WTOK, FQ), BF),
        vm((2, WTOK, FQ), BF),
        vm((2, WTOK, FQ), BF),
        vm((WTOK, 768)),
        vm((WTOK, 768), BF),
        vm((WTOK, 768), BF),
        vm((WTOK, 768), BF),
        vm((WTOK, 768), BF),
        vm((WTOK, 768)),
        vm((WPAD, 768), BF),
        vm((WTOK, WPAD), BF),
        vm((WPAD, 768)),
        vm((4, WTOK, 768), BF),
        vm((4, WTOK, 768), BF),
        vm((8, 768)),
        vm((4, 8, 768)),
        vm((4, 16, 768)),
        vm((4, 16, 768)),
        vm((2, 16, 768)),
        vm((4, 16, 768)),
        vm((WPAD, 768), BF),
        vm((768, WPAD), BF),
        vm((768, WPAD), BF),
        vm((TOK, 768), BF),
        vm((WTOK, 768)),
        vm((TOK, 768), BF),
        vm((TOK, 768), BF),
        vm((3, SHARD, 192)),
        vm((192, SHARD)),
        vm((SHARD, 768)),
        vm((SHARD, 768)),
        vm((6, 768)),
        vm((2, 192)),
        vm((FQ,)),
        vm((HG, 529)),
        vm((SHARD, 768)),
        vm((SHARD, 768)),
        vm((SHARD, 768)),
        dma(8, 7), dma(8, 7),
        dma(8), dma(8),
        dma(4), dma(4),
        dma(3), dma(3),
        dma(6, 5), dma(6, 5),
        dma(4, 4, 2), dma(4, 4),
        dma(8), dma(8),
        dma(18),
    ]
    return pl.pallas_call(
        main_kernel,
        out_shape=(
            f32(SHARD, 768), f32(SHARD, 768), f32(SHARD, 768), f32(16, 768),
            bf(TOK, 768), bf(4, WTOK, 768),
        ),
        in_specs=specs,
        out_specs=tuple([hbm] * 3 + [vspec] + [hbm] * 2),
        scratch_shapes=scratch,
        compiler_params=pltpu.CompilerParams(
            collective_id=0, has_side_effects=True, vmem_limit_bytes=62 * 2**20
        ),
        cost_estimate=pl.CostEstimate(flops=7 * 10**9, bytes_accessed=10**7, transcendentals=10**6),
    )(*args)


def last_kernel(n_in, n_out, *refs):
    given, made = refs[:n_in], refs[n_in : n_in + n_out]
    held = refs[n_in + n_out : 2 * n_in + n_out]
    done = refs[2 * n_in + n_out : 2 * (n_in + n_out)]
    in_sem, out_sem = refs[2 * (n_in + n_out) :]
    g_a, g_u, g_d, sm, bo, ig = range(6)

    def load(j):
        return pltpu.make_async_copy(given[j], held[j], in_sem.at[j])

    def store(j):
        return pltpu.make_async_copy(done[j], made[j], out_sem.at[j])

    order = [ig, bo, g_u, 12, 13, 14, g_d, 15, 16, 17, g_a, 6, 7, 8, 9, 10, 11, sm] + list(range(18, 30))
    for j in order:
        load(j).start()

    def wait(*js):
        for j in js:
            load(j).wait()

    back = token_rows()
    wait(ig)
    done[1][0] = dot(back, held[ig][...].reshape(TOK, 768))
    store(1).start()
    wait(bo)
    pltpu.make_async_copy(held[bo], made[0].at[0], out_sem.at[0]).start()

    def adam(param, out, at, grad, low, vector=False):
        w, f, s = (held[param + j][at] for j in range(3))
        rate, decay = (RATE_VECTOR, 0.0) if vector else (RATE_MATRIX, DECAY_MATRIX)
        moment, square, updated = adam_update(w, f, s, grad, rate, decay)
        done[out][at], done[out + 1][at], done[out + 2][at] = moment, square, updated
        if low:
            done[out + 3][at] = updated.astype(BF)

    def finish(out, count):
        for j in range(out, out + count):
            store(j).start()

    whole = slice(None)
    wait(g_u, 12, 13, 14)
    adam(12, 10, whole, held[g_u][...], True)
    finish(10, 4)
    wait(g_d, 15, 16, 17)
    adam(15, 14, whole, held[g_d][...], True)
    finish(14, 4)
    wait(g_a, 6, 7, 8)
    for j, lane in ((0, 0), (1, 384), (2, 192)):
        adam(6, 2, j, held[g_a][:, lane : lane + 192], True)
    finish(2, 4)
    eye = jnp.where(iota((SHARD, SHARD), 0) == iota((SHARD, SHARD), 1), 1.0, 0.0)
    turned = lax.dot_general(
        held[g_a][:, 576:768], eye, (((0,), (0,)), ((), ())),
        precision=lax.Precision.HIGHEST, preferred_element_type=F32,
    )
    wait(9, 10, 11)
    adam(9, 6, whole, turned, True)
    finish(6, 4)
    small = held[sm]
    wait(sm, *range(18, 30))
    adam(18, 18, whole, small[9:15, :], False, True)
    for j in (0, 1):
        adam(21, 21, slice(j, j + 1), small[6:7, 192 * j : 192 * j + 192], False, True)
    adam(24, 24, whole, small[8:9, :].reshape(FQ), False, True)
    adam(27, 27, whole, small[0:HG, 0:529], False, True)
    finish(18, 12)
    pltpu.make_async_copy(held[bo], made[0].at[0], out_sem.at[0]).wait()
    for j in range(1, n_out):
        store(j).wait()


def last_call(sums, params):
    hbm = pl.BlockSpec(memory_space=pl.ANY)
    like = lambda a, t=F32: jax.ShapeDtypeStruct(a.shape, t)
    outs = [jax.ShapeDtypeStruct((1, TOK, 768), BF), jax.ShapeDtypeStruct((1, TOK, 768), F32)]
    for j in range(0, 12, 3):
        outs += [like(params[j])] * 3 + [like(params[j], BF)]
    for j in range(12, 24, 3):
        outs += [like(params[j])] * 3
    ins = list(sums) + list(params)
    return pl.pallas_call(
        functools.partial(last_kernel, len(ins), len(outs)),
        out_shape=tuple(outs),
        in_specs=[hbm] * len(ins),
        out_specs=tuple([hbm] * len(outs)),
        scratch_shapes=[vm(a.shape, a.dtype) for a in ins + outs]
        + [pltpu.SemaphoreType.DMA((len(ins),)), pltpu.SemaphoreType.DMA((len(outs),))],
        compiler_params=pltpu.CompilerParams(vmem_limit_bytes=62 * 2**20),
        cost_estimate=pl.CostEstimate(flops=10**9, bytes_accessed=15 * 10**6, transcendentals=10**6),
    )(*ins)


def on_device_windows(images, cotangent, image_mask, *params):
    params = list(params)
    turned = (9, 10, 11, 21, 22, 23)
    for j in turned:
        params[j] = params[j].T
    (in_w, _, _, out_w, _, _, up_w, _, _, dn_w, _, _, nv, _, _, hb, _, _, ub, _, _, tab, _, _) = params
    sums = main_call(
        (
            images.reshape(TOK, D), cotangent.reshape(TOK, D), image_mask,
            in_w, out_w, up_w, dn_w, nv, hb, ub, tab,
        )
    )
    outs = list(last_call(sums, params))
    for j in (14, 15, 16, 17, 27, 28, 29):
        outs[j] = outs[j].T
    return tuple(outs)


def solution(mesh):
    shape = mesh.shape
    windows = shape["dp"] == 8 and shape["tensor"] == 4
    return jax.shard_map(
        on_device_windows if windows else on_device,
        mesh=mesh,
        in_specs=(
            P("dp", None, None),
            P("dp", None, None),
            P("dp"),
            P(None, "dp", "tensor"),
            P(None, "dp", "tensor"),
            P(None, "dp", "tensor"),
            P("tensor", "dp"),
            P("tensor", "dp"),
            P("tensor", "dp"),
            P("dp", "tensor"),
            P("dp", "tensor"),
            P("dp", "tensor"),
            P("tensor", "dp"),
            P("tensor", "dp"),
            P("tensor", "dp"),
            P(),
            P(),
            P(),
            P(None, "tensor"),
            P(None, "tensor"),
            P(None, "tensor"),
            P("tensor"),
            P("tensor"),
            P("tensor"),
            P(None, "tensor"),
            P(None, "tensor"),
            P(None, "tensor"),
        ),
        out_specs=(
            P("dp", None, None),
            P("dp", None, None),
            P(None, "dp", "tensor"),
            P(None, "dp", "tensor"),
            P(None, "dp", "tensor"),
            P(None, "dp", "tensor"),
            P("tensor", "dp"),
            P("tensor", "dp"),
            P("tensor", "dp"),
            P("tensor", "dp"),
            P("dp", "tensor"),
            P("dp", "tensor"),
            P("dp", "tensor"),
            P("dp", "tensor"),
            P("tensor", "dp"),
            P("tensor", "dp"),
            P("tensor", "dp"),
            P("tensor", "dp"),
            P(),
            P(),
            P(),
            P(None, "tensor"),
            P(None, "tensor"),
            P(None, "tensor"),
            P("tensor"),
            P("tensor"),
            P("tensor"),
            P(None, "tensor"),
            P(None, "tensor"),
            P(None, "tensor"),
        ),
        check_vma=False,
    )
```
